32 devices in a mesh: shard: 8 (over z, x), rep: 4 (over y, core).
Axes of the slice: x: 2, y: 2, z: 4, core: 2. Of those that a mesh axis runs over, the one named last changes fastest.
Arguments:
- embeddings: bfloat16 [51200, 1024], P('shard'), may hold values from -6 to 6
- send_index: int32 [51200], P('shard'), may hold values from 0 to 6399, as said below
- place_index: int32 [51200], P('shard'), may hold values from 0 to 6654, as said below
- slot_cluster: int32 [53248], P('shard'), may hold values from -1 to 207, as said below
- pair_list: int32 [2816, 2], P(('shard', 'rep')), may hold values from 0 to 25, as said below
Outputs:
- best_cosine: float32 [51200], P('shard')
The draws below stay inside these ranges and needn't reach their ends.
Inputs may be any that keep to these rules, and one draw needn't show every extreme that they name: `send_index`: on each device, the entries o * 800 to (o + 1) * 800 - 1 of its block are the local documents sent to owner o; the device's 8 * 800 entries are a permutation of its 6400 documents, so each device sends exactly 800 documents to each owner. `place_index`: on each owner, the 6400 entries are distinct slots, exactly the slots whose slot_cluster is not -1. `slot_cluster`: an owner's 26 * 256 slots form 26 blocks of 256; it holds two or more clusters, each filling one or more consecutive whole blocks with its members first and 1 to 255 padding slots (-1) at the end of its last block, 256 padding slots in all. Ids of owner o lie in o * 26 to o * 26 + 25. `pair_list`: row (o * 4 + r) * 88 + p holds a pair (i, j), i <= j, of blocks of owner o that belong to one cluster; over its 352 rows, owner o lists every such pair at least once, some of them more than once.
All inputs are finite; a program needn't handle non-finite values.
Results may differ from the reference program's by a relative error of at most 0.0014.
Values may be sent and summed in bfloat16 or wider, within the bound.
No kernel may reach another device: no remote copies, remote signals or barrier semaphores. Data moves between devices by JAX's collectives and lax.ppermute only.
A program may use at most 128 MiB of HBM per device.

```python
import jax
import jax.numpy as jnp
import numpy as np
from jax import lax

D = 1024
BLK = 256
NB = 26
DOC_DEV = 6400
PAIRS = 88
DOCS = 51200
N_SHARD = 8
N_REP = 4


def owner_layout(key):

    def single(owner_key):
        keys = jax.random.split(owner_key, 3)
        count = jax.random.randint(keys[0], (), 2, NB + 1).astype(jnp.int32)
        lanes = jnp.arange(NB - 1, dtype=jnp.int32)
        block_perm = jax.random.permutation(keys[1], NB - 1).astype(jnp.int32) + 1
        block_cuts = jnp.sort(jnp.where(lanes < count - 1, block_perm, NB))
        pad_perm = jax.random.permutation(keys[2], BLK - 2)[:NB - 1].astype(jnp.int32) + 1
        pad_perm = pad_perm.at[0].set(BLK - 1)
        pad_cuts = jnp.sort(jnp.where(lanes < count - 1, pad_perm, BLK))
        zero = jnp.zeros((1,), jnp.int32)
        edges = jnp.concatenate([zero, block_cuts, jnp.full((1,), NB, jnp.int32)])
        padding = jnp.diff(jnp.concatenate([zero, pad_cuts, jnp.full((1,), BLK, jnp.int32)]))
        block_ids = jnp.arange(NB, dtype=jnp.int32)
        cluster_of_block = jnp.sum((block_cuts[None, :] <= block_ids[:, None]).astype(jnp.int32), axis=1)
        last_block = edges[1:] - 1
        is_last = last_block[cluster_of_block] == block_ids
        pad_here = padding[cluster_of_block]
        position = jnp.arange(BLK, dtype=jnp.int32)
        live = ~(is_last[:, None] & (position[None, :] >= BLK - pad_here[:, None]))
        return (cluster_of_block, live.reshape(-1))
    return jax.vmap(single)(jax.random.split(key, N_SHARD))


def draw_send_index(key, part):
    key = jax.random.fold_in(key, 5)
    keys = jax.random.split(key, N_SHARD)
    orders = jax.vmap(lambda k: jax.random.permutation(k, DOC_DEV).astype(jnp.int32))(keys)
    return orders.reshape(-1)


def draw_slot_cluster(key, part):
    cluster_of_block, live = owner_layout(key)
    lift = NB - 1 - jnp.max(cluster_of_block, axis=1, keepdims=True)
    ids = jnp.arange(N_SHARD, dtype=jnp.int32)[:, None] * NB + cluster_of_block + lift
    spread = jnp.repeat(ids, BLK, axis=1)
    return jnp.where(live, spread, -1).astype(jnp.int32).reshape(-1)


def draw_place_index(key, part):
    cluster_of_block, live = owner_layout(key)
    key = jax.random.fold_in(key, 9)
    order = jnp.argsort(1 - live.astype(jnp.int32), axis=1, stable=True).astype(jnp.int32)[:, :DOC_DEV]
    keys = jax.random.split(key, N_SHARD)
    shuffles = jax.vmap(lambda k: jax.random.permutation(k, DOC_DEV).astype(jnp.int32))(keys)
    return jnp.take_along_axis(order, shuffles, axis=1).reshape(-1)


def draw_pair_list(key, part):
    cluster_of_block, live = owner_layout(key)
    upper = np.triu_indices(NB)
    first = jnp.asarray(upper[0], dtype=jnp.int32)
    second = jnp.asarray(upper[1], dtype=jnp.int32)
    valid = (cluster_of_block[:, first] == cluster_of_block[:, second]).astype(jnp.int32)
    order = jnp.argsort(1 - valid, axis=1, stable=True).astype(jnp.int32)
    total = jnp.sum(valid, axis=1).astype(jnp.int32)
    rank = jnp.arange(N_REP, dtype=jnp.int32)
    held = (total[:, None] - rank[None, :] + N_REP - 1) // N_REP
    row = jnp.arange(PAIRS, dtype=jnp.int32)
    picks = rank[None, :, None] + N_REP * (row[None, None, :] % held[:, :, None])
    picks = picks.reshape(N_SHARD, N_REP * PAIRS).astype(jnp.int32)
    chosen = jnp.take_along_axis(order, picks, axis=1)
    pairs = jnp.stack([first[chosen], second[chosen]], axis=-1)
    return pairs.reshape(-1, 2).astype(jnp.int32)


def shard_levels(stream_key, shape, cuts, least, top_value):
    def one(dim, shards_of):
        heights = jax.random.uniform(jax.random.fold_in(jax.random.fold_in(stream_key, 6), dim), (shards_of,), jnp.float32, least / len(cuts), top_value / len(cuts))
        return jnp.repeat(jnp.exp(heights), shape[dim] // shards_of).reshape((-1,) + (1,) * (len(shape) - dim - 1))

    loudness = one(*cuts[0])
    for cut in cuts[1:]:
        loudness = loudness * one(*cut)
    return loudness


def scatter_about(key, shape, scale, limit, cuts=(), kind=jnp.bfloat16):
    entries = scale * jax.random.normal(key, shape, jnp.float32)
    if cuts:
        entries = entries * shard_levels(key, shape, cuts, -0.22, 0.18)
    return jnp.clip(entries, -limit, limit).astype(kind)


def setup_inputs(seed: int = 0) -> dict:
    seeds = jax.random.split(jax.random.key(seed), 6)
    embeddings = scatter_about(seeds[0], (DOCS, D), 1.0, 6.0, ((0, 8),))
    send_index = draw_send_index(jax.random.fold_in(seeds[5], 71), 0)
    place_index = draw_place_index(jax.random.fold_in(seeds[5], 71), 0)
    slot_cluster = draw_slot_cluster(jax.random.fold_in(seeds[5], 71), 0)
    pair_list = draw_pair_list(jax.random.fold_in(seeds[5], 71), 0)
    return dict(embeddings=embeddings, send_index=send_index, place_index=place_index, slot_cluster=slot_cluster, pair_list=pair_list)


def reference(embeddings, send_index, place_index, slot_cluster, pair_list):
    wide = embeddings.astype(jnp.float32)
    normed = (wide * lax.rsqrt(lax.optimization_barrier(jnp.sum(wide * wide, axis=1, keepdims=True)) + 1e-06)).astype(jnp.bfloat16)
    share = DOC_DEV // N_SHARD
    sends = send_index.reshape(N_SHARD, N_SHARD, share)
    offsets = (jnp.arange(N_SHARD, dtype=jnp.int32) * DOC_DEV)[None, :, None]
    documents = jnp.transpose(sends, (1, 0, 2)) + offsets
    places = place_index.reshape(N_SHARD, N_SHARD * share)
    clusters = slot_cluster.reshape(N_SHARD, NB, BLK)
    pairs = pair_list.reshape(N_SHARD, N_REP * PAIRS, 2)
    diagonal = jnp.eye(BLK, dtype=bool)

    def owner(items):
        doc_owner, place_owner, cluster_owner, pair_owner = items
        slot_doc = jnp.zeros((NB * BLK,), jnp.int32).at[place_owner].set(doc_owner.reshape(-1))
        blocks = normed[slot_doc].reshape(NB, BLK, D)
        count = pair_owner.shape[0]
        same = (pair_owner[:, None, 0] == pair_owner[None, :, 0]) & (pair_owner[:, None, 1] == pair_owner[None, :, 1])
        earlier = jnp.arange(count)[None, :] < jnp.arange(count)[:, None]
        repeat = jnp.any(same & earlier, axis=1)

        def visit(best, item):
            pair, again = item

            def fresh(current):
                first = pair[0]
                second = pair[1]
                gram = jnp.dot(blocks[first], blocks[second].T, preferred_element_type=jnp.float32)
                left = cluster_owner[first]
                right = cluster_owner[second]
                counts = (left[:, None] == right[None, :]) & (left[:, None] >= 0)
                counts = counts & ~((first == second) & diagonal)
                values = jnp.where(counts, gram, jnp.float32(-1.0))
                current = current.at[first].max(lax.optimization_barrier(jnp.max(values, axis=1)))
                return current.at[second].max(lax.optimization_barrier(jnp.max(values, axis=0)))
            return (lax.cond(again, lambda current: current, fresh, best), None)
        start = jnp.full((NB, BLK), -1.0, jnp.float32)
        best = lax.scan(visit, start, (pair_owner, repeat))[0]
        return best.reshape(-1)[place_owner]
    values = lax.map(owner, (documents, places, clusters, pairs))
    return jnp.zeros((N_SHARD * DOC_DEV,), jnp.float32).at[documents.reshape(-1)].set(values.reshape(-1))
```

```python
import functools

import jax
import jax.numpy as jnp
import numpy as np
from jax import lax
from jax.experimental import pallas as pl
from jax.experimental.pallas import tpu as pltpu
from jax.sharding import PartitionSpec as P

BLK = 256
LANES = 128
NT = (((1,), (1,)), ((), ()))
VMEM_LIMIT = 56 * 1024 * 1024

HOSTS = (2, 3, 4, 5)
ROUNDS = ((4, 6, 5, 7, 2, 1, 3), (2, 1, 3, 6, 4, 7, 5))


def host_of(owner):
    z, x = owner // 2, owner % 2
    return (1 if z < 2 else 2) * 2 + x, z % 2


def plan():
    owner_at = {host_of(owner): owner for owner in range(8)}
    sends = np.zeros((8, 4, 4), np.int32)
    order = np.zeros((8, 4, 16), np.int32)
    for s in range(8):
        for rep in range(4):
            y, core = divmod(rep, 2)
            steps = [(step, k) for step, k in enumerate(ROUNDS[core]) if s ^ k in HOSTS]
            assert [step // 2 for step, _ in steps] == list(range(len(steps)))
            targets = [s ^ k for _, k in steps]
            if s in HOSTS:
                targets.append(s)
            sends[s, rep] = [owner_at[target, y] for target in targets]
            for side in range(2):
                half = core ^ side
                for step, k in enumerate((0,) + ROUNDS[half]):
                    order[s, rep, 2 * step + side] = (s ^ k) * 2 + half
    return sends, order


def round_pairs(step):
    pairs = []
    for rep in range(4):
        for host in HOSTS:
            pairs.append(((host ^ ROUNDS[rep % 2][step]) * 4 + rep, host * 4 + rep))
    return pairs


SIBLINGS = [(host * 4 + rep, host * 4 + (rep ^ 1)) for host in HOSTS for rep in range(4)]


def metadata_pairs():
    pairs = []
    for owner in range(8):
        host, y = host_of(owner)
        for core in range(2):
            pairs.append((owner * 4 + y * 2 + core, host * 4 + y * 2 + core))
    return pairs


def normalize(rows):
    wide = rows.astype(jnp.float32)
    return (wide * lax.rsqrt(jnp.sum(wide * wide, axis=1, keepdims=True) + 1e-06)).astype(
        jnp.bfloat16
    )


def arrival_clusters(place_index, slot_cluster):
    heads = slot_cluster.reshape(-1, BLK)[:, 0]
    block = place_index // BLK
    hit = block[None, :] == jnp.arange(heads.shape[0], dtype=jnp.int32)[:, None]
    return jnp.sum(jnp.where(hit, heads[:, None], 0), axis=0)


def row_layout(column, size):
    return jnp.max(jnp.transpose(column), axis=0, keepdims=True)[:, :size]


def gram_kernel(news, count, size, first, *refs):
    chunks = refs[:count]
    cluster_row, cluster_column, best_ref, held, acc, sems = refs[count:]
    for i in range(count):
        pltpu.make_async_copy(chunks[i], held.at[i], sems.at[i]).start()
    best_ref[...] = jnp.full_like(best_ref, -1.0)
    ids = lax.broadcasted_iota(jnp.int32, (size, size), 0)
    diagonal = ids == lax.broadcasted_iota(jnp.int32, (size, size), 1)
    for a in range(news):
        pltpu.make_async_copy(chunks[a], held.at[a], sems.at[a]).wait()
    for a in range(news):
        acc[...] = jnp.full_like(acc, -1.0)

        def visit(i, _, a=a):
            @pl.when((a == 0) & (i >= news))
            def _():
                pltpu.make_async_copy(held.at[i], held.at[i], sems.at[i]).wait()

            gram = lax.dot_general(held[a], held[i], NT, preferred_element_type=jnp.float32)
            left = jnp.tile(cluster_column[a], (1, -(-size // LANES)))[:, :size]
            counts = (left == cluster_row[i]) & ~((i == a) & diagonal)
            values = jnp.where(counts, gram, jnp.float32(-1.0))
            best_ref[i] = jnp.maximum(best_ref[i], jnp.max(values, axis=0, keepdims=True))
            acc[0:size, :] = jnp.maximum(
                acc[0:size, :], jnp.broadcast_to(jnp.max(values, axis=1, keepdims=True), (size, LANES))
            )
            return 0

        lax.fori_loop(first, count, visit, 0)
        best_ref[a] = jnp.maximum(best_ref[a], row_layout(acc[...], size))


def gram_best(chunks, news, cluster_row, first=0):
    count = len(chunks)
    size, width = chunks[0].shape
    padded = -(-size // LANES) * LANES
    cluster_column = jnp.broadcast_to(cluster_row[:news, 0, :, None], (news, size, LANES))
    return pl.pallas_call(
        functools.partial(gram_kernel, news, count, size, first),
        out_shape=jax.ShapeDtypeStruct((count, 1, size), jnp.float32),
        in_specs=[pl.BlockSpec(memory_space=pl.ANY)] * count
        + [pl.BlockSpec(memory_space=pltpu.VMEM)] * 2,
        out_specs=pl.BlockSpec(memory_space=pltpu.VMEM),
        scratch_shapes=[
            pltpu.VMEM((count, size, width), jnp.bfloat16),
            pltpu.VMEM((padded, LANES), jnp.float32),
            pltpu.SemaphoreType.DMA((count,)),
        ],
        compiler_params=pltpu.CompilerParams(vmem_limit_bytes=VMEM_LIMIT),
        cost_estimate=pl.CostEstimate(
            flops=2 * news * count * size * size * width,
            bytes_accessed=2 * count * size * width,
            transcendentals=0,
        ),
    )(*chunks, cluster_row, cluster_column)


def settle_kernel(groups, size, high, index_ref, values_ref, out_ref):
    total = jnp.zeros((high, LANES), jnp.float32)
    for g in range(groups):
        index = index_ref[g : g + 1, :]
        rows = lax.broadcasted_iota(jnp.int32, (high, size), 0)
        lanes = lax.broadcasted_iota(jnp.int32, (LANES, size), 0)
        left = jnp.where(rows == index // LANES, values_ref[g : g + 1, :], 0.0)
        right = jnp.where(lanes == index % LANES, jnp.float32(1.0), jnp.float32(0.0))
        total += lax.dot_general(
            left, right, NT, precision=lax.Precision.HIGHEST, preferred_element_type=jnp.float32
        )
    out_ref[...] = total


def settle(index, values, documents):
    groups, size = index.shape
    high = -(-documents // (8 * LANES)) * 8
    out = pl.pallas_call(
        functools.partial(settle_kernel, groups, size, high),
        out_shape=jax.ShapeDtypeStruct((high, LANES), jnp.float32),
        compiler_params=pltpu.CompilerParams(vmem_limit_bytes=VMEM_LIMIT),
    )(index, values)
    return out.reshape(-1)[:documents]


def hosted(embeddings, send_index, place_index, slot_cluster):
    documents = embeddings.shape[0]
    share = send_index.shape[0] // 8
    size = share // 2
    s, rep = lax.axis_index("shard"), lax.axis_index("rep")
    core = rep % 2
    axes = ("shard", "rep")
    sends, order = plan()
    sends = jnp.asarray(sends)[s, rep]
    order = jnp.asarray(order)[s, rep]
    outgoing = []
    for slot in range(4):
        index = lax.dynamic_slice(send_index, (sends[slot] * share + core * size,), (size,))
        outgoing.append(normalize(embeddings.at[index].get(mode="promise_in_bounds")))
    clusters = lax.ppermute(arrival_clusters(place_index, slot_cluster), axes, metadata_pairs())
    clusters = clusters.reshape(16, 1, size)[order]
    own = [outgoing[3]] + [lax.ppermute(outgoing[r // 2], axes, round_pairs(r)) for r in range(7)]
    other = [lax.ppermute(chunk, axes, SIBLINGS) for chunk in own]

    best = jnp.full((16, 1, size), -1.0, jnp.float32)
    for steps in ((0, 1, 2, 3), (4, 5), (6,), (7,)):
        news = [2 * step for step in steps]
        rest = [i for i in range(2 * steps[-1] + 2) if i not in news]
        picks = news + rest
        chunks = [(own, other)[i % 2][i // 2] for i in picks]
        found = gram_best(chunks, len(news), clusters[jnp.asarray(picks)])
        best = best.at[jnp.asarray(picks)].max(found)
    home = jnp.zeros((16, size), jnp.float32).at[order].set(best[:, 0])
    outbound = jnp.broadcast_to(home.reshape(8, 1, 2, size), (8, 4, 2, size)).reshape(32, 2, size)
    returned = lax.all_to_all(outbound, axes, split_axis=0, concat_axis=0, tiled=True)
    returned = jnp.max(returned.reshape(8, 2, 2, 2, size), axis=2)
    values = jnp.concatenate([returned[host_of(owner)] for owner in range(8)])
    return settle(send_index.reshape(16, size), values, documents)


def gathered(embeddings, send_index, place_index, slot_cluster):
    documents, width = embeddings.shape
    owners = lax.axis_size("shard")
    reps = lax.axis_size("rep")
    rep = lax.axis_index("rep")
    share = send_index.shape[0] // owners
    outgoing = normalize(embeddings.at[send_index].get(mode="promise_in_bounds"))
    arrived = lax.all_to_all(
        outgoing.reshape(owners, share, width), "shard", split_axis=0, concat_axis=0, tiled=True
    )
    parts = 16
    size = documents // parts
    news = parts // reps
    turn = rep * news
    arrived = jnp.roll(arrived.reshape(parts, size, width), -turn, axis=0)
    clusters = arrival_clusters(place_index, slot_cluster).reshape(parts, 1, size)
    clusters = jnp.roll(clusters, -turn, axis=0)
    best = gram_best([arrived[i] for i in range(parts)], news, clusters)[:news]
    best = lax.all_gather(best.reshape(-1), "rep", axis=0, tiled=True)
    returned = lax.all_to_all(
        best.reshape(owners, share), "shard", split_axis=0, concat_axis=0, tiled=True
    )
    return settle(send_index.reshape(parts, size), returned.reshape(parts, size), documents)


def solution(mesh):
    planned = mesh.shape["shard"] == 8 and mesh.shape["rep"] == 4

    def shards(embeddings, send_index, place_index, slot_cluster, pair_list):
        del pair_list
        run = hosted if planned else gathered
        return run(embeddings, send_index, place_index, slot_cluster)

    return jax.shard_map(
        shards,
        mesh=mesh,
        in_specs=(P("shard", None), P("shard"), P("shard"), P("shard"), P(("shard", "rep"), None)),
        out_specs=P("shard"),
        check_vma=False,
    )
```

```python
import functools

import jax
import jax.numpy as jnp
import numpy as np
from jax import lax
from jax.experimental import pallas as pl
from jax.experimental.pallas import tpu as pltpu
from jax.sharding import PartitionSpec as P

BLK = 256
LANES = 128
NT = (((1,), (1,)), ((), ()))
VMEM_LIMIT = 56 * 1024 * 1024

HOSTS = (2, 3, 4, 5)
ROUNDS = ((4, 6, 5, 7, 2, 1, 3), (2, 1, 3, 6, 4, 7, 5))


def host_of(owner):
    z, x = owner // 2, owner % 2
    return (1 if z < 2 else 2) * 2 + x, z % 2


def plan():
    owner_at = {host_of(owner): owner for owner in range(8)}
    sends = np.zeros((8, 4, 4), np.int32)
    order = np.zeros((8, 4, 16), np.int32)
    for s in range(8):
        for rep in range(4):
            y, core = divmod(rep, 2)
            steps = [(step, k) for step, k in enumerate(ROUNDS[core]) if s ^ k in HOSTS]
            assert [step // 2 for step, _ in steps] == list(range(len(steps)))
            targets = [s ^ k for _, k in steps]
            if s in HOSTS:
                targets.append(s)
            sends[s, rep] = [owner_at[target, y] for target in targets]
            for side in range(2):
                half = core ^ side
                for step, k in enumerate((0,) + ROUNDS[half]):
                    order[s, rep, 2 * step + side] = (s ^ k) * 2 + half
    return sends, order


def round_pairs(step):
    pairs = []
    for rep in range(4):
        for host in HOSTS:
            pairs.append(((host ^ ROUNDS[rep % 2][step]) * 4 + rep, host * 4 + rep))
    return pairs


SIBLINGS = [(host * 4 + rep, host * 4 + (rep ^ 1)) for host in HOSTS for rep in range(4)]


def metadata_pairs():
    pairs = []
    for owner in range(8):
        host, y = host_of(owner)
        for core in range(2):
            pairs.append((owner * 4 + y * 2 + core, host * 4 + y * 2 + core))
    return pairs


def normalize(rows):
    wide = rows.astype(jnp.float32)
    return (wide * lax.rsqrt(jnp.sum(wide * wide, axis=1, keepdims=True) + 1e-06)).astype(
        jnp.bfloat16
    )


def arrival_clusters(place_index, slot_cluster):
    heads = slot_cluster.reshape(-1, BLK)[:, 0]
    block = place_index // BLK
    hit = block[None, :] == jnp.arange(heads.shape[0], dtype=jnp.int32)[:, None]
    return jnp.sum(jnp.where(hit, heads[:, None], 0), axis=0)


def gather_kernel(count, size, sections, *refs):
    table_ref, index_ref, rows_ref = refs[:3]
    out_ref, raw, wide, picked, sems = refs[-5:]
    part = raw.shape[0] // sections
    copies = []
    for i in range(sections):
        rows = pl.ds(i * part, part)
        copies.append(pltpu.make_async_copy(rows_ref.at[rows], raw.at[rows], sems.at[i]))
        copies[-1].start()
    step = 80
    for i in range(sections):
        copies[i].wait()

        def widen(j, _, i=i):
            rows = pl.ds(pl.multiple_of(i * part + j * step, step), step)
            wide[rows, :] = raw[rows, :].astype(jnp.float32)
            return 0

        lax.fori_loop(0, part // step, widen, 0)
    group = 16
    for c in range(count):
        base = table_ref[c]

        def pick(j, _, c=c, base=base):
            for t in range(group):
                source = index_ref[base + j * group + t]
                picked[pl.ds(t, 1), :] = wide[pl.ds(source, 1), :]
            rows = picked[...]
            scale = lax.rsqrt(jnp.sum(rows * rows, axis=1, keepdims=True) + 1e-06)
            out_ref[c, pl.ds(pl.multiple_of(j * group, group), group), :] = (rows * scale).astype(
                jnp.bfloat16
            )
            return 0

        lax.fori_loop(0, size // group, pick, 0)


def gather_rows(embeddings, index, starts, size, after=()):
    documents, width = embeddings.shape
    count = starts.shape[0]
    sections = 8
    return pl.pallas_call(
        functools.partial(gather_kernel, count, size, sections),
        out_shape=jax.ShapeDtypeStruct((count, size, width), jnp.bfloat16),
        in_specs=[
            pl.BlockSpec(memory_space=pltpu.SMEM),
            pl.BlockSpec(memory_space=pltpu.SMEM),
            pl.BlockSpec(memory_space=pl.ANY),
        ]
        + [pl.BlockSpec(memory_space=pl.ANY)] * len(after),
        out_specs=pl.BlockSpec(memory_space=pltpu.VMEM),
        scratch_shapes=[
            pltpu.VMEM((documents, width), jnp.bfloat16),
            pltpu.VMEM((documents, width), jnp.float32),
            pltpu.VMEM((16, width), jnp.float32),
            pltpu.SemaphoreType.DMA((sections,)),
        ],
        compiler_params=pltpu.CompilerParams(vmem_limit_bytes=VMEM_LIMIT),
        cost_estimate=pl.CostEstimate(
            flops=3 * count * size * width, bytes_accessed=2 * documents * width, transcendentals=0
        ),
    )(starts, index, embeddings, *after)


def best_of_rows(acc, size):
    return jnp.max(jnp.transpose(acc), axis=0, keepdims=True)[:, :size]


def gram_kernel(passes, count, size, first, *refs):
    chunks = refs[:count]
    cluster_row, cluster_column, before_ref, best_ref, held, acc, sems = refs[count:]
    limit = count * size

    def copy(i):
        return pltpu.make_async_copy(chunks[i], held.at[pl.ds(i * size, size)], sems.at[i])

    def arrive(i):
        rows = held.at[pl.ds(0, size)]
        pltpu.make_async_copy(rows, rows, sems.at[i]).wait()

    copy(first).start()
    for i in range(count):
        if i != first:
            copy(i).start()
    best_ref[...] = before_ref[...]
    copy(first).wait()
    for n, (chunk, place, groups, group, meets, last) in enumerate(passes):
        acc[...] = jnp.full_like(acc, -1.0)
        rows = held[chunk * size : (chunk + 1) * size, :]
        left = cluster_column[place]
        left = jnp.concatenate([left, left], axis=1)

        def tile(start, special, chunk=chunk, rows=rows, left=left):
            gram = lax.dot_general(
                rows, held[pl.ds(start, BLK), :], NT, preferred_element_type=jnp.float32
            )
            counts = left == cluster_row[:, pl.ds(start, BLK)]
            if special:
                column = start + lax.broadcasted_iota(jnp.int32, (size, BLK), 1)
                row = chunk * size + lax.broadcasted_iota(jnp.int32, (size, BLK), 0)
                counts = counts & (column != row) & (column < limit)
            values = jnp.where(counts, gram, jnp.float32(-1.0))
            top = jnp.max(values, axis=0, keepdims=True)
            best_ref[:, pl.ds(start, BLK)] = jnp.maximum(best_ref[:, pl.ds(start, BLK)], top)
            acc[0:size, :] = jnp.maximum(
                acc[0:size, :], jnp.maximum(values[:, :LANES], values[:, LANES:])
            )

        def visit(u, _, n=n, group=group, meets=meets, tile=tile):
            if n == 0:
                for i in (2 * u, 2 * u + 1):

                    @pl.when(i < count)
                    def _(i=i):
                        @pl.when(i != first)
                        def _():
                            arrive(i)

            for t in range(group):
                tile(pl.multiple_of((u * group + t) * BLK, BLK), meets)
            return 0

        lax.fori_loop(0, groups, visit, 0)
        if n == 0:
            for i in range(2 * groups, count):
                if i != first:
                    arrive(i)
        for t in last:
            tile(t * BLK, True)
        span = slice(chunk * size, (chunk + 1) * size)
        best_ref[:, span] = jnp.maximum(best_ref[:, span], best_of_rows(acc[...], size))


def gram_best(chunks, cluster_row, cluster_column, before, passes, first):
    count = len(chunks)
    size, width = chunks[0].shape
    total = before.shape[1]
    held = -(-count * size // BLK) * BLK
    padded = -(-size // LANES) * LANES
    work = sum((groups * group + len(last)) * BLK for _, _, groups, group, _, last in passes)
    return pl.pallas_call(
        functools.partial(gram_kernel, passes, count, size, first),
        out_shape=jax.ShapeDtypeStruct((1, total), jnp.float32),
        in_specs=[pl.BlockSpec(memory_space=pl.ANY)] * count
        + [pl.BlockSpec(memory_space=pltpu.VMEM)] * 3,
        out_specs=pl.BlockSpec(memory_space=pltpu.VMEM),
        scratch_shapes=[
            pltpu.VMEM((held, width), jnp.bfloat16),
            pltpu.VMEM((padded, LANES), jnp.float32),
            pltpu.SemaphoreType.DMA((count,)),
        ],
        compiler_params=pltpu.CompilerParams(vmem_limit_bytes=VMEM_LIMIT),
        cost_estimate=pl.CostEstimate(
            flops=2 * size * work * width,
            bytes_accessed=2 * count * size * width,
            transcendentals=0,
        ),
    )(*chunks, cluster_row, cluster_column, before)


def step_passes(step, size):
    groups = 2 * step * size // (3 * BLK)
    tiles = -(-(2 * step + 1) * size // BLK)
    passes = [(2 * step, step, groups, 3, False, tuple(range(3 * groups, tiles)))]
    low = (2 * step - 1) * size // BLK if step > 1 else 0
    passes.append((2 * step - 2, step - 1, 0, 1, True, tuple(range(low, -(-2 * step * size // BLK)))))
    return tuple(passes)


def finish_kernel(size, order_ref, own_ref, other_ref, clusters_ref, column_ref, best_ref, out_ref, acc):
    gram = lax.dot_general(own_ref[...], other_ref[...], NT, preferred_element_type=jnp.float32)
    left = jnp.tile(column_ref[...], (1, -(-size // LANES)))[:, :size]
    last = 15 * size
    values = jnp.where(left == clusters_ref[:, last : last + size], gram, jnp.float32(-1.0))
    acc[...] = jnp.full_like(acc, -1.0)
    acc[0:size, :] = jnp.broadcast_to(jnp.max(values, axis=1, keepdims=True), (size, LANES))
    for i in range(16):
        found = best_ref[:, i * size : (i + 1) * size]
        if i == 14:
            found = jnp.maximum(found, best_of_rows(acc[...], size))
        if i == 15:
            found = jnp.maximum(found, jnp.max(values, axis=0, keepdims=True))
        place = order_ref[i]
        source, half = place // 2, place % 2
        for rep in range(4):
            out_ref[source * 4 + rep, pl.ds(half, 1), :] = found


def finish(order, own, other, clusters, column, best):
    size = own.shape[0]
    padded = -(-size // LANES) * LANES
    return pl.pallas_call(
        functools.partial(finish_kernel, size),
        out_shape=jax.ShapeDtypeStruct((32, 2, size), jnp.float32),
        in_specs=[pl.BlockSpec(memory_space=pltpu.SMEM)]
        + [pl.BlockSpec(memory_space=pltpu.VMEM)] * 5,
        out_specs=pl.BlockSpec(memory_space=pltpu.VMEM),
        scratch_shapes=[pltpu.VMEM((padded, LANES), jnp.float32)],
        compiler_params=pltpu.CompilerParams(vmem_limit_bytes=VMEM_LIMIT),
    )(order, own, other, clusters, column, best)


def settle_kernel(sources, size, high, index_ref, values_ref, out_ref, left_ref, right_ref):
    wide = left_ref.shape[1] // len(sources)
    left_ref[...] = jnp.zeros_like(left_ref)
    right_ref[...] = jnp.zeros_like(right_ref)
    rows = lax.broadcasted_iota(jnp.int32, (high, size), 0)
    lanes = lax.broadcasted_iota(jnp.int32, (LANES, size), 0)
    for g, places in enumerate(sources):
        index = index_ref[g // 2, g % 2 : g % 2 + 1, :] if index_ref.ndim == 3 else index_ref[g : g + 1, :]
        value = values_ref[places[0][0], places[0][1] : places[0][1] + 1, :]
        for a, b in places[1:]:
            value = jnp.maximum(value, values_ref[a, b : b + 1, :])
        span = slice(g * wide, g * wide + size)
        here = rows == index // LANES
        for piece in range(3):
            head = value.astype(jnp.bfloat16).astype(jnp.float32)
            value = value - head
            left_ref[piece * high : (piece + 1) * high, span] = jnp.where(here, head, 0.0).astype(
                jnp.bfloat16
            )
        right_ref[:, span] = jnp.where(lanes == index % LANES, 1.0, 0.0).astype(jnp.bfloat16)
    total = lax.dot_general(left_ref[...], right_ref[...], NT, preferred_element_type=jnp.float32)
    total = total[2 * high : 3 * high] + total[high : 2 * high] + total[:high]
    out_ref[...] = total[: out_ref.shape[0]]


def settle(index, values, sources, documents):
    size = index.shape[-1]
    high = -(-documents // (16 * LANES)) * 16
    wide = -(-size // LANES) * LANES * len(sources)
    out = pl.pallas_call(
        functools.partial(settle_kernel, sources, size, high),
        out_shape=jax.ShapeDtypeStruct((documents // LANES, LANES), jnp.float32),
        scratch_shapes=[
            pltpu.VMEM((3 * high, wide), jnp.bfloat16),
            pltpu.VMEM((LANES, wide), jnp.bfloat16),
        ],
        compiler_params=pltpu.CompilerParams(vmem_limit_bytes=VMEM_LIMIT),
    )(index, values)
    return out.reshape(-1)


def hosted(embeddings, send_index, place_index, slot_cluster):
    documents = embeddings.shape[0]
    share = send_index.shape[0] // 8
    size = share // 2
    s, rep = lax.axis_index("shard"), lax.axis_index("rep")
    axes = ("shard", "rep")
    sends, order = plan()
    starts = sends * share + (np.arange(4) % 2 * size)[None, :, None].astype(np.int32)
    starts = jnp.asarray(starts)[s, rep]
    order = jnp.asarray(order)[s, rep]
    early = gather_rows(embeddings, send_index, starts[:1], size)
    late = gather_rows(embeddings, send_index, starts[1:], size, (early,))
    outgoing = [early[0], late[0], late[1], late[2]]
    own = [outgoing[3]] + [lax.ppermute(outgoing[r // 2], axes, round_pairs(r)) for r in range(7)]
    other = [lax.ppermute(chunk, axes, SIBLINGS) for chunk in own]
    clusters = lax.ppermute(arrival_clusters(place_index, slot_cluster), axes, metadata_pairs())
    clusters = clusters.reshape(16, size)[order]
    column = jnp.broadcast_to(clusters[0::2, :, None], (8, size, LANES))
    clusters = clusters.reshape(1, 16 * size)

    best = jnp.full((1, 16 * size), -1.0, jnp.float32)
    chunks = [(own, other)[i % 2][i // 2] for i in range(16)]
    for step in range(1, 8):
        best = gram_best(
            chunks[: 2 * step + 1], clusters, column, best, step_passes(step, size), 2 * step
        )
    outbound = finish(order, own[7], other[7], clusters, column[7], best)
    returned = lax.all_to_all(outbound, axes, split_axis=0, concat_axis=0, tiled=True)
    sources = []
    for owner in range(8):
        host, y = host_of(owner)
        for half in range(2):
            sources.append(tuple((host * 4 + y * 2 + core, half) for core in range(2)))
    return settle(send_index.reshape(8, 2, size), returned, tuple(sources), documents)


def gathered(embeddings, send_index, place_index, slot_cluster):
    documents, width = embeddings.shape
    owners = lax.axis_size("shard")
    reps = lax.axis_size("rep")
    share = send_index.shape[0] // owners
    outgoing = normalize(embeddings.at[send_index].get(mode="promise_in_bounds"))
    arrived = lax.all_to_all(
        outgoing.reshape(owners, share, width), "shard", split_axis=0, concat_axis=0, tiled=True
    )
    parts = 16
    size = documents // parts
    news = parts // reps
    turn = lax.axis_index("rep") * news
    arrived = jnp.roll(arrived.reshape(parts, size, width), -turn, axis=0)
    clusters = arrival_clusters(place_index, slot_cluster).reshape(parts, size)
    clusters = jnp.roll(clusters, -turn, axis=0)
    column = jnp.broadcast_to(clusters[:news, :, None], (news, size, LANES))
    best = jnp.full((1, documents), -1.0, jnp.float32)
    tiles = tuple(range(documents // BLK))
    passes = tuple((chunk, chunk, 0, 1, True, tiles) for chunk in range(news))
    best = gram_best(
        [arrived[i] for i in range(parts)], clusters.reshape(1, -1), column, best, passes, 0
    )
    best = lax.all_gather(best[0, : news * size], "rep", axis=0, tiled=True)
    returned = lax.all_to_all(
        best.reshape(owners, share), "shard", split_axis=0, concat_axis=0, tiled=True
    )
    sources = tuple(((0, g),) for g in range(parts))
    return settle(send_index.reshape(parts, size), returned.reshape(1, parts, size), sources, documents)


def solution(mesh):
    planned = mesh.shape["shard"] == 8 and mesh.shape["rep"] == 4

    def shards(embeddings, send_index, place_index, slot_cluster, pair_list):
        del pair_list
        run = hosted if planned else gathered
        return run(embeddings, send_index, place_index, slot_cluster)

    return jax.shard_map(
        shards,
        mesh=mesh,
        in_specs=(P("shard", None), P("shard"), P("shard"), P("shard"), P(("shard", "rep"), None)),
        out_specs=P("shard"),
        check_vma=False,
    )
```

```python
import functools

import jax
import jax.numpy as jnp
import numpy as np
from jax import lax
from jax.experimental import pallas as pl
from jax.experimental.pallas import tpu as pltpu
from jax.sharding import PartitionSpec as P

BLK = 256
LANES = 128
NT = (((1,), (1,)), ((), ()))
VMEM_LIMIT = 56 * 1024 * 1024

HOSTS = (2, 3, 4, 5)
ROUNDS = ((4, 6, 5, 7, 2, 1, 3), (2, 1, 3, 6, 4, 7, 5))


CHUNKS = (
    (0, 0), (1, 0), (0, 1), (1, 1),
    (2, 0), (3, 0), (2, 1), (3, 1),
    (4, 0), (5, 0), (4, 1), (5, 1),
    (6, 0), (6, 1), (7, 0), (7, 1),
)


def host_of(owner):
    z, x = owner // 2, owner % 2
    return (1 if z < 2 else 2) * 2 + x, z % 2


def plan():
    owner_at = {host_of(owner): owner for owner in range(8)}
    sends = np.zeros((8, 4, 4), np.int32)
    order = np.zeros((8, 4, 16), np.int32)
    for s in range(8):
        for rep in range(4):
            y, core = divmod(rep, 2)
            steps = [(step, k) for step, k in enumerate(ROUNDS[core]) if s ^ k in HOSTS]
            assert [step // 2 for step, _ in steps] == list(range(len(steps)))
            targets = [s ^ k for _, k in steps]
            if s in HOSTS:
                targets.append(s)
            sends[s, rep] = [owner_at[target, y] for target in targets]
            for side in range(2):
                half = core ^ side
                for step, k in enumerate((0,) + ROUNDS[half]):
                    order[s, rep, CHUNKS.index((step, side))] = (s ^ k) * 2 + half
    return sends, order


def round_pairs(step):
    pairs = []
    for rep in range(4):
        for host in HOSTS:
            pairs.append(((host ^ ROUNDS[rep % 2][step]) * 4 + rep, host * 4 + rep))
    return pairs


SIBLINGS = [(host * 4 + rep, host * 4 + (rep ^ 1)) for host in HOSTS for rep in range(4)]


def metadata_pairs():
    pairs = []
    for owner in range(8):
        host, y = host_of(owner)
        for core in range(2):
            pairs.append((owner * 4 + y * 2 + core, host * 4 + y * 2 + core))
    return pairs


def tie(value, *after):
    return lax.optimization_barrier((value, *after))[0]


def normalize(rows):
    wide = rows.astype(jnp.float32)
    return (wide * lax.rsqrt(jnp.sum(wide * wide, axis=1, keepdims=True) + 1e-06)).astype(
        jnp.bfloat16
    )


def arrival_clusters(place_index, slot_cluster):
    heads = slot_cluster.reshape(-1, BLK)[:, 0]
    block = place_index // BLK
    hit = block[None, :] == jnp.arange(heads.shape[0], dtype=jnp.int32)[:, None]
    return jnp.sum(jnp.where(hit, heads[:, None], 0), axis=0)


def gather_kernel(count, size, sections, *refs):
    table_ref, index_ref, rows_ref = refs[:3]
    out_ref, raw, wide, picked, sems = refs[-5:]
    part = raw.shape[0] // sections
    copies = []
    for i in range(sections):
        rows = pl.ds(i * part, part)
        copies.append(pltpu.make_async_copy(rows_ref.at[rows], raw.at[rows], sems.at[i]))
        copies[-1].start()
    step = 80
    for i in range(sections):
        copies[i].wait()

        def widen(j, _, i=i):
            rows = pl.ds(pl.multiple_of(i * part + j * step, step), step)
            wide[rows, :] = raw[rows, :].astype(jnp.float32)
            return 0

        lax.fori_loop(0, part // step, widen, 0)
    group = 16
    for c in range(count):
        base = table_ref[c]

        def pick(j, _, c=c, base=base):
            for t in range(group):
                source = index_ref[base + j * group + t]
                picked[pl.ds(t, 1), :] = wide[pl.ds(source, 1), :]
            rows = picked[...]
            scale = lax.rsqrt(jnp.sum(rows * rows, axis=1, keepdims=True) + 1e-06)
            out_ref[c, pl.ds(pl.multiple_of(j * group, group), group), :] = (rows * scale).astype(
                jnp.bfloat16
            )
            return 0

        lax.fori_loop(0, size // group, pick, 0)


def gather_rows(embeddings, index, starts, size, after=()):
    documents, width = embeddings.shape
    count = starts.shape[0]
    sections = 8
    return pl.pallas_call(
        functools.partial(gather_kernel, count, size, sections),
        out_shape=jax.ShapeDtypeStruct((count, size, width), jnp.bfloat16),
        in_specs=[
            pl.BlockSpec(memory_space=pltpu.SMEM),
            pl.BlockSpec(memory_space=pltpu.SMEM),
            pl.BlockSpec(memory_space=pl.ANY),
        ]
        + [pl.BlockSpec(memory_space=pl.ANY)] * len(after),
        out_specs=pl.BlockSpec(memory_space=pltpu.VMEM),
        scratch_shapes=[
            pltpu.VMEM((documents, width), jnp.bfloat16),
            pltpu.VMEM((documents, width), jnp.float32),
            pltpu.VMEM((16, width), jnp.float32),
            pltpu.SemaphoreType.DMA((sections,)),
        ],
        compiler_params=pltpu.CompilerParams(vmem_limit_bytes=VMEM_LIMIT),
        cost_estimate=pl.CostEstimate(flops=0, bytes_accessed=0, transcendentals=0),
    )(starts, index, embeddings, *after)


def best_of_rows(acc, size):
    return jnp.max(jnp.transpose(acc), axis=0, keepdims=True)[:, :size]


def gram_kernel(passes, count, size, first, *refs):
    chunks = refs[:count]
    cluster_row, cluster_column, before_ref, best_ref, held, acc, sems = refs[count:]
    limit = count * size

    def copy(i):
        return pltpu.make_async_copy(chunks[i], held.at[pl.ds(i * size, size)], sems.at[i])

    def arrive(i):
        rows = held.at[pl.ds(0, size)]
        pltpu.make_async_copy(rows, rows, sems.at[i]).wait()

    for i in first:
        copy(i).start()
    for i in range(count):
        if i not in first:
            copy(i).start()
    best_ref[...] = before_ref[...]
    for i in first:
        copy(i).wait()
    for n, (chunk, news, groups, group, meets, last) in enumerate(passes):
        height = news * size
        acc[...] = jnp.full_like(acc, -1.0)
        rows = held[chunk * size : chunk * size + height, :]
        left = cluster_column[n]
        left = jnp.concatenate([left, left], axis=1)

        def tile(start, special, chunk=chunk, height=height, rows=rows, left=left):
            gram = lax.dot_general(
                rows, held[pl.ds(start, BLK), :], NT, preferred_element_type=jnp.float32
            )
            counts = left == cluster_row[:, pl.ds(start, BLK)]
            if special:
                column = start + lax.broadcasted_iota(jnp.int32, (height, BLK), 1)
                row = chunk * size + lax.broadcasted_iota(jnp.int32, (height, BLK), 0)
                counts = counts & (column != row) & (column < limit)
            values = jnp.where(counts, gram, jnp.float32(-1.0))
            top = jnp.max(values, axis=0, keepdims=True)
            best_ref[:, pl.ds(start, BLK)] = jnp.maximum(best_ref[:, pl.ds(start, BLK)], top)
            acc[0:height, :] = jnp.maximum(
                acc[0:height, :], jnp.maximum(values[:, :LANES], values[:, LANES:])
            )

        def visit(u, _, n=n, group=group, meets=meets, tile=tile):
            if n == 0:
                for i in (2 * u, 2 * u + 1):

                    @pl.when(i < first[0])
                    def _(i=i):
                        arrive(i)

            for t in range(group):
                tile(pl.multiple_of((u * group + t) * BLK, BLK), meets)
            return 0

        lax.fori_loop(0, groups, visit, 0)
        if n == 0:
            for i in range(count):
                if i not in first and not i < min(2 * groups, first[0]):
                    arrive(i)
        for t in last:
            tile(t * BLK, True)
        span = slice(chunk * size, chunk * size + height)
        best_ref[:, span] = jnp.maximum(best_ref[:, span], best_of_rows(acc[...], height))


def gram_best(chunks, cluster_row, cluster_column, before, passes, first):
    count = len(chunks)
    size, width = chunks[0].shape
    total = before.shape[1]
    held = -(-count * size // BLK) * BLK
    tall = max(news for _, news, *_ in passes) * size
    padded = -(-tall // LANES) * LANES
    work = sum(news * (groups * group + len(last)) * BLK for _, news, groups, group, _, last in passes)
    return pl.pallas_call(
        functools.partial(gram_kernel, passes, count, size, first),
        out_shape=jax.ShapeDtypeStruct((1, total), jnp.float32),
        in_specs=[pl.BlockSpec(memory_space=pl.ANY)] * count
        + [pl.BlockSpec(memory_space=pltpu.VMEM)] * 3,
        out_specs=pl.BlockSpec(memory_space=pltpu.VMEM),
        scratch_shapes=[
            pltpu.VMEM((held, width), jnp.bfloat16),
            pltpu.VMEM((padded, LANES), jnp.float32),
            pltpu.SemaphoreType.DMA((count,)),
        ],
        compiler_params=pltpu.CompilerParams(vmem_limit_bytes=VMEM_LIMIT),
        cost_estimate=pl.CostEstimate(flops=0, bytes_accessed=0, transcendentals=0),
    )(*chunks, cluster_row, cluster_column, before)


def one_pass(chunk, news, count, size):
    group = 3
    groups = chunk * size // (group * BLK)
    tiles = -(-count * size // BLK)
    return ((chunk, news, groups, group, False, tuple(range(groups * group, tiles))),)


def finish_kernel(size, order_ref, own_ref, other_ref, clusters_ref, column_ref, best_ref, out_ref, acc):
    gram = lax.dot_general(own_ref[...], other_ref[...], NT, preferred_element_type=jnp.float32)
    left = jnp.tile(column_ref[...], (1, -(-size // LANES)))[:, :size]
    last = 15 * size
    values = jnp.where(left == clusters_ref[:, last : last + size], gram, jnp.float32(-1.0))
    acc[...] = jnp.full_like(acc, -1.0)
    acc[0:size, :] = jnp.broadcast_to(jnp.max(values, axis=1, keepdims=True), (size, LANES))
    for i in range(16):
        found = best_ref[:, i * size : (i + 1) * size]
        if i == 14:
            found = jnp.maximum(found, best_of_rows(acc[...], size))
        if i == 15:
            found = jnp.maximum(found, jnp.max(values, axis=0, keepdims=True))
        place = order_ref[i]
        source, half = place // 2, place % 2
        for rep in range(4):
            out_ref[source * 4 + rep, pl.ds(half, 1), :] = found


def finish(order, own, other, clusters, column, best):
    size = own.shape[0]
    padded = -(-size // LANES) * LANES
    return pl.pallas_call(
        functools.partial(finish_kernel, size),
        out_shape=jax.ShapeDtypeStruct((32, 2, size), jnp.float32),
        in_specs=[pl.BlockSpec(memory_space=pltpu.SMEM)]
        + [pl.BlockSpec(memory_space=pltpu.VMEM)] * 5,
        out_specs=pl.BlockSpec(memory_space=pltpu.VMEM),
        scratch_shapes=[pltpu.VMEM((padded, LANES), jnp.float32)],
        compiler_params=pltpu.CompilerParams(vmem_limit_bytes=VMEM_LIMIT),
    )(order, own, other, clusters, column, best)


def settle_kernel(sources, size, high, index_ref, values_ref, out_ref, left_ref, right_ref):
    wide = left_ref.shape[1] // len(sources)
    left_ref[...] = jnp.zeros_like(left_ref)
    right_ref[...] = jnp.zeros_like(right_ref)
    rows = lax.broadcasted_iota(jnp.int32, (high, size), 0)
    lanes = lax.broadcasted_iota(jnp.int32, (LANES, size), 0)
    for g, places in enumerate(sources):
        index = index_ref[g // 2, g % 2 : g % 2 + 1, :] if index_ref.ndim == 3 else index_ref[g : g + 1, :]
        value = values_ref[places[0][0], places[0][1] : places[0][1] + 1, :]
        for a, b in places[1:]:
            value = jnp.maximum(value, values_ref[a, b : b + 1, :])
        span = slice(g * wide, g * wide + size)
        here = rows == index // LANES
        for piece in range(3):
            head = value.astype(jnp.bfloat16).astype(jnp.float32)
            value = value - head
            left_ref[piece * high : (piece + 1) * high, span] = jnp.where(here, head, 0.0).astype(
                jnp.bfloat16
            )
        right_ref[:, span] = jnp.where(lanes == index % LANES, 1.0, 0.0).astype(jnp.bfloat16)
    total = lax.dot_general(left_ref[...], right_ref[...], NT, preferred_element_type=jnp.float32)
    total = total[2 * high : 3 * high] + total[high : 2 * high] + total[:high]
    out_ref[...] = total[: out_ref.shape[0]]


def settle(index, values, sources, documents):
    size = index.shape[-1]
    high = -(-documents // (16 * LANES)) * 16
    wide = -(-size // LANES) * LANES * len(sources)
    out = pl.pallas_call(
        functools.partial(settle_kernel, sources, size, high),
        out_shape=jax.ShapeDtypeStruct((documents // LANES, LANES), jnp.float32),
        scratch_shapes=[
            pltpu.VMEM((3 * high, wide), jnp.bfloat16),
            pltpu.VMEM((LANES, wide), jnp.bfloat16),
        ],
        compiler_params=pltpu.CompilerParams(vmem_limit_bytes=VMEM_LIMIT),
    )(index, values)
    return out.reshape(-1)


def hosted(embeddings, send_index, place_index, slot_cluster):
    documents = embeddings.shape[0]
    share = send_index.shape[0] // 8
    size = share // 2
    s, rep = lax.axis_index("shard"), lax.axis_index("rep")
    axes = ("shard", "rep")
    sends, order = plan()
    halves = np.arange(4)[:, None] % 2 ^ np.array([0, 0, 0, 0, 1])
    starts = sends[:, :, [0, 1, 2, 3, 3]] * share + (halves * size).astype(np.int32)
    starts = jnp.asarray(starts)[s, rep]
    order = jnp.asarray(order)[s, rep]
    clusters = lax.ppermute(arrival_clusters(place_index, slot_cluster), axes, metadata_pairs())
    clusters = clusters.reshape(16, size)[order]
    early = gather_rows(embeddings, send_index, starts[:2], size)

    def go(step, chunk):
        return lax.ppermute(chunk, axes, round_pairs(step - 1))

    def swap(chunk):
        return lax.ppermute(chunk, axes, SIBLINGS)

    own, other = [None] * 8, [None] * 8
    for step in (1, 2, 3):
        own[step] = go(step, early[(step - 1) // 2])
    own[4] = go(4, tie(early[1], own[1]))
    late = gather_rows(embeddings, send_index, starts[2:], size, (own[1],))
    own[0], other[0] = late[1], late[2]
    other[1] = swap(own[1])
    other[2] = swap(own[2])
    own[5] = go(5, tie(late[0], own[2]))
    def columns(chunk, news):
        part = clusters[chunk : chunk + news].reshape(1, news * size, 1)
        return jnp.broadcast_to(part, (1, news * size, LANES))

    flat = clusters.reshape(1, 16 * size)
    best = jnp.full((1, 16 * size), -1.0, jnp.float32)

    def score(best, chunk, news, count):
        return gram_best(
            [(own, other)[side][r] for r, side in CHUNKS[:count]],
            flat,
            columns(chunk, news),
            best,
            one_pass(chunk, news, count, size),
            tuple(range(chunk, chunk + news)),
        )

    best = score(best, 0, 2, 4)
    own[3] = tie(own[3], best)
    other[3] = swap(own[3])
    own[6] = go(6, tie(late[0], own[3]))
    own[4] = tie(own[4], best)
    other[4] = swap(own[4])
    own[7] = go(7, tie(late[1], own[4]))
    best = score(best, 4, 2, 8)
    own[5] = tie(own[5], best)
    other[5] = swap(own[5])
    own[6] = tie(own[6], best)
    other[6] = swap(own[6])
    best = score(best, 8, 2, 12)
    own[7] = tie(own[7], best)
    other[7] = swap(own[7])
    best = score(best, 12, 1, 14)
    best = score(best, 14, 1, 15)
    outbound = finish(order, own[7], other[7], flat, columns(14, 1)[0], best)
    returned = lax.all_to_all(outbound, axes, split_axis=0, concat_axis=0, tiled=True)
    sources = []
    for owner in range(8):
        host, y = host_of(owner)
        for half in range(2):
            sources.append(tuple((host * 4 + y * 2 + core, half) for core in range(2)))
    return settle(send_index.reshape(8, 2, size), returned, tuple(sources), documents)


def gathered(embeddings, send_index, place_index, slot_cluster):
    documents, width = embeddings.shape
    owners = lax.axis_size("shard")
    reps = lax.axis_size("rep")
    share = send_index.shape[0] // owners
    outgoing = normalize(embeddings.at[send_index].get(mode="promise_in_bounds"))
    arrived = lax.all_to_all(
        outgoing.reshape(owners, share, width), "shard", split_axis=0, concat_axis=0, tiled=True
    )
    parts = 16
    size = documents // parts
    news = parts // reps
    turn = lax.axis_index("rep") * news
    arrived = jnp.roll(arrived.reshape(parts, size, width), -turn, axis=0)
    clusters = arrival_clusters(place_index, slot_cluster).reshape(parts, size)
    clusters = jnp.roll(clusters, -turn, axis=0)
    column = jnp.broadcast_to(clusters[:news].reshape(1, -1, 1), (1, news * size, LANES))
    best = jnp.full((1, documents), -1.0, jnp.float32)
    tiles = tuple(range(documents // BLK))
    passes = ((0, news, 0, 1, True, tiles),)
    best = gram_best(
        [arrived[i] for i in range(parts)], clusters.reshape(1, -1), column, best, passes, tuple(range(news))
    )
    best = lax.all_gather(best[0, : news * size], "rep", axis=0, tiled=True)
    returned = lax.all_to_all(
        best.reshape(owners, share), "shard", split_axis=0, concat_axis=0, tiled=True
    )
    sources = tuple(((0, g),) for g in range(parts))
    return settle(send_index.reshape(parts, size), returned.reshape(1, parts, size), sources, documents)


def solution(mesh):
    planned = mesh.shape["shard"] == 8 and mesh.shape["rep"] == 4

    def shards(embeddings, send_index, place_index, slot_cluster, pair_list):
        del pair_list
        run = hosted if planned else gathered
        return run(embeddings, send_index, place_index, slot_cluster)

    return jax.shard_map(
        shards,
        mesh=mesh,
        in_specs=(P("shard", None), P("shard"), P("shard"), P("shard"), P(("shard", "rep"), None)),
        out_specs=P("shard"),
        check_vma=False,
    )
```

```python
import functools

import jax
import jax.numpy as jnp
import numpy as np
from jax import lax
from jax.experimental import pallas as pl
from jax.experimental.pallas import tpu as pltpu
from jax.sharding import PartitionSpec as P

BLK = 256
LANES = 128
NT = (((1,), (1,)), ((), ()))
VMEM_LIMIT = 56 * 1024 * 1024
LONG = 25_000_000_000

HOSTS = (2, 3, 4, 5)
ROUNDS = ((4, 6, 5, 7, 2, 1, 3), (2, 1, 3, 6, 4, 7, 5))


CHUNKS = (
    (0, 0), (1, 0), (2, 0), (0, 1), (1, 1), (2, 1),
    (3, 0), (4, 0), (3, 1), (4, 1),
    (5, 0), (6, 0), (5, 1), (6, 1),
    (7, 0), (7, 1),
)


def host_of(owner):
    z, x = owner // 2, owner % 2
    return (1 if z < 2 else 2) * 2 + x, z % 2


def plan():
    owner_at = {host_of(owner): owner for owner in range(8)}
    sends = np.zeros((8, 4, 4), np.int32)
    order = np.zeros((8, 4, 16), np.int32)
    for s in range(8):
        for rep in range(4):
            y, core = divmod(rep, 2)
            steps = [(step, k) for step, k in enumerate(ROUNDS[core]) if s ^ k in HOSTS]
            assert [step // 2 for step, _ in steps] == list(range(len(steps)))
            targets = [s ^ k for _, k in steps]
            if s in HOSTS:
                targets.append(s)
            sends[s, rep] = [owner_at[target, y] for target in targets]
            for side in range(2):
                half = core ^ side
                for step, k in enumerate((0,) + ROUNDS[half]):
                    order[s, rep, CHUNKS.index((step, side))] = (s ^ k) * 2 + half
    return sends, order


def round_pairs(step):
    pairs = []
    for rep in range(4):
        for host in HOSTS:
            pairs.append(((host ^ ROUNDS[rep % 2][step]) * 4 + rep, host * 4 + rep))
    return pairs


SIBLINGS = [(host * 4 + rep, host * 4 + (rep ^ 1)) for host in HOSTS for rep in range(4)]


def metadata_pairs():
    pairs = []
    for owner in range(8):
        host, y = host_of(owner)
        for core in range(2):
            pairs.append((owner * 4 + y * 2 + core, host * 4 + y * 2 + core))
    return pairs


def tie(value, *after):
    return lax.optimization_barrier((value, *after))[0]


def normalize(rows):
    wide = rows.astype(jnp.float32)
    return (wide * lax.rsqrt(jnp.sum(wide * wide, axis=1, keepdims=True) + 1e-06)).astype(
        jnp.bfloat16
    )


def arrival_clusters(place_index, slot_cluster):
    heads = slot_cluster.reshape(-1, BLK)[:, 0]
    block = place_index // BLK
    hit = block[None, :] == jnp.arange(heads.shape[0], dtype=jnp.int32)[:, None]
    return jnp.sum(jnp.where(hit, heads[:, None], 0), axis=0)


def gather_kernel(count, size, sections, *refs):
    table_ref, index_ref, rows_ref = refs[:3]
    outs, (raw, wide, picked, sems) = refs[-4 - count : -4], refs[-4:]
    width = raw.shape[1]
    tiles = width // LANES
    part = raw.shape[0] // sections
    copies = []
    for i in range(sections):
        rows = pl.ds(i * part, part)
        copies.append(pltpu.make_async_copy(rows_ref.at[rows], raw.at[rows], sems.at[i]))
        copies[-1].start()
    step = 80
    for i in range(sections):
        copies[i].wait()

        def widen(j, _, i=i):
            first = i * part + j * step
            rows = raw[pl.ds(pl.multiple_of(first, step), step), :].astype(jnp.float32)
            for t in range(tiles):
                wide[pl.ds(first * tiles + t, step, stride=tiles), :] = rows[:, t * LANES : (t + 1) * LANES]
            return 0

        lax.fori_loop(0, part // step, widen, 0)
    group = 16
    for c in range(count):
        base = table_ref[c]

        def pick(j, _, c=c, base=base):
            for t in range(group):
                source = pl.multiple_of(index_ref[base + j * group + t] * tiles, tiles)
                picked[t * tiles : (t + 1) * tiles, :] = wide[pl.ds(source, tiles), :]
            rows = jnp.concatenate(
                [picked[pl.ds(t, group, stride=tiles), :] for t in range(tiles)], axis=1
            )
            scale = lax.rsqrt(jnp.sum(rows * rows, axis=1, keepdims=True) + 1e-06)
            outs[c][pl.ds(pl.multiple_of(j * group, group), group), :] = (rows * scale).astype(
                jnp.bfloat16
            )
            return 0

        lax.fori_loop(0, size // group, pick, 0)


def gather_rows(embeddings, index, starts, size, work=0, after=()):
    documents, width = embeddings.shape
    count = starts.shape[0]
    sections = 8
    return pl.pallas_call(
        functools.partial(gather_kernel, count, size, sections),
        out_shape=[jax.ShapeDtypeStruct((size, width), jnp.bfloat16)] * count,
        in_specs=[
            pl.BlockSpec(memory_space=pltpu.SMEM),
            pl.BlockSpec(memory_space=pltpu.SMEM),
            pl.BlockSpec(memory_space=pl.ANY),
        ]
        + [pl.BlockSpec(memory_space=pl.ANY)] * len(after),
        out_specs=[pl.BlockSpec(memory_space=pltpu.VMEM)] * count,
        scratch_shapes=[
            pltpu.VMEM((documents, width), jnp.bfloat16),
            pltpu.VMEM((documents * width // LANES, LANES), jnp.float32),
            pltpu.VMEM((16 * width // LANES, LANES), jnp.float32),
            pltpu.SemaphoreType.DMA((sections,)),
        ],
        compiler_params=pltpu.CompilerParams(vmem_limit_bytes=VMEM_LIMIT),
        cost_estimate=pl.CostEstimate(flops=work, bytes_accessed=0, transcendentals=0),
    )(starts, index, embeddings, *after)


def best_of_rows(acc, size):
    return jnp.max(jnp.transpose(acc), axis=0, keepdims=True)[:, :size]


def as_column(row_ref, start, size):
    wide = -(-size // LANES) * LANES
    row = row_ref[:, start : start + wide]
    return jnp.transpose(jnp.broadcast_to(row, (LANES, wide)))[:size]


def gram_kernel(passes, count, size, first, *refs):
    chunks = refs[:count]
    cluster_row, before_ref, best_ref, held, acc, sems = refs[count:]
    limit = count * size

    def copy(i):
        return pltpu.make_async_copy(chunks[i], held.at[pl.ds(i * size, size)], sems.at[i])

    def arrive(i):
        rows = held.at[pl.ds(0, size)]
        pltpu.make_async_copy(rows, rows, sems.at[i]).wait()

    for i in first:
        copy(i).start()
    for i in range(count):
        if i not in first:
            copy(i).start()
    best_ref[...] = before_ref[...]
    for i in first:
        copy(i).wait()
    for n, (chunk, news, groups, group, meets, last) in enumerate(passes):
        height = news * size
        acc[...] = jnp.full_like(acc, -1.0)
        rows = held[chunk * size : chunk * size + height, :]
        left = as_column(cluster_row, chunk * size, height)
        left = jnp.concatenate([left, left], axis=1)

        def tile(start, special, chunk=chunk, height=height, rows=rows, left=left):
            gram = lax.dot_general(
                rows, held[pl.ds(start, BLK), :], NT, preferred_element_type=jnp.float32
            )
            counts = left == cluster_row[:, pl.ds(start, BLK)]
            if special:
                column = start + lax.broadcasted_iota(jnp.int32, (height, BLK), 1)
                row = chunk * size + lax.broadcasted_iota(jnp.int32, (height, BLK), 0)
                counts = counts & (column != row) & (column < limit)
            values = jnp.where(counts, gram, jnp.float32(-1.0))
            top = jnp.max(values, axis=0, keepdims=True)
            best_ref[:, pl.ds(start, BLK)] = jnp.maximum(best_ref[:, pl.ds(start, BLK)], top)
            acc[0:height, :] = jnp.maximum(
                acc[0:height, :], jnp.maximum(values[:, :LANES], values[:, LANES:])
            )

        def visit(u, _, n=n, group=group, meets=meets, tile=tile):
            if n == 0:
                for i in (2 * u, 2 * u + 1):

                    @pl.when(i < first[0])
                    def _(i=i):
                        arrive(i)

            for t in range(group):
                tile(pl.multiple_of((u * group + t) * BLK, BLK), meets)
            return 0

        lax.fori_loop(0, groups, visit, 0)
        if n == 0:
            for i in range(count):
                if i not in first and not i < min(2 * groups, first[0]):
                    arrive(i)
        for t in last:
            tile(t * BLK, True)
        span = slice(chunk * size, chunk * size + height)
        best_ref[:, span] = jnp.maximum(best_ref[:, span], best_of_rows(acc[...], height))


def gram_best(chunks, cluster_row, before, passes, first):
    count = len(chunks)
    size, width = chunks[0].shape
    total = before.shape[1]
    held = -(-count * size // BLK) * BLK
    tall = max(news for _, news, *_ in passes) * size
    padded = -(-tall // LANES) * LANES
    return pl.pallas_call(
        functools.partial(gram_kernel, passes, count, size, first),
        out_shape=jax.ShapeDtypeStruct((1, total), jnp.float32),
        in_specs=[pl.BlockSpec(memory_space=pl.ANY)] * count
        + [pl.BlockSpec(memory_space=pltpu.VMEM)] * 2,
        out_specs=pl.BlockSpec(memory_space=pltpu.VMEM),
        scratch_shapes=[
            pltpu.VMEM((held, width), jnp.bfloat16),
            pltpu.VMEM((padded, LANES), jnp.float32),
            pltpu.SemaphoreType.DMA((count,)),
        ],
        compiler_params=pltpu.CompilerParams(vmem_limit_bytes=VMEM_LIMIT),
        cost_estimate=pl.CostEstimate(flops=0, bytes_accessed=0, transcendentals=0),
    )(*chunks, cluster_row, before)


def one_pass(chunk, news, count, size):
    group = 3
    groups = chunk * size // (group * BLK)
    tiles = -(-count * size // BLK)
    return ((chunk, news, groups, group, False, tuple(range(groups * group, tiles))),)


def finish_kernel(size, order_ref, own_ref, other_ref, clusters_ref, best_ref, out_ref, acc):
    gram = lax.dot_general(own_ref[...], other_ref[...], NT, preferred_element_type=jnp.float32)
    left = as_column(clusters_ref, 14 * size, size)
    left = jnp.tile(left, (1, -(-size // LANES)))[:, :size]
    last = 15 * size
    values = jnp.where(left == clusters_ref[:, last : last + size], gram, jnp.float32(-1.0))
    acc[...] = jnp.full_like(acc, -1.0)
    acc[0:size, :] = jnp.broadcast_to(jnp.max(values, axis=1, keepdims=True), (size, LANES))
    for i in range(16):
        found = best_ref[:, i * size : (i + 1) * size]
        if i == 14:
            found = jnp.maximum(found, best_of_rows(acc[...], size))
        if i == 15:
            found = jnp.maximum(found, jnp.max(values, axis=0, keepdims=True))
        place = order_ref[i]
        source, half = place // 2, place % 2
        for rep in range(4):
            out_ref[source * 4 + rep, pl.ds(half, 1), :] = found


def finish(order, own, other, clusters, best):
    size = own.shape[0]
    padded = -(-size // LANES) * LANES
    return pl.pallas_call(
        functools.partial(finish_kernel, size),
        out_shape=jax.ShapeDtypeStruct((32, 2, size), jnp.float32),
        in_specs=[pl.BlockSpec(memory_space=pltpu.SMEM)]
        + [pl.BlockSpec(memory_space=pltpu.VMEM)] * 4,
        out_specs=pl.BlockSpec(memory_space=pltpu.VMEM),
        scratch_shapes=[pltpu.VMEM((padded, LANES), jnp.float32)],
        compiler_params=pltpu.CompilerParams(vmem_limit_bytes=VMEM_LIMIT),
    )(order, own, other, clusters, best)


def settle_kernel(sources, size, high, index_ref, values_ref, out_ref, left_ref, right_ref):
    wide = left_ref.shape[1] // len(sources)
    left_ref[...] = jnp.zeros_like(left_ref)
    right_ref[...] = jnp.zeros_like(right_ref)
    rows = lax.broadcasted_iota(jnp.int32, (high, size), 0)
    lanes = lax.broadcasted_iota(jnp.int32, (LANES, size), 0)
    for g, places in enumerate(sources):
        index = index_ref[g // 2, g % 2 : g % 2 + 1, :] if index_ref.ndim == 3 else index_ref[g : g + 1, :]
        value = values_ref[places[0][0], places[0][1] : places[0][1] + 1, :]
        for a, b in places[1:]:
            value = jnp.maximum(value, values_ref[a, b : b + 1, :])
        span = slice(g * wide, g * wide + size)
        here = rows == index // LANES
        for piece in range(3):
            head = value.astype(jnp.bfloat16).astype(jnp.float32)
            value = value - head
            left_ref[piece * high : (piece + 1) * high, span] = jnp.where(here, head, 0.0).astype(
                jnp.bfloat16
            )
        right_ref[:, span] = jnp.where(lanes == index % LANES, 1.0, 0.0).astype(jnp.bfloat16)
    total = lax.dot_general(left_ref[...], right_ref[...], NT, preferred_element_type=jnp.float32)
    total = total[2 * high : 3 * high] + total[high : 2 * high] + total[:high]
    out_ref[...] = total[: out_ref.shape[0]]


def settle(index, values, sources, documents):
    size = index.shape[-1]
    high = -(-documents // (16 * LANES)) * 16
    wide = -(-size // LANES) * LANES * len(sources)
    out = pl.pallas_call(
        functools.partial(settle_kernel, sources, size, high),
        out_shape=jax.ShapeDtypeStruct((documents // LANES, LANES), jnp.float32),
        scratch_shapes=[
            pltpu.VMEM((3 * high, wide), jnp.bfloat16),
            pltpu.VMEM((LANES, wide), jnp.bfloat16),
        ],
        compiler_params=pltpu.CompilerParams(vmem_limit_bytes=VMEM_LIMIT),
    )(index, values)
    return out.reshape(-1)


def hosted(embeddings, send_index, place_index, slot_cluster):
    documents = embeddings.shape[0]
    share = send_index.shape[0] // 8
    size = share // 2
    s, rep = lax.axis_index("shard"), lax.axis_index("rep")
    axes = ("shard", "rep")
    sends, order = plan()
    halves = np.arange(4)[:, None] % 2 ^ np.array([0, 0, 0, 0, 1])
    starts = sends[:, :, [0, 1, 2, 3, 3]] * share + (halves * size).astype(np.int32)
    starts = jnp.asarray(starts)[s, rep]
    order = jnp.asarray(order)[s, rep]
    clusters = lax.ppermute(arrival_clusters(place_index, slot_cluster), axes, metadata_pairs())
    clusters = clusters.reshape(16, size)[order]
    early = gather_rows(embeddings, send_index, starts[:2], size)

    def go(step, chunk):
        return lax.ppermute(chunk, axes, round_pairs(step - 1))

    def swap(chunk):
        return lax.ppermute(chunk, axes, SIBLINGS)

    own, other = [None] * 8, [None] * 8
    for step in (1, 2, 3, 4):
        own[step] = go(step, early[(step - 1) // 2])
    late = gather_rows(embeddings, send_index, starts[2:], size, LONG, (early[0],))
    own[0], other[0] = late[1], late[2]
    flat = clusters.reshape(1, 16 * size)

    def score(best, chunk, news, count):
        return gram_best(
            [(own, other)[side][r] for r, side in CHUNKS[:count]],
            flat,
            best,
            one_pass(chunk, news, count, size),
            tuple(range(chunk, chunk + news)),
        )

    best = jnp.full((1, 16 * size), -1.0, jnp.float32)
    own[1], own[2] = tie(own[1], late[0]), tie(own[2], late[0])
    other[1], other[2] = swap(own[1]), swap(own[2])
    own[5] = go(5, tie(late[0], own[1]))
    own[6] = go(6, tie(late[0], own[2]))
    best = score(best, 0, 3, 6)
    own[3], own[4] = tie(own[3], best), tie(own[4], best)
    other[3], other[4] = swap(own[3]), swap(own[4])
    own[7] = go(7, tie(late[1], own[3]))
    best = score(best, 6, 2, 10)
    own[5], own[6] = tie(own[5], best), tie(own[6], best)
    other[5], other[6] = swap(own[5]), swap(own[6])
    best = score(best, 10, 2, 14)
    own[7] = tie(own[7], best)
    other[7] = swap(own[7])
    best = score(best, 14, 1, 15)
    outbound = finish(order, own[7], other[7], flat, best)
    returned = lax.all_to_all(outbound, axes, split_axis=0, concat_axis=0, tiled=True)
    sources = []
    for owner in range(8):
        host, y = host_of(owner)
        for half in range(2):
            sources.append(tuple((host * 4 + y * 2 + core, half) for core in range(2)))
    return settle(send_index.reshape(8, 2, size), returned, tuple(sources), documents)


def gathered(embeddings, send_index, place_index, slot_cluster):
    documents, width = embeddings.shape
    owners = lax.axis_size("shard")
    reps = lax.axis_size("rep")
    share = send_index.shape[0] // owners
    outgoing = normalize(embeddings.at[send_index].get(mode="promise_in_bounds"))
    arrived = lax.all_to_all(
        outgoing.reshape(owners, share, width), "shard", split_axis=0, concat_axis=0, tiled=True
    )
    parts = 16
    size = documents // parts
    news = parts // reps
    turn = lax.axis_index("rep") * news
    arrived = jnp.roll(arrived.reshape(parts, size, width), -turn, axis=0)
    clusters = arrival_clusters(place_index, slot_cluster).reshape(parts, size)
    clusters = jnp.roll(clusters, -turn, axis=0)
    best = jnp.full((1, documents), -1.0, jnp.float32)
    tiles = tuple(range(documents // BLK))
    passes = ((0, news, 0, 1, True, tiles),)
    best = gram_best(
        [arrived[i] for i in range(parts)], clusters.reshape(1, -1), best, passes, tuple(range(news))
    )
    best = lax.all_gather(best[0, : news * size], "rep", axis=0, tiled=True)
    returned = lax.all_to_all(
        best.reshape(owners, share), "shard", split_axis=0, concat_axis=0, tiled=True
    )
    sources = tuple(((0, g),) for g in range(parts))
    return settle(send_index.reshape(parts, size), returned.reshape(1, parts, size), sources, documents)


def solution(mesh):
    planned = mesh.shape["shard"] == 8 and mesh.shape["rep"] == 4

    def shards(embeddings, send_index, place_index, slot_cluster, pair_list):
        del pair_list
        run = hosted if planned else gathered
        return run(embeddings, send_index, place_index, slot_cluster)

    return jax.shard_map(
        shards,
        mesh=mesh,
        in_specs=(P("shard", None), P("shard"), P("shard"), P("shard"), P(("shard", "rep"), None)),
        out_specs=P("shard"),
        check_vma=False,
    )
```

```python
import functools

import jax
import jax.numpy as jnp
import numpy as np
from jax import lax
from jax.experimental import pallas as pl
from jax.experimental.pallas import tpu as pltpu
from jax.sharding import PartitionSpec as P

BLK = 256
LANES = 128
NT = (((1,), (1,)), ((), ()))
VMEM_LIMIT = 56 * 1024 * 1024
LONG = 25_000_000_000

HOSTS = (2, 3, 4, 5)
ROUNDS = ((4, 6, 5, 7, 2, 1, 3), (2, 1, 3, 6, 4, 7, 5))


CHUNKS = (
    (0, 0), (1, 0), (2, 0), (0, 1),
    (1, 1), (2, 1), (3, 0), (4, 0),
    (3, 1), (4, 1), (5, 0), (6, 0),
    (5, 1), (6, 1), (7, 0), (7, 1),
)


def host_of(owner):
    z, x = owner // 2, owner % 2
    return (1 if z < 2 else 2) * 2 + x, z % 2


def plan():
    owner_at = {host_of(owner): owner for owner in range(8)}
    sends = np.zeros((8, 4, 4), np.int32)
    order = np.zeros((8, 4, 16), np.int32)
    hosts = np.zeros((8, 4), np.int32)
    for s in range(8):
        for rep in range(4):
            y, core = divmod(rep, 2)
            steps = [(step, k) for step, k in enumerate(ROUNDS[core]) if s ^ k in HOSTS]
            assert [step // 2 for step, _ in steps] == list(range(len(steps)))
            targets = [s ^ k for _, k in steps]
            if s in HOSTS:
                targets.append(s)
                hosts[s, rep] = owner_at[s, y]
            sends[s, rep] = [owner_at[target, y] for target in targets]
            for side in range(2):
                half = core ^ side
                for step, k in enumerate((0,) + ROUNDS[half]):
                    order[s, rep, CHUNKS.index((step, side))] = (s ^ k) * 2 + half
    return sends, order, hosts


def round_pairs(step):
    pairs = []
    for rep in range(4):
        for host in HOSTS:
            pairs.append(((host ^ ROUNDS[rep % 2][step]) * 4 + rep, host * 4 + rep))
    return pairs


SIBLINGS = [(host * 4 + rep, host * 4 + (rep ^ 1)) for host in HOSTS for rep in range(4)]


def tie(value, *after):
    return lax.optimization_barrier((value, *after))[0]


def normalize(rows):
    wide = rows.astype(jnp.float32)
    return (wide * lax.rsqrt(jnp.sum(wide * wide, axis=1, keepdims=True) + 1e-06)).astype(
        jnp.bfloat16
    )


def arrival_clusters(place_index, slot_cluster):
    heads = slot_cluster.reshape(-1, BLK)[:, 0]
    block = place_index // BLK
    hit = block[None, :] == jnp.arange(heads.shape[0], dtype=jnp.int32)[:, None]
    return jnp.sum(jnp.where(hit, heads[:, None], 0), axis=0)


def gather_kernel(count, size, group, sections, named, *refs):
    table_ref, index_ref, rows_ref = refs[:3]
    raw, wide, picked, sems = refs[-4:]
    outs = refs[-4 - count : -4]
    width = raw.shape[1]
    tiles = width // LANES
    part = raw.shape[0] // sections
    copies = []
    for i in range(sections):
        rows = pl.ds(i * part, part)
        copies.append(pltpu.make_async_copy(rows_ref.at[rows], raw.at[rows], sems.at[i]))
        copies[-1].start()
    if named:
        place_ref, slots_ref = refs[3:5]
        block = place_ref[...] // BLK
        found = jnp.zeros_like(block)
        for i in range(slots_ref.shape[0] // BLK):
            found = jnp.where(block == i, slots_ref[i * BLK], found)
        refs[-5 - count][...] = found
    step = 80
    for i in range(sections):
        copies[i].wait()

        def widen(j, _, i=i):
            first = i * part + j * step
            rows = raw[pl.ds(pl.multiple_of(first, step), step), :].astype(jnp.float32)
            for t in range(tiles):
                wide[pl.ds(first * tiles + t, step, stride=tiles), :] = rows[:, t * LANES : (t + 1) * LANES]
            return 0

        lax.fori_loop(0, part // step, widen, 0)
    for c in range(count):
        base = table_ref[c]

        def pick(j, _, c=c, base=base):
            for t in range(group):
                source = pl.multiple_of(index_ref[base + j * group + t] * tiles, tiles)
                picked[t * tiles : (t + 1) * tiles, :] = wide[pl.ds(source, tiles), :]
            for first in range(0, group, 16):
                rows = jnp.concatenate(
                    [picked[pl.ds(first * tiles + t, 16, stride=tiles), :] for t in range(tiles)],
                    axis=1,
                )
                scale = lax.rsqrt(jnp.sum(rows * rows, axis=1, keepdims=True) + 1e-06)
                outs[c][pl.ds(pl.multiple_of(j * group + first, 16), 16), :] = (rows * scale).astype(
                    jnp.bfloat16
                )
            return 0

        lax.fori_loop(0, size // group, pick, 0)


def gather_rows(embeddings, index, starts, size, work=0, names=(), after=()):
    documents, width = embeddings.shape
    count = starts.shape[0]
    sections = 8
    group = 80
    extra = []
    if names:
        places = names[0].reshape(-1, LANES)
        names = (places, names[1])
        extra = [jax.ShapeDtypeStruct(places.shape, jnp.int32)]
    return pl.pallas_call(
        functools.partial(gather_kernel, count, size, group, sections, bool(names)),
        out_shape=extra + [jax.ShapeDtypeStruct((size, width), jnp.bfloat16)] * count,
        in_specs=[
            pl.BlockSpec(memory_space=pltpu.SMEM),
            pl.BlockSpec(memory_space=pltpu.SMEM),
            pl.BlockSpec(memory_space=pl.ANY),
        ]
        + [pl.BlockSpec(memory_space=pltpu.VMEM), pl.BlockSpec(memory_space=pltpu.SMEM)][: len(names)]
        + [pl.BlockSpec(memory_space=pl.ANY)] * len(after),
        out_specs=[pl.BlockSpec(memory_space=pltpu.VMEM)] * (count + len(extra)),
        scratch_shapes=[
            pltpu.VMEM((documents, width), jnp.bfloat16),
            pltpu.VMEM((documents * width // LANES, LANES), jnp.float32),
            pltpu.VMEM((group * width // LANES, LANES), jnp.float32),
            pltpu.SemaphoreType.DMA((sections,)),
        ],
        compiler_params=pltpu.CompilerParams(vmem_limit_bytes=VMEM_LIMIT),
        cost_estimate=pl.CostEstimate(flops=work, bytes_accessed=0, transcendentals=0),
    )(starts, index, embeddings, *names, *after)


def best_of_rows(acc, size):
    return jnp.max(jnp.transpose(acc), axis=0, keepdims=True)[:, :size]


def as_column(row_ref, start, size):
    wide = -(-size // LANES) * LANES
    row = row_ref[:, start : start + wide]
    return jnp.transpose(jnp.broadcast_to(row, (LANES, wide)))[:size]


def gram_kernel(passes, loads, size, limit, *refs):
    chunks = refs[: len(loads)]
    cluster_row, before_ref, best_ref, held, acc, sems = refs[-6:]
    first = range(passes[0][0], passes[0][0] + passes[0][1])

    def copy(i):
        rows = held.at[pl.ds(i * size, size)]
        return pltpu.make_async_copy(chunks[loads.index(i)], rows, sems.at[i])

    def arrive(i):
        rows = held.at[pl.ds(0, size)]
        pltpu.make_async_copy(rows, rows, sems.at[i]).wait()

    for i in first:
        copy(i).start()
    for i in loads:
        if i not in first:
            copy(i).start()
    best_ref[...] = before_ref[...]
    for i in first:
        copy(i).wait()
    for n, (chunk, news, groups, group, meets, last) in enumerate(passes):
        height = news * size
        acc[...] = jnp.full_like(acc, -1.0)
        rows = held[chunk * size : chunk * size + height, :]
        left = as_column(cluster_row, chunk * size, height)
        left = jnp.concatenate([left, left], axis=1)

        def tile(start, special, chunk=chunk, height=height, rows=rows, left=left):
            gram = lax.dot_general(
                rows, held[pl.ds(start, BLK), :], NT, preferred_element_type=jnp.float32
            )
            counts = left == cluster_row[:, pl.ds(start, BLK)]
            if special:
                column = start + lax.broadcasted_iota(jnp.int32, (height, BLK), 1)
                row = chunk * size + lax.broadcasted_iota(jnp.int32, (height, BLK), 0)
                counts = counts & (column != row) & (column < limit)
            values = jnp.where(counts, gram, jnp.float32(-1.0))
            top = jnp.max(values, axis=0, keepdims=True)
            best_ref[:, pl.ds(start, BLK)] = jnp.maximum(best_ref[:, pl.ds(start, BLK)], top)
            acc[0:height, :] = jnp.maximum(
                acc[0:height, :], jnp.maximum(values[:, :LANES], values[:, LANES:])
            )

        def visit(u, _, n=n, group=group, meets=meets, tile=tile):
            if n == 0:
                for i in (2 * u, 2 * u + 1):

                    @pl.when(i < first[0])
                    def _(i=i):
                        arrive(i)

            for t in range(group):
                tile(pl.multiple_of((u * group + t) * BLK, BLK), meets)
            return 0

        lax.fori_loop(0, groups, visit, 0)
        if n == 0:
            for i in loads:
                if i not in first and not i < min(2 * groups, first[0]):
                    arrive(i)
        for t in last:
            tile(t * BLK, True)
        span = slice(chunk * size, chunk * size + height)
        best_ref[:, span] = jnp.maximum(best_ref[:, span], best_of_rows(acc[...], height))


def gram_best(chunks, loads, size, cluster_row, before, passes, after=()):
    width = chunks[0].shape[1]
    total = before.shape[1]
    limit = (max(loads) + 1) * size
    held = -(-limit // BLK) * BLK
    tall = max(news for _, news, *_ in passes) * size
    padded = -(-tall // LANES) * LANES
    return pl.pallas_call(
        functools.partial(gram_kernel, passes, loads, size, limit),
        out_shape=jax.ShapeDtypeStruct((1, total), jnp.float32),
        in_specs=[pl.BlockSpec(memory_space=pltpu.HBM)] * len(loads)
        + [pl.BlockSpec(memory_space=pl.ANY)] * len(after)
        + [pl.BlockSpec(memory_space=pltpu.VMEM)] * 2,
        out_specs=pl.BlockSpec(memory_space=pltpu.VMEM),
        scratch_shapes=[
            pltpu.VMEM((held, width), jnp.bfloat16),
            pltpu.VMEM((padded, LANES), jnp.float32),
            pltpu.SemaphoreType.DMA((max(loads) + 1,)),
        ],
        compiler_params=pltpu.CompilerParams(vmem_limit_bytes=VMEM_LIMIT),
        cost_estimate=pl.CostEstimate(flops=0, bytes_accessed=0, transcendentals=0),
    )(*chunks, *after, cluster_row, before)


def new_pass(chunk, news, count, size):
    group = 3
    groups = chunk * size // (group * BLK)
    tiles = -(-count * size // BLK)
    return (chunk, news, groups, group, False, tuple(range(groups * group, tiles)))


def late_pass(chunk, news, low, high, size):
    return (chunk, news, 0, 1, True, tuple(range(low * size // BLK, -(-high * size // BLK))))


def finish_kernel(size, order_ref, own_ref, other_ref, clusters_ref, best_ref, out_ref, acc):
    gram = lax.dot_general(own_ref[...], other_ref[...], NT, preferred_element_type=jnp.float32)
    left = as_column(clusters_ref, 14 * size, size)
    left = jnp.tile(left, (1, -(-size // LANES)))[:, :size]
    last = 15 * size
    values = jnp.where(left == clusters_ref[:, last : last + size], gram, jnp.float32(-1.0))
    acc[...] = jnp.full_like(acc, -1.0)
    acc[0:size, :] = jnp.broadcast_to(jnp.max(values, axis=1, keepdims=True), (size, LANES))
    for i in range(16):
        found = best_ref[:, i * size : (i + 1) * size]
        if i == 14:
            found = jnp.maximum(found, best_of_rows(acc[...], size))
        if i == 15:
            found = jnp.maximum(found, jnp.max(values, axis=0, keepdims=True))
        place = order_ref[i]
        source, half = place // 2, place % 2
        for rep in range(4):
            out_ref[source * 4 + rep, pl.ds(half, 1), :] = found


def finish(order, own, other, clusters, best):
    size = own.shape[0]
    padded = -(-size // LANES) * LANES
    return pl.pallas_call(
        functools.partial(finish_kernel, size),
        out_shape=jax.ShapeDtypeStruct((32, 2, size), jnp.float32),
        in_specs=[pl.BlockSpec(memory_space=pltpu.SMEM)]
        + [pl.BlockSpec(memory_space=pltpu.VMEM)] * 4,
        out_specs=pl.BlockSpec(memory_space=pltpu.VMEM),
        scratch_shapes=[pltpu.VMEM((padded, LANES), jnp.float32)],
        compiler_params=pltpu.CompilerParams(vmem_limit_bytes=VMEM_LIMIT),
    )(order, own, other, clusters, best)


def settle_kernel(sources, size, high, index_ref, values_ref, out_ref, left_ref, right_ref):
    wide = left_ref.shape[1] // len(sources)
    left_ref[...] = jnp.zeros_like(left_ref)
    right_ref[...] = jnp.zeros_like(right_ref)
    rows = lax.broadcasted_iota(jnp.int32, (high, size), 0)
    lanes = lax.broadcasted_iota(jnp.int32, (LANES, size), 0)
    for g, places in enumerate(sources):
        index = index_ref[g // 2, g % 2 : g % 2 + 1, :] if index_ref.ndim == 3 else index_ref[g : g + 1, :]
        value = values_ref[places[0][0], places[0][1] : places[0][1] + 1, :]
        for a, b in places[1:]:
            value = jnp.maximum(value, values_ref[a, b : b + 1, :])
        span = slice(g * wide, g * wide + size)
        here = rows == index // LANES
        for piece in range(3):
            head = value.astype(jnp.bfloat16).astype(jnp.float32)
            value = value - head
            left_ref[piece * high : (piece + 1) * high, span] = jnp.where(here, head, 0.0).astype(
                jnp.bfloat16
            )
        right_ref[:, span] = jnp.where(lanes == index % LANES, 1.0, 0.0).astype(jnp.bfloat16)
    total = lax.dot_general(left_ref[...], right_ref[...], NT, preferred_element_type=jnp.float32)
    total = total[2 * high : 3 * high] + total[high : 2 * high] + total[:high]
    out_ref[...] = total[: out_ref.shape[0]]


def settle(index, values, sources, documents):
    size = index.shape[-1]
    high = -(-documents // (16 * LANES)) * 16
    wide = -(-size // LANES) * LANES * len(sources)
    out = pl.pallas_call(
        functools.partial(settle_kernel, sources, size, high),
        out_shape=jax.ShapeDtypeStruct((documents // LANES, LANES), jnp.float32),
        scratch_shapes=[
            pltpu.VMEM((3 * high, wide), jnp.bfloat16),
            pltpu.VMEM((LANES, wide), jnp.bfloat16),
        ],
        compiler_params=pltpu.CompilerParams(vmem_limit_bytes=VMEM_LIMIT),
    )(index, values)
    return out.reshape(-1)


def hosted(embeddings, send_index, place_index, slot_cluster):
    documents = embeddings.shape[0]
    share = send_index.shape[0] // 8
    size = share // 2
    s, rep = lax.axis_index("shard"), lax.axis_index("rep")
    axes = ("shard", "rep")
    sends, order, hosts = plan()
    halves = np.arange(4)[:, None] % 2 ^ np.array([0, 0, 0, 0, 1])
    starts = sends[:, :, [0, 1, 2, 3, 3]] * share + (halves * size).astype(np.int32)
    starts = jnp.asarray(starts)[s, rep]
    order = jnp.asarray(order)[s, rep]
    clusters, early = gather_rows(
        embeddings, send_index, starts[:1], size, names=(place_index, slot_cluster)
    )
    clusters = lax.all_gather(clusters, "shard")[jnp.asarray(hosts)[s, rep]]
    clusters = clusters.reshape(16, size)[order]
    index = send_index.reshape(8, 2, size)

    def go(step, chunk):
        return lax.ppermute(chunk, axes, round_pairs(step - 1))

    def swap(chunk):
        return lax.ppermute(chunk, axes, SIBLINGS)

    own, other = [None] * 8, [None] * 8
    own[1], own[2] = go(1, early), go(2, early)
    late = gather_rows(embeddings, send_index, starts[1:], size, LONG, after=(early,))
    own[0], other[0] = late[2:]
    own[3], own[4] = go(3, late[0]), go(4, late[0])
    flat = clusters.reshape(1, 16 * size)

    def score(best, loads, passes, after=()):
        chunks = [(own, other)[side][r] for r, side in [CHUNKS[i] for i in loads]]
        return gram_best(chunks, tuple(loads), size, flat, best, passes, after)

    own[1], own[2] = tie(own[1], late[0]), tie(own[2], late[0])
    own[5] = go(5, tie(late[1], own[1]))
    own[6] = go(6, tie(late[1], own[2]))
    best = jnp.full((1, 16 * size), -1.0, jnp.float32)
    best = score(best, range(4), (new_pass(0, 3, 4, size),), (order, index))
    other[1], other[2] = swap(tie(own[1], best)), swap(tie(own[2], best))
    own[3], own[4] = tie(own[3], best), tie(own[4], best)
    own[7] = go(7, tie(late[2], own[3]))
    best = score(best, range(8), (new_pass(6, 2, 8, size), late_pass(1, 2, 4, 6, size)))
    other[3], other[4] = swap(tie(own[3], best)), swap(tie(own[4], best))
    own[5], own[6] = tie(own[5], best), tie(own[6], best)
    other[5], other[6] = swap(own[5]), swap(own[6])
    best = score(best, range(12), (new_pass(10, 2, 12, size), late_pass(6, 2, 8, 10, size)))
    best = score(best, range(10, 14), (late_pass(10, 2, 12, 14, size),))
    own[7] = tie(own[7], best)
    other[7] = swap(own[7])
    best = score(best, range(15), (new_pass(14, 1, 15, size),))
    outbound = finish(order, own[7], other[7], flat, best)
    returned = lax.all_to_all(outbound, axes, split_axis=0, concat_axis=0, tiled=True)
    sources = []
    for owner in range(8):
        host, y = host_of(owner)
        for half in range(2):
            sources.append(tuple((host * 4 + y * 2 + core, half) for core in range(2)))
    return settle(index, returned, tuple(sources), documents)


def gathered(embeddings, send_index, place_index, slot_cluster):
    documents, width = embeddings.shape
    owners = lax.axis_size("shard")
    reps = lax.axis_size("rep")
    share = send_index.shape[0] // owners
    outgoing = normalize(embeddings.at[send_index].get(mode="promise_in_bounds"))
    arrived = lax.all_to_all(
        outgoing.reshape(owners, share, width), "shard", split_axis=0, concat_axis=0, tiled=True
    )
    parts = 16
    size = documents // parts
    news = parts // reps
    turn = lax.axis_index("rep") * news
    arrived = jnp.roll(arrived.reshape(parts, size, width), -turn, axis=0)
    clusters = arrival_clusters(place_index, slot_cluster).reshape(parts, size)
    clusters = jnp.roll(clusters, -turn, axis=0)
    best = jnp.full((1, documents), -1.0, jnp.float32)
    tiles = tuple(range(documents // BLK))
    passes = ((0, news, 0, 1, True, tiles),)
    chunks = [arrived[i] for i in range(parts)]
    best = gram_best(chunks, tuple(range(parts)), size, clusters.reshape(1, -1), best, passes)
    best = lax.all_gather(best[0, : news * size], "rep", axis=0, tiled=True)
    returned = lax.all_to_all(
        best.reshape(owners, share), "shard", split_axis=0, concat_axis=0, tiled=True
    )
    sources = tuple(((0, g),) for g in range(parts))
    return settle(send_index.reshape(parts, size), returned.reshape(1, parts, size), sources, documents)


def solution(mesh):
    planned = mesh.shape["shard"] == 8 and mesh.shape["rep"] == 4

    def shards(embeddings, send_index, place_index, slot_cluster, pair_list):
        del pair_list
        run = hosted if planned else gathered
        return run(embeddings, send_index, place_index, slot_cluster)

    return jax.shard_map(
        shards,
        mesh=mesh,
        in_specs=(P("shard", None), P("shard"), P("shard"), P("shard"), P(("shard", "rep"), None)),
        out_specs=P("shard"),
        check_vma=False,
    )
```

```python
import functools

import jax
import jax.numpy as jnp
import numpy as np
from jax import lax
from jax.experimental import pallas as pl
from jax.experimental.pallas import tpu as pltpu
from jax.sharding import PartitionSpec as P

BLK = 256
LANES = 128
NT = (((1,), (1,)), ((), ()))
MIB = 1024 * 1024
LONG = 25_000_000_000

HOSTS = (2, 3, 4, 5)
ROUNDS = ((4, 6, 5, 7, 2, 1, 3), (2, 1, 3, 6, 4, 7, 5))


CHUNKS = (
    (0, 0), (1, 0), (2, 0), (0, 1),
    (1, 1), (2, 1), (3, 0), (4, 0),
    (3, 1), (4, 1), (5, 0), (6, 0),
    (5, 1), (6, 1), (7, 0), (7, 1),
)


def host_of(owner):
    z, x = owner // 2, owner % 2
    return (1 if z < 2 else 2) * 2 + x, z % 2


def plan():
    owner_at = {host_of(owner): owner for owner in range(8)}
    sends = np.zeros((8, 4, 4), np.int32)
    order = np.zeros((8, 4, 16), np.int32)
    for s in range(8):
        for rep in range(4):
            y, core = divmod(rep, 2)
            steps = [(step, k) for step, k in enumerate(ROUNDS[core]) if s ^ k in HOSTS]
            assert [step // 2 for step, _ in steps] == list(range(len(steps)))
            targets = [s ^ k for _, k in steps]
            if s in HOSTS:
                targets.append(s)
            sends[s, rep] = [owner_at[target, y] for target in targets]
            for side in range(2):
                half = core ^ side
                for step, k in enumerate((0,) + ROUNDS[half]):
                    order[s, rep, CHUNKS.index((step, side))] = (s ^ k) * 2 + half
    return sends, order


def round_pairs(step):
    pairs = []
    for rep in range(4):
        for host in HOSTS:
            pairs.append(((host ^ ROUNDS[rep % 2][step]) * 4 + rep, host * 4 + rep))
    return pairs


SIBLINGS = [(host * 4 + rep, host * 4 + (rep ^ 1)) for host in HOSTS for rep in range(4)]


def metadata_pairs():
    pairs = []
    for owner in range(8):
        host, y = host_of(owner)
        for core in range(2):
            pairs.append((owner * 4 + y * 2 + core, host * 4 + y * 2 + core))
    return pairs


def tie(value, *after):
    return lax.optimization_barrier((value, *after))[0]


def normalize(rows):
    wide = rows.astype(jnp.float32)
    return (wide * lax.rsqrt(jnp.sum(wide * wide, axis=1, keepdims=True) + 1e-06)).astype(
        jnp.bfloat16
    )


def names_kernel(place_ref, slots_ref, out_ref):
    block = place_ref[...] // BLK
    found = jnp.zeros_like(block)
    for i in range(slots_ref.shape[0] * LANES // BLK):
        row = i * BLK // LANES
        found = jnp.where(block == i, slots_ref[row : row + 1, 0:1], found)
    out_ref[...] = found


def arrival_names(place_index, slot_cluster):
    places = place_index.reshape(-1, LANES)
    return pl.pallas_call(
        names_kernel, out_shape=jax.ShapeDtypeStruct(places.shape, jnp.int32)
    )(places, slot_cluster.reshape(-1, LANES))


def gather_kernel(count, size, group, sections, *refs):
    table_ref, index_ref, rows_ref = refs[:3]
    raw, wide, picked, sems = refs[-4:]
    outs = refs[-4 - count : -4]
    width = raw.shape[1]
    tiles = width // LANES
    part = raw.shape[0] // sections
    copies = []
    for i in range(sections):
        rows = pl.ds(i * part, part)
        copies.append(pltpu.make_async_copy(rows_ref.at[rows], raw.at[rows], sems.at[i]))
        copies[-1].start()
    step = 160
    for i in range(sections):
        copies[i].wait()

        def widen(j, _, i=i):
            first = i * part + j * step
            rows = raw[pl.ds(pl.multiple_of(first, step), step), :].astype(jnp.float32)
            for t in range(tiles):
                wide[pl.ds(first * tiles + t, step, stride=tiles), :] = rows[:, t * LANES : (t + 1) * LANES]
            return 0

        lax.fori_loop(0, part // step, widen, 0)
    for c in range(count):
        base = table_ref[c]

        def pick(j, _, c=c, base=base):
            for t in range(group):
                source = pl.multiple_of(index_ref[base + j * group + t] * tiles, tiles)
                picked[t * tiles : (t + 1) * tiles, :] = wide[pl.ds(source, tiles), :]
            for first in range(0, group, 16):
                rows = jnp.concatenate(
                    [picked[pl.ds(first * tiles + t, 16, stride=tiles), :] for t in range(tiles)],
                    axis=1,
                )
                scale = lax.rsqrt(jnp.sum(rows * rows, axis=1, keepdims=True) + 1e-06)
                outs[c][pl.ds(pl.multiple_of(j * group + first, 16), 16), :] = (rows * scale).astype(
                    jnp.bfloat16
                )
            return 0

        lax.fori_loop(0, size // group, pick, 0)


def gather_rows(embeddings, index, starts, size, after=()):
    documents, width = embeddings.shape
    count = starts.shape[0]
    sections = 10
    group = 80
    return pl.pallas_call(
        functools.partial(gather_kernel, count, size, group, sections),
        out_shape=[jax.ShapeDtypeStruct((size, width), jnp.bfloat16)] * count,
        in_specs=[
            pl.BlockSpec(memory_space=pltpu.SMEM),
            pl.BlockSpec(memory_space=pltpu.SMEM),
            pl.BlockSpec(memory_space=pl.ANY),
        ]
        + [pl.BlockSpec(memory_space=pl.ANY)] * len(after),
        out_specs=[pl.BlockSpec(memory_space=pltpu.VMEM)] * count,
        scratch_shapes=[
            pltpu.VMEM((documents, width), jnp.bfloat16),
            pltpu.VMEM((documents * width // LANES, LANES), jnp.float32),
            pltpu.VMEM((group * width // LANES, LANES), jnp.float32),
            pltpu.SemaphoreType.DMA((sections,)),
        ],
        compiler_params=pltpu.CompilerParams(vmem_limit_bytes=45 * MIB),
        cost_estimate=pl.CostEstimate(flops=LONG, bytes_accessed=0, transcendentals=0),
    )(starts, index, embeddings, *after)


def best_of_rows(acc, size):
    return jnp.max(jnp.transpose(acc), axis=0, keepdims=True)[:, :size]


def as_column(row_ref, start, size):
    wide = -(-size // LANES) * LANES
    row = row_ref[:, start : start + wide]
    return jnp.transpose(jnp.broadcast_to(row, (LANES, wide)))[:size]


def gram_kernel(passes, loads, size, limit, *refs):
    chunks = refs[: len(loads)]
    cluster_row, before_ref, best_ref, held, acc, sems = refs[-6:]
    first = range(passes[0][0], passes[0][0] + passes[0][1])

    def copy(i):
        rows = held.at[pl.ds(i * size, size)]
        return pltpu.make_async_copy(chunks[loads.index(i)], rows, sems.at[i])

    def arrive(i):
        rows = held.at[pl.ds(0, size)]
        pltpu.make_async_copy(rows, rows, sems.at[i]).wait()

    for i in first:
        copy(i).start()
    for i in loads:
        if i not in first:
            copy(i).start()
    best_ref[...] = before_ref[...]
    for i in first:
        copy(i).wait()
    for n, (chunk, news, groups, group, meets, last) in enumerate(passes):
        height = news * size
        acc[...] = jnp.full_like(acc, -1.0)
        rows = held[chunk * size : chunk * size + height, :]
        left = as_column(cluster_row, chunk * size, height)
        left = jnp.concatenate([left, left], axis=1)

        def tile(start, special, chunk=chunk, height=height, rows=rows, left=left):
            gram = lax.dot_general(
                rows, held[pl.ds(start, BLK), :], NT, preferred_element_type=jnp.float32
            )
            counts = left == cluster_row[:, pl.ds(start, BLK)]
            if special:
                column = start + lax.broadcasted_iota(jnp.int32, (height, BLK), 1)
                row = chunk * size + lax.broadcasted_iota(jnp.int32, (height, BLK), 0)
                counts = counts & (column != row) & (column < limit)
            values = jnp.where(counts, gram, jnp.float32(-1.0))
            top = jnp.max(values, axis=0, keepdims=True)
            best_ref[:, pl.ds(start, BLK)] = jnp.maximum(best_ref[:, pl.ds(start, BLK)], top)
            acc[0:height, :] = jnp.maximum(
                acc[0:height, :], jnp.maximum(values[:, :LANES], values[:, LANES:])
            )

        def visit(u, _, n=n, group=group, meets=meets, tile=tile):
            if n == 0:
                for i in (2 * u, 2 * u + 1):

                    @pl.when(i < first[0])
                    def _(i=i):
                        arrive(i)

            for t in range(group):
                tile(pl.multiple_of((u * group + t) * BLK, BLK), meets)
            return 0

        lax.fori_loop(0, groups, visit, 0)
        if n == 0:
            for i in loads:
                if i not in first and not i < min(2 * groups, first[0]):
                    arrive(i)
        for t in last:
            tile(t * BLK, True)
        span = slice(chunk * size, chunk * size + height)
        best_ref[:, span] = jnp.maximum(best_ref[:, span], best_of_rows(acc[...], height))


def gram_best(chunks, size, cluster_row, before, passes, after=()):
    loads = tuple(range(len(chunks)))
    width = chunks[0].shape[1]
    total = before.shape[1]
    limit = (max(loads) + 1) * size
    held = -(-limit // BLK) * BLK
    tall = max(news for _, news, *_ in passes) * size
    padded = -(-tall // LANES) * LANES
    return pl.pallas_call(
        functools.partial(gram_kernel, passes, loads, size, limit),
        out_shape=jax.ShapeDtypeStruct((1, total), jnp.float32),
        in_specs=[pl.BlockSpec(memory_space=pl.ANY)] * len(loads)
        + [pl.BlockSpec(memory_space=pl.ANY)] * len(after)
        + [pl.BlockSpec(memory_space=pltpu.VMEM)] * 2,
        out_specs=pl.BlockSpec(memory_space=pltpu.VMEM),
        scratch_shapes=[
            pltpu.VMEM((held, width), jnp.bfloat16),
            pltpu.VMEM((padded, LANES), jnp.float32),
            pltpu.SemaphoreType.DMA((max(loads) + 1,)),
        ],
        compiler_params=pltpu.CompilerParams(vmem_limit_bytes=24 * MIB),
        cost_estimate=pl.CostEstimate(flops=0, bytes_accessed=0, transcendentals=0),
    )(*chunks, *after, cluster_row, before)


def new_pass(chunk, news, count, size):
    group = 3
    groups = chunk * size // (group * BLK)
    tiles = -(-count * size // BLK)
    return (chunk, news, groups, group, False, tuple(range(groups * group, tiles)))


def late_pass(chunk, news, low, high, size):
    return (chunk, news, 0, 1, True, tuple(range(low * size // BLK, -(-high * size // BLK))))


def finish_kernel(size, order_ref, own_ref, other_ref, clusters_ref, best_ref, out_ref, acc):
    gram = lax.dot_general(own_ref[...], other_ref[...], NT, preferred_element_type=jnp.float32)
    left = as_column(clusters_ref, 14 * size, size)
    left = jnp.tile(left, (1, -(-size // LANES)))[:, :size]
    last = 15 * size
    values = jnp.where(left == clusters_ref[:, last : last + size], gram, jnp.float32(-1.0))
    acc[...] = jnp.full_like(acc, -1.0)
    acc[0:size, :] = jnp.broadcast_to(jnp.max(values, axis=1, keepdims=True), (size, LANES))
    for i in range(16):
        found = best_ref[:, i * size : (i + 1) * size]
        if i == 14:
            found = jnp.maximum(found, best_of_rows(acc[...], size))
        if i == 15:
            found = jnp.maximum(found, jnp.max(values, axis=0, keepdims=True))
        place = order_ref[i]
        source, half = place // 2, place % 2
        for rep in range(4):
            out_ref[source * 4 + rep, pl.ds(half, 1), :] = found


def finish(order, own, other, clusters, best):
    size = own.shape[0]
    padded = -(-size // LANES) * LANES
    return pl.pallas_call(
        functools.partial(finish_kernel, size),
        out_shape=jax.ShapeDtypeStruct((32, 2, size), jnp.float32),
        in_specs=[pl.BlockSpec(memory_space=pltpu.SMEM)]
        + [pl.BlockSpec(memory_space=pltpu.VMEM)] * 4,
        out_specs=pl.BlockSpec(memory_space=pltpu.VMEM),
        scratch_shapes=[pltpu.VMEM((padded, LANES), jnp.float32)],
        compiler_params=pltpu.CompilerParams(vmem_limit_bytes=16 * MIB),
    )(order, own, other, clusters, best)


def settle_kernel(sources, size, high, index_ref, values_ref, out_ref, left_ref, right_ref):
    wide = left_ref.shape[1] // len(sources)
    left_ref[...] = jnp.zeros_like(left_ref)
    right_ref[...] = jnp.zeros_like(right_ref)
    rows = lax.broadcasted_iota(jnp.int32, (high, size), 0)
    lanes = lax.broadcasted_iota(jnp.int32, (LANES, size), 0)
    for g, places in enumerate(sources):
        index = index_ref[g // 2, g % 2 : g % 2 + 1, :] if index_ref.ndim == 3 else index_ref[g : g + 1, :]
        value = values_ref[places[0][0], places[0][1] : places[0][1] + 1, :]
        for a, b in places[1:]:
            value = jnp.maximum(value, values_ref[a, b : b + 1, :])
        span = slice(g * wide, g * wide + size)
        here = rows == index // LANES
        for piece in range(3):
            head = value.astype(jnp.bfloat16).astype(jnp.float32)
            value = value - head
            left_ref[piece * high : (piece + 1) * high, span] = jnp.where(here, head, 0.0).astype(
                jnp.bfloat16
            )
        right_ref[:, span] = jnp.where(lanes == index % LANES, 1.0, 0.0).astype(jnp.bfloat16)
    total = lax.dot_general(left_ref[...], right_ref[...], NT, preferred_element_type=jnp.float32)
    total = total[2 * high : 3 * high] + total[high : 2 * high] + total[:high]
    out_ref[...] = total[: out_ref.shape[0]]


def settle(index, values, sources, documents):
    size = index.shape[-1]
    high = -(-documents // (16 * LANES)) * 16
    wide = -(-size // LANES) * LANES * len(sources)
    out = pl.pallas_call(
        functools.partial(settle_kernel, sources, size, high),
        out_shape=jax.ShapeDtypeStruct((documents // LANES, LANES), jnp.float32),
        scratch_shapes=[
            pltpu.VMEM((3 * high, wide), jnp.bfloat16),
            pltpu.VMEM((LANES, wide), jnp.bfloat16),
        ],
        compiler_params=pltpu.CompilerParams(vmem_limit_bytes=16 * MIB),
    )(index, values)
    return out.reshape(-1)


def hosted(embeddings, send_index, place_index, slot_cluster):
    documents = embeddings.shape[0]
    share = send_index.shape[0] // 8
    size = share // 2
    s, rep = lax.axis_index("shard"), lax.axis_index("rep")
    axes = ("shard", "rep")
    sends, order = plan()
    halves = np.arange(4)[:, None] % 2 ^ np.array([0, 0, 0, 0, 1])
    starts = sends[:, :, [0, 1, 2, 3, 3]] * share + (halves * size).astype(np.int32)
    starts = jnp.asarray(starts)[s, rep]
    order = jnp.asarray(order)[s, rep]
    named = arrival_names(place_index, slot_cluster)
    (early,) = gather_rows(embeddings, send_index, starts[:1], size, (named,))
    named = lax.ppermute(named, axes, metadata_pairs())
    early = tie(early, named)
    clusters = named.reshape(16, size)[order]
    index = send_index.reshape(8, 2, size)

    def go(step, chunk):
        return lax.ppermute(chunk, axes, round_pairs(step - 1))

    def swap(chunk):
        return lax.ppermute(chunk, axes, SIBLINGS)

    own, other = [None] * 8, [None] * 8
    own[1], own[2] = go(1, early), go(2, early)
    late = gather_rows(embeddings, send_index, starts[1:], size, (early,))
    own[0], other[0] = late[2:]
    own[3], own[4] = go(3, late[0]), go(4, late[0])
    flat = clusters.reshape(1, 16 * size)

    def score(best, count, passes, after=()):
        chunks = [(own, other)[side][r] for r, side in CHUNKS[:count]]
        return gram_best(chunks, size, flat, best, passes, after)

    own[1], own[2] = tie(own[1], late[0]), tie(own[2], late[0])
    other[1], other[2] = swap(own[1]), swap(own[2])
    own[5] = go(5, tie(late[1], own[1]))
    own[6] = go(6, tie(late[1], own[2]))
    best = jnp.full((1, 16 * size), -1.0, jnp.float32)
    best = score(best, 6, (new_pass(0, 3, 6, size),), (order, index))
    own[3], own[4] = tie(own[3], best), tie(own[4], best)
    other[3], other[4] = swap(own[3]), swap(own[4])
    own[7] = go(7, tie(late[2], own[3]))
    best = score(best, 8, (new_pass(6, 2, 8, size),))
    own[5], own[6] = tie(own[5], best), tie(own[6], best)
    other[5], other[6] = swap(own[5]), swap(own[6])
    best = score(best, 12, (new_pass(10, 2, 12, size), late_pass(6, 2, 8, 10, size)))
    own[7] = tie(own[7], best)
    other[7] = swap(own[7])
    best = score(best, 15, (new_pass(14, 1, 15, size), late_pass(10, 2, 12, 14, size)))
    outbound = finish(order, own[7], other[7], flat, best)
    returned = lax.all_to_all(outbound, axes, split_axis=0, concat_axis=0, tiled=True)
    sources = []
    for owner in range(8):
        host, y = host_of(owner)
        for half in range(2):
            sources.append(tuple((host * 4 + y * 2 + core, half) for core in range(2)))
    return settle(index, returned, tuple(sources), documents)


def gathered(embeddings, send_index, place_index, slot_cluster):
    documents, width = embeddings.shape
    owners = lax.axis_size("shard")
    reps = lax.axis_size("rep")
    share = send_index.shape[0] // owners
    outgoing = normalize(embeddings.at[send_index].get(mode="promise_in_bounds"))
    arrived = lax.all_to_all(
        outgoing.reshape(owners, share, width), "shard", split_axis=0, concat_axis=0, tiled=True
    )
    parts = 16
    size = documents // parts
    news = parts // reps
    turn = lax.axis_index("rep") * news
    arrived = jnp.roll(arrived.reshape(parts, size, width), -turn, axis=0)
    clusters = arrival_names(place_index, slot_cluster).reshape(parts, size)
    clusters = jnp.roll(clusters, -turn, axis=0)
    best = jnp.full((1, documents), -1.0, jnp.float32)
    tiles = tuple(range(documents // BLK))
    passes = ((0, news, 0, 1, True, tiles),)
    chunks = [arrived[i] for i in range(parts)]
    best = gram_best(chunks, size, clusters.reshape(1, -1), best, passes)
    best = lax.all_gather(best[0, : news * size], "rep", axis=0, tiled=True)
    returned = lax.all_to_all(
        best.reshape(owners, share), "shard", split_axis=0, concat_axis=0, tiled=True
    )
    sources = tuple(((0, g),) for g in range(parts))
    return settle(send_index.reshape(parts, size), returned.reshape(1, parts, size), sources, documents)


def solution(mesh):
    planned = mesh.shape["shard"] == 8 and mesh.shape["rep"] == 4

    def shards(embeddings, send_index, place_index, slot_cluster, pair_list):
        del pair_list
        run = hosted if planned else gathered
        return run(embeddings, send_index, place_index, slot_cluster)

    return jax.shard_map(
        shards,
        mesh=mesh,
        in_specs=(P("shard", None), P("shard"), P("shard"), P("shard"), P(("shard", "rep"), None)),
        out_specs=P("shard"),
        check_vma=False,
    )
```

```python
import functools

import jax
import jax.numpy as jnp
import numpy as np
from jax import lax
from jax.experimental import pallas as pl
from jax.experimental.pallas import tpu as pltpu
from jax.sharding import PartitionSpec as P

BLK = 256
LANES = 128
NT = (((1,), (1,)), ((), ()))
MIB = 1024 * 1024
LONG = 25_000_000_000

HOSTS = (2, 3, 4, 5)
ROUNDS = ((2, 6, 5, 1, 3, 7, 4), (3, 7, 2, 6, 4, 1, 5))


CHUNKS = (
    (0, 0), (1, 0), (2, 0), (0, 1),
    (1, 1), (2, 1), (3, 0), (4, 0),
    (3, 1), (4, 1), (5, 0), (6, 0),
    (5, 1), (6, 1), (7, 0), (7, 1),
)


def host_of(owner):
    z, x = owner // 2, owner % 2
    return (1 if z < 2 else 2) * 2 + x, z % 2


def chunk_order():
    order = np.zeros((8, 4, 16), np.int32)
    for s in range(8):
        for rep in range(4):
            for i, (step, side) in enumerate(CHUNKS):
                half = rep % 2 ^ side
                order[s, rep, i] = (s ^ ((0,) + ROUNDS[half])[step]) * 2 + half
    return order


def round_pairs(step):
    pairs = []
    for rep in range(4):
        for host in HOSTS:
            pairs.append(((host ^ ROUNDS[rep % 2][step]) * 4 + rep, host * 4 + rep))
    return pairs


SIBLINGS = [(host * 4 + rep, host * 4 + (rep ^ 1)) for host in HOSTS for rep in range(4)]


def metadata_pairs():
    pairs = []
    for owner in range(8):
        host, y = host_of(owner)
        for core in range(2):
            pairs.append((owner * 4 + y * 2 + core, host * 4 + y * 2 + core))
    return pairs


def tie(value, *after):
    return lax.optimization_barrier((value, *after))[0]


def normalize(rows):
    wide = rows.astype(jnp.float32)
    return (wide * lax.rsqrt(jnp.sum(wide * wide, axis=1, keepdims=True) + 1e-06)).astype(
        jnp.bfloat16
    )


def names_kernel(place_ref, slots_ref, out_ref):
    block = place_ref[...] // BLK
    found = jnp.zeros_like(block)
    for i in range(slots_ref.shape[0] * LANES // BLK):
        row = i * BLK // LANES
        found = jnp.where(block == i, slots_ref[row : row + 1, 0:1], found)
    out_ref[...] = found


def arrival_names(place_index, slot_cluster):
    places = place_index.reshape(-1, LANES)
    return pl.pallas_call(
        names_kernel, out_shape=jax.ShapeDtypeStruct(places.shape, jnp.int32)
    )(places, slot_cluster.reshape(-1, LANES))


def chunk_start(slot, size):
    s, rep = lax.axis_index("shard"), lax.axis_index("rep")
    y, core = rep // 2, rep % 2
    inner = (s >= HOSTS[0]) & (s <= HOSTS[-1])
    turn = min(slot, 3)
    steps = [(order[2 * turn], (order + (0,))[2 * turn + 1]) for order in ROUNDS]
    outer_step = jnp.where(core == 0, steps[0][0], steps[1][0])
    inner_step = jnp.where(core == 0, steps[0][1], steps[1][1])
    target = s ^ jnp.where(inner, inner_step, outer_step)
    owner = (2 * (target // 2 - 1) + y) * 2 + target % 2
    half = 1 - core if slot == 4 else core
    return owner * (2 * size) + half * size


def gather_kernel(slots, size, group, sections, *refs):
    index_hbm, rows_ref = refs[:2]
    index_ref, raw, wide, picked, sems = refs[-5:]
    outs = refs[-5 - len(slots) : -5]
    listed = pltpu.make_async_copy(index_hbm, index_ref, sems.at[sections])
    listed.start()
    width = raw.shape[1]
    tiles = width // LANES
    part = raw.shape[0] // sections
    copies = []
    for i in range(sections):
        rows = pl.ds(i * part, part)
        copies.append(pltpu.make_async_copy(rows_ref.at[rows], raw.at[rows], sems.at[i]))
        copies[-1].start()
    step = 160
    for i in range(sections):
        copies[i].wait()

        def widen(j, _, i=i):
            first = i * part + j * step
            rows = raw[pl.ds(pl.multiple_of(first, step), step), :].astype(jnp.float32)
            for t in range(tiles):
                wide[pl.ds(first * tiles + t, step, stride=tiles), :] = rows[:, t * LANES : (t + 1) * LANES]
            return 0

        lax.fori_loop(0, part // step, widen, 0)
    listed.wait()
    for c, slot in enumerate(slots):
        base = chunk_start(slot, size)

        def pick(j, _, c=c, base=base):
            for t in range(group):
                source = pl.multiple_of(index_ref[base + j * group + t] * tiles, tiles)
                picked[t * tiles : (t + 1) * tiles, :] = wide[pl.ds(source, tiles), :]
            for first in range(0, group, 16):
                rows = jnp.concatenate(
                    [picked[pl.ds(first * tiles + t, 16, stride=tiles), :] for t in range(tiles)],
                    axis=1,
                )
                scale = lax.rsqrt(jnp.sum(rows * rows, axis=1, keepdims=True) + 1e-06)
                outs[c][pl.ds(pl.multiple_of(j * group + first, 16), 16), :] = (rows * scale).astype(
                    jnp.bfloat16
                )
            return 0

        lax.fori_loop(0, size // group, pick, 0)


def gather_rows(embeddings, index, slots, size, after=()):
    documents, width = embeddings.shape
    count = len(slots)
    sections = 10
    group = 80
    return pl.pallas_call(
        functools.partial(gather_kernel, slots, size, group, sections),
        out_shape=[jax.ShapeDtypeStruct((size, width), jnp.bfloat16)] * count,
        in_specs=[pl.BlockSpec(memory_space=pltpu.HBM)] * 2
        + [pl.BlockSpec(memory_space=pl.ANY)] * len(after),
        out_specs=[pl.BlockSpec(memory_space=pltpu.VMEM)] * count,
        scratch_shapes=[
            pltpu.SMEM(index.shape, jnp.int32),
            pltpu.VMEM((documents, width), jnp.bfloat16),
            pltpu.VMEM((documents * width // LANES, LANES), jnp.float32),
            pltpu.VMEM((group * width // LANES, LANES), jnp.float32),
            pltpu.SemaphoreType.DMA((sections + 1,)),
        ],
        compiler_params=pltpu.CompilerParams(vmem_limit_bytes=45 * MIB),
        cost_estimate=pl.CostEstimate(flops=LONG, bytes_accessed=0, transcendentals=0),
    )(index, embeddings, *after)


def best_of_rows(acc, size):
    return jnp.max(jnp.transpose(acc), axis=0, keepdims=True)[:, :size]


def as_column(row_ref, start, size):
    wide = -(-size // LANES) * LANES
    row = row_ref[:, start : start + wide]
    return jnp.transpose(jnp.broadcast_to(row, (LANES, wide)))[:size]


def gram_kernel(passes, loads, size, limit, *refs):
    chunks = refs[: len(loads)]
    cluster_row, before_ref, best_ref, held, acc, sems = refs[-6:]
    first = range(passes[0][0], passes[0][0] + passes[0][1])

    def copy(i):
        rows = held.at[pl.ds(i * size, size)]
        return pltpu.make_async_copy(chunks[loads.index(i)], rows, sems.at[i])

    def arrive(i):
        rows = held.at[pl.ds(0, size)]
        pltpu.make_async_copy(rows, rows, sems.at[i]).wait()

    for i in first:
        copy(i).start()
    for i in loads:
        if i not in first:
            copy(i).start()
    best_ref[...] = before_ref[...]
    for i in first:
        copy(i).wait()
    for n, (chunk, news, groups, group, meets, last) in enumerate(passes):
        height = news * size
        acc[...] = jnp.full_like(acc, -1.0)
        rows = held[chunk * size : chunk * size + height, :]
        left = as_column(cluster_row, chunk * size, height)
        left = jnp.concatenate([left, left], axis=1)

        def tile(start, special, chunk=chunk, height=height, rows=rows, left=left):
            gram = lax.dot_general(
                rows, held[pl.ds(start, BLK), :], NT, preferred_element_type=jnp.float32
            )
            counts = left == cluster_row[:, pl.ds(start, BLK)]
            if special:
                column = start + lax.broadcasted_iota(jnp.int32, (height, BLK), 1)
                row = chunk * size + lax.broadcasted_iota(jnp.int32, (height, BLK), 0)
                counts = counts & (column != row) & (column < limit)
            values = jnp.where(counts, gram, jnp.float32(-1.0))
            top = jnp.max(values, axis=0, keepdims=True)
            best_ref[:, pl.ds(start, BLK)] = jnp.maximum(best_ref[:, pl.ds(start, BLK)], top)
            acc[0:height, :] = jnp.maximum(
                acc[0:height, :], jnp.maximum(values[:, :LANES], values[:, LANES:])
            )

        def visit(u, _, n=n, group=group, meets=meets, tile=tile):
            if n == 0:
                for i in (2 * u, 2 * u + 1):

                    @pl.when(i < first[0])
                    def _(i=i):
                        arrive(i)

            for t in range(group):
                tile(pl.multiple_of((u * group + t) * BLK, BLK), meets)
            return 0

        lax.fori_loop(0, groups, visit, 0)
        if n == 0:
            for i in loads:
                if i not in first and not i < min(2 * groups, first[0]):
                    arrive(i)
        for t in last:
            tile(t * BLK, True)
        span = slice(chunk * size, chunk * size + height)
        best_ref[:, span] = jnp.maximum(best_ref[:, span], best_of_rows(acc[...], height))


def gram_best(chunks, size, cluster_row, before, passes, after=()):
    loads = tuple(range(len(chunks)))
    width = chunks[0].shape[1]
    total = before.shape[1]
    limit = (max(loads) + 1) * size
    held = -(-limit // BLK) * BLK
    tall = max(news for _, news, *_ in passes) * size
    padded = -(-tall // LANES) * LANES
    return pl.pallas_call(
        functools.partial(gram_kernel, passes, loads, size, limit),
        out_shape=jax.ShapeDtypeStruct((1, total), jnp.float32),
        in_specs=[pl.BlockSpec(memory_space=pl.ANY)] * len(loads)
        + [pl.BlockSpec(memory_space=pl.ANY)] * len(after)
        + [pl.BlockSpec(memory_space=pltpu.VMEM)] * 2,
        out_specs=pl.BlockSpec(memory_space=pltpu.VMEM),
        scratch_shapes=[
            pltpu.VMEM((held, width), jnp.bfloat16),
            pltpu.VMEM((padded, LANES), jnp.float32),
            pltpu.SemaphoreType.DMA((max(loads) + 1,)),
        ],
        compiler_params=pltpu.CompilerParams(vmem_limit_bytes=24 * MIB),
        cost_estimate=pl.CostEstimate(flops=0, bytes_accessed=0, transcendentals=0),
    )(*chunks, *after, cluster_row, before)


def new_pass(chunk, news, count, size):
    group = 3
    groups = chunk * size // (group * BLK)
    tiles = -(-count * size // BLK)
    return (chunk, news, groups, group, False, tuple(range(groups * group, tiles)))


def late_pass(chunk, news, low, high, size):
    return (chunk, news, 0, 1, True, tuple(range(low * size // BLK, -(-high * size // BLK))))


def finish_kernel(size, order_ref, own_ref, other_ref, clusters_ref, best_ref, out_ref, acc):
    gram = lax.dot_general(own_ref[...], other_ref[...], NT, preferred_element_type=jnp.float32)
    left = as_column(clusters_ref, 14 * size, size)
    left = jnp.tile(left, (1, -(-size // LANES)))[:, :size]
    last = 15 * size
    values = jnp.where(left == clusters_ref[:, last : last + size], gram, jnp.float32(-1.0))
    acc[...] = jnp.full_like(acc, -1.0)
    acc[0:size, :] = jnp.broadcast_to(jnp.max(values, axis=1, keepdims=True), (size, LANES))
    for i in range(16):
        found = best_ref[:, i * size : (i + 1) * size]
        if i == 14:
            found = jnp.maximum(found, best_of_rows(acc[...], size))
        if i == 15:
            found = jnp.maximum(found, jnp.max(values, axis=0, keepdims=True))
        place = order_ref[i]
        source, half = place // 2, place % 2
        for rep in range(4):
            out_ref[source * 4 + rep, pl.ds(half, 1), :] = found


def finish(order, own, other, clusters, best):
    size = own.shape[0]
    padded = -(-size // LANES) * LANES
    return pl.pallas_call(
        functools.partial(finish_kernel, size),
        out_shape=jax.ShapeDtypeStruct((32, 2, size), jnp.float32),
        in_specs=[pl.BlockSpec(memory_space=pltpu.SMEM)]
        + [pl.BlockSpec(memory_space=pltpu.VMEM)] * 4,
        out_specs=pl.BlockSpec(memory_space=pltpu.VMEM),
        scratch_shapes=[pltpu.VMEM((padded, LANES), jnp.float32)],
        compiler_params=pltpu.CompilerParams(vmem_limit_bytes=16 * MIB),
    )(order, own, other, clusters, best)


def settle_kernel(sources, size, high, index_ref, values_ref, out_ref, left_ref, right_ref):
    wide = left_ref.shape[1] // len(sources)
    left_ref[...] = jnp.zeros_like(left_ref)
    right_ref[...] = jnp.zeros_like(right_ref)
    rows = lax.broadcasted_iota(jnp.int32, (high, size), 0)
    lanes = lax.broadcasted_iota(jnp.int32, (LANES, size), 0)
    for g, places in enumerate(sources):
        index = index_ref[g // 2, g % 2 : g % 2 + 1, :] if index_ref.ndim == 3 else index_ref[g : g + 1, :]
        value = values_ref[places[0][0], places[0][1] : places[0][1] + 1, :]
        for a, b in places[1:]:
            value = jnp.maximum(value, values_ref[a, b : b + 1, :])
        span = slice(g * wide, g * wide + size)
        here = rows == index // LANES
        for piece in range(3):
            head = value.astype(jnp.bfloat16).astype(jnp.float32)
            value = value - head
            left_ref[piece * high : (piece + 1) * high, span] = jnp.where(here, head, 0.0).astype(
                jnp.bfloat16
            )
        right_ref[:, span] = jnp.where(lanes == index % LANES, 1.0, 0.0).astype(jnp.bfloat16)
    total = lax.dot_general(left_ref[...], right_ref[...], NT, preferred_element_type=jnp.float32)
    total = total[2 * high : 3 * high] + total[high : 2 * high] + total[:high]
    out_ref[...] = total[: out_ref.shape[0]]


def settle(index, values, sources, documents):
    size = index.shape[-1]
    high = -(-documents // (16 * LANES)) * 16
    wide = -(-size // LANES) * LANES * len(sources)
    out = pl.pallas_call(
        functools.partial(settle_kernel, sources, size, high),
        out_shape=jax.ShapeDtypeStruct((documents // LANES, LANES), jnp.float32),
        scratch_shapes=[
            pltpu.VMEM((3 * high, wide), jnp.bfloat16),
            pltpu.VMEM((LANES, wide), jnp.bfloat16),
        ],
        compiler_params=pltpu.CompilerParams(vmem_limit_bytes=16 * MIB),
    )(index, values)
    return out.reshape(-1)


def hosted(embeddings, send_index, place_index, slot_cluster):
    documents = embeddings.shape[0]
    size = send_index.shape[0] // 16
    s, rep = lax.axis_index("shard"), lax.axis_index("rep")
    axes = ("shard", "rep")
    order = jnp.asarray(chunk_order())[s, rep]
    named = arrival_names(place_index, slot_cluster)
    (early,) = gather_rows(embeddings, send_index, (0,), size, (named,))
    named = lax.ppermute(named, axes, metadata_pairs())
    early = tie(early, named)
    clusters = named.reshape(16, size)[order]
    index = send_index.reshape(8, 2, size)

    def go(step, chunk):
        return lax.ppermute(chunk, axes, round_pairs(step - 1))

    def swap(chunk):
        return lax.ppermute(chunk, axes, SIBLINGS)

    own, other = [None] * 8, [None] * 8
    own[1], own[2] = go(1, early), go(2, early)
    late = gather_rows(embeddings, send_index, (1, 2, 3, 4), size, (early,))
    own[0], other[0] = late[2:]
    own[3], own[4] = go(3, late[0]), go(4, late[0])
    flat = clusters.reshape(1, 16 * size)

    def score(best, count, passes, after=()):
        chunks = [(own, other)[side][r] for r, side in CHUNKS[:count]]
        return gram_best(chunks, size, flat, best, passes, after)

    own[1], own[2] = tie(own[1], late[0]), tie(own[2], late[0])
    own[5] = go(5, tie(late[1], own[1]))
    own[6] = go(6, tie(late[1], own[2]))
    best = jnp.full((1, 16 * size), -1.0, jnp.float32)
    best = score(best, 4, (new_pass(0, 3, 4, size),), (order, index))
    other[1], other[2] = swap(tie(own[1], best)), swap(tie(own[2], best))
    own[3], own[4] = tie(own[3], best), tie(own[4], best)
    other[3], other[4] = swap(own[3]), swap(own[4])
    own[7] = go(7, tie(late[2], own[3]))
    best = score(best, 8, (new_pass(6, 2, 8, size), late_pass(1, 2, 4, 6, size)))
    own[5], own[6] = tie(own[5], best), tie(own[6], best)
    other[5], other[6] = swap(own[5]), swap(own[6])
    best = score(best, 12, (new_pass(10, 2, 12, size), late_pass(6, 2, 8, 10, size)))
    own[7] = tie(own[7], best)
    other[7] = swap(own[7])
    best = score(best, 15, (new_pass(14, 1, 15, size), late_pass(10, 2, 12, 14, size)))
    outbound = finish(order, own[7], other[7], flat, best)
    returned = lax.all_to_all(outbound, axes, split_axis=0, concat_axis=0, tiled=True)
    sources = []
    for owner in range(8):
        host, y = host_of(owner)
        for half in range(2):
            sources.append(tuple((host * 4 + y * 2 + core, half) for core in range(2)))
    return settle(index, returned, tuple(sources), documents)


def gathered(embeddings, send_index, place_index, slot_cluster):
    documents, width = embeddings.shape
    owners = lax.axis_size("shard")
    reps = lax.axis_size("rep")
    share = send_index.shape[0] // owners
    outgoing = normalize(embeddings.at[send_index].get(mode="promise_in_bounds"))
    arrived = lax.all_to_all(
        outgoing.reshape(owners, share, width), "shard", split_axis=0, concat_axis=0, tiled=True
    )
    parts = 16
    size = documents // parts
    news = parts // reps
    turn = lax.axis_index("rep") * news
    arrived = jnp.roll(arrived.reshape(parts, size, width), -turn, axis=0)
    clusters = arrival_names(place_index, slot_cluster).reshape(parts, size)
    clusters = jnp.roll(clusters, -turn, axis=0)
    best = jnp.full((1, documents), -1.0, jnp.float32)
    tiles = tuple(range(documents // BLK))
    passes = ((0, news, 0, 1, True, tiles),)
    chunks = [arrived[i] for i in range(parts)]
    best = gram_best(chunks, size, clusters.reshape(1, -1), best, passes)
    best = lax.all_gather(best[0, : news * size], "rep", axis=0, tiled=True)
    returned = lax.all_to_all(
        best.reshape(owners, share), "shard", split_axis=0, concat_axis=0, tiled=True
    )
    sources = tuple(((0, g),) for g in range(parts))
    return settle(send_index.reshape(parts, size), returned.reshape(1, parts, size), sources, documents)


def solution(mesh):
    planned = mesh.shape["shard"] == 8 and mesh.shape["rep"] == 4

    def shards(embeddings, send_index, place_index, slot_cluster, pair_list):
        del pair_list
        run = hosted if planned else gathered
        return run(embeddings, send_index, place_index, slot_cluster)

    return jax.shard_map(
        shards,
        mesh=mesh,
        in_specs=(P("shard", None), P("shard"), P("shard"), P("shard"), P(("shard", "rep"), None)),
        out_specs=P("shard"),
        check_vma=False,
    )
```

```python
import functools

import jax
import jax.numpy as jnp
import numpy as np
from jax import lax
from jax.experimental import pallas as pl
from jax.experimental.pallas import tpu as pltpu
from jax.sharding import PartitionSpec as P

BLK = 256
LANES = 128
NT = (((1,), (1,)), ((), ()))
MIB = 1024 * 1024
LONG = 25_000_000_000

HOSTS = (2, 3, 4, 5)
ROUNDS = ((2, 6, 5, 1, 3, 7, 4), (3, 7, 2, 6, 4, 1, 5))


CHUNKS = (
    (0, 0), (1, 0), (2, 0), (0, 1),
    (1, 1), (2, 1), (3, 0), (4, 0),
    (3, 1), (4, 1), (5, 0), (6, 0),
    (5, 1), (6, 1), (7, 0), (7, 1),
)


def host_of(owner):
    z, x = owner // 2, owner % 2
    return (1 if z < 2 else 2) * 2 + x, z % 2


def chunk_order():
    order = np.zeros((8, 4, 16), np.int32)
    for s in range(8):
        for rep in range(4):
            for i, (step, side) in enumerate(CHUNKS):
                half = rep % 2 ^ side
                order[s, rep, i] = (s ^ ((0,) + ROUNDS[half])[step]) * 2 + half
    return order


def round_pairs(step):
    pairs = []
    for rep in range(4):
        for host in HOSTS:
            pairs.append(((host ^ ROUNDS[rep % 2][step]) * 4 + rep, host * 4 + rep))
    return pairs


SIBLINGS = [(host * 4 + rep, host * 4 + (rep ^ 1)) for host in HOSTS for rep in range(4)]


def metadata_pairs():
    pairs = []
    for owner in range(8):
        host, y = host_of(owner)
        for core in range(2):
            pairs.append((owner * 4 + y * 2 + core, host * 4 + y * 2 + core))
    return pairs


def tie(value, *after):
    return lax.optimization_barrier((value, *after))[0]


def normalize(rows):
    wide = rows.astype(jnp.float32)
    return (wide * lax.rsqrt(jnp.sum(wide * wide, axis=1, keepdims=True) + 1e-06)).astype(
        jnp.bfloat16
    )


def names_kernel(place_ref, slots_ref, out_ref):
    block = place_ref[...] // BLK
    found = jnp.zeros_like(block)
    for i in range(slots_ref.shape[0] * LANES // BLK):
        row = i * BLK // LANES
        found = jnp.where(block == i, slots_ref[row : row + 1, 0:1], found)
    out_ref[...] = found


def arrival_names(place_index, slot_cluster):
    places = place_index.reshape(-1, LANES)
    return pl.pallas_call(
        names_kernel, out_shape=jax.ShapeDtypeStruct(places.shape, jnp.int32)
    )(places, slot_cluster.reshape(-1, LANES))


def chunk_start(slot, size):
    s, rep = lax.axis_index("shard"), lax.axis_index("rep")
    y, core = rep // 2, rep % 2
    inner = (s >= HOSTS[0]) & (s <= HOSTS[-1])
    turn = min(slot, 3)
    steps = [(order[2 * turn], (order + (0,))[2 * turn + 1]) for order in ROUNDS]
    outer_step = jnp.where(core == 0, steps[0][0], steps[1][0])
    inner_step = jnp.where(core == 0, steps[0][1], steps[1][1])
    target = s ^ jnp.where(inner, inner_step, outer_step)
    owner = (2 * (target // 2 - 1) + y) * 2 + target % 2
    half = 1 - core if slot == 4 else core
    return owner * (2 * size) + half * size


def gather_kernel(slots, size, group, sections, *refs):
    index_hbm, rows_ref = refs[:2]
    index_ref, raw, wide, picked, sems = refs[-5:]
    outs = refs[-5 - len(slots) : -5]
    listed = pltpu.make_async_copy(index_hbm, index_ref, sems.at[sections])
    listed.start()
    width = raw.shape[1]
    tiles = width // LANES
    part = raw.shape[0] // sections
    copies = []
    for i in range(sections):
        rows = pl.ds(i * part, part)
        copies.append(pltpu.make_async_copy(rows_ref.at[rows], raw.at[rows], sems.at[i]))
        copies[-1].start()
    step = 160
    for i in range(sections):
        copies[i].wait()

        def widen(j, _, i=i):
            first = i * part + j * step
            rows = raw[pl.ds(pl.multiple_of(first, step), step), :].astype(jnp.float32)
            for t in range(tiles):
                wide[pl.ds(first * tiles + t, step, stride=tiles), :] = rows[:, t * LANES : (t + 1) * LANES]
            return 0

        lax.fori_loop(0, part // step, widen, 0)
    listed.wait()
    for c, slot in enumerate(slots):
        base = chunk_start(slot, size)

        def pick(j, _, c=c, base=base):
            for t in range(group):
                source = pl.multiple_of(index_ref[base + j * group + t] * tiles, tiles)
                picked[t * tiles : (t + 1) * tiles, :] = wide[pl.ds(source, tiles), :]
            for first in range(0, group, 16):
                rows = jnp.concatenate(
                    [picked[pl.ds(first * tiles + t, 16, stride=tiles), :] for t in range(tiles)],
                    axis=1,
                )
                scale = lax.rsqrt(jnp.sum(rows * rows, axis=1, keepdims=True) + 1e-06)
                outs[c][pl.ds(pl.multiple_of(j * group + first, 16), 16), :] = (rows * scale).astype(
                    jnp.bfloat16
                )
            return 0

        lax.fori_loop(0, size // group, pick, 0)


def gather_rows(embeddings, index, slots, size):
    documents, width = embeddings.shape
    count = len(slots)
    sections = 10
    group = 80
    return pl.pallas_call(
        functools.partial(gather_kernel, slots, size, group, sections),
        out_shape=[jax.ShapeDtypeStruct((size, width), jnp.bfloat16)] * count,
        in_specs=[pl.BlockSpec(memory_space=pltpu.HBM)] * 2,
        out_specs=[pl.BlockSpec(memory_space=pltpu.VMEM)] * count,
        scratch_shapes=[
            pltpu.SMEM(index.shape, jnp.int32),
            pltpu.VMEM((documents, width), jnp.bfloat16),
            pltpu.VMEM((documents * width // LANES, LANES), jnp.float32),
            pltpu.VMEM((group * width // LANES, LANES), jnp.float32),
            pltpu.SemaphoreType.DMA((sections + 1,)),
        ],
        compiler_params=pltpu.CompilerParams(vmem_limit_bytes=45 * MIB),
        cost_estimate=pl.CostEstimate(flops=LONG, bytes_accessed=0, transcendentals=0),
    )(index, embeddings)


def best_of_rows(acc, size):
    return jnp.max(jnp.transpose(acc), axis=0, keepdims=True)[:, :size]


def as_column(row_ref, start, size):
    wide = -(-size // LANES) * LANES
    row = row_ref[:, start : start + wide]
    return jnp.transpose(jnp.broadcast_to(row, (LANES, wide)))[:size]


def gram_kernel(passes, loads, carry, size, limit, *refs):
    cluster_row, before_ref, best_ref, pair_ref, held, acc, sems = refs[-7:]
    count = len(loads)
    first = range(passes[0][0], passes[0][0] + passes[0][1])

    def source(i):
        array, place = loads[i]
        return refs[array].at[pl.ds(place * size, size)]

    def copy(i):
        return pltpu.make_async_copy(source(i), held.at[pl.ds(i * size, size)], sems.at[i])

    handed = [
        pltpu.make_async_copy(source(i), pair_ref.at[pl.ds(n * size, size)], sems.at[count + n])
        for n, i in enumerate(carry)
    ]

    def arrive(i):
        rows = held.at[pl.ds(0, size)]
        pltpu.make_async_copy(rows, rows, sems.at[i]).wait()

    for i in first:
        copy(i).start()
    for i in range(count):
        if i not in first:
            copy(i).start()
    for item in handed:
        item.start()
    best_ref[...] = before_ref[...]
    for i in first:
        copy(i).wait()
    for n, (chunk, news, groups, group, meets, last) in enumerate(passes):
        height = news * size
        acc[...] = jnp.full_like(acc, -1.0)
        rows = held[chunk * size : chunk * size + height, :]
        left = as_column(cluster_row, chunk * size, height)
        left = jnp.concatenate([left, left], axis=1)

        def tile(start, special, chunk=chunk, height=height, rows=rows, left=left):
            gram = lax.dot_general(
                rows, held[pl.ds(start, BLK), :], NT, preferred_element_type=jnp.float32
            )
            counts = left == cluster_row[:, pl.ds(start, BLK)]
            if special:
                column = start + lax.broadcasted_iota(jnp.int32, (height, BLK), 1)
                row = chunk * size + lax.broadcasted_iota(jnp.int32, (height, BLK), 0)
                counts = counts & (column != row) & (column < limit)
            values = jnp.where(counts, gram, jnp.float32(-1.0))
            top = jnp.max(values, axis=0, keepdims=True)
            best_ref[:, pl.ds(start, BLK)] = jnp.maximum(best_ref[:, pl.ds(start, BLK)], top)
            acc[0:height, :] = jnp.maximum(
                acc[0:height, :], jnp.maximum(values[:, :LANES], values[:, LANES:])
            )

        def visit(u, _, n=n, group=group, meets=meets, tile=tile):
            if n == 0:
                for i in (2 * u, 2 * u + 1):

                    @pl.when(i < first[0])
                    def _(i=i):
                        arrive(i)

            for t in range(group):
                tile(pl.multiple_of((u * group + t) * BLK, BLK), meets)
            return 0

        lax.fori_loop(0, groups, visit, 0)
        if n == 0:
            for i in range(count):
                if i not in first and not i < min(2 * groups, first[0]):
                    arrive(i)
        for t in last:
            tile(t * BLK, True)
        span = slice(chunk * size, chunk * size + height)
        best_ref[:, span] = jnp.maximum(best_ref[:, span], best_of_rows(acc[...], height))
    for item in handed:
        item.wait()


def gram_best(arrays, loads, size, cluster_row, before, passes, carry=(), after=()):
    width = arrays[0].shape[1]
    limit = len(loads) * size
    held = -(-limit // BLK) * BLK
    tall = max(news for _, news, *_ in passes) * size
    padded = -(-tall // LANES) * LANES
    return pl.pallas_call(
        functools.partial(gram_kernel, passes, loads, carry, size, limit),
        out_shape=[
            jax.ShapeDtypeStruct(before.shape, jnp.float32),
            jax.ShapeDtypeStruct((max(1, len(carry)) * size, width), jnp.bfloat16),
        ],
        in_specs=[pl.BlockSpec(memory_space=pl.ANY)] * (len(arrays) + len(after))
        + [pl.BlockSpec(memory_space=pltpu.VMEM)] * 2,
        out_specs=[pl.BlockSpec(memory_space=pltpu.VMEM), pl.BlockSpec(memory_space=pl.ANY)],
        scratch_shapes=[
            pltpu.VMEM((held, width), jnp.bfloat16),
            pltpu.VMEM((padded, LANES), jnp.float32),
            pltpu.SemaphoreType.DMA((len(loads) + len(carry),)),
        ],
        compiler_params=pltpu.CompilerParams(vmem_limit_bytes=24 * MIB),
        cost_estimate=pl.CostEstimate(flops=0, bytes_accessed=0, transcendentals=0),
    )(*arrays, *after, cluster_row, before)


def join_kernel(first_ref, second_ref, out_ref, sems):
    size = first_ref.shape[0]
    copies = [
        pltpu.make_async_copy(ref, out_ref.at[pl.ds(i * size, size)], sems.at[i])
        for i, ref in enumerate((first_ref, second_ref))
    ]
    for copy in copies:
        copy.start()
    for copy in copies:
        copy.wait()


def join(first, second, work):
    size, width = first.shape
    return pl.pallas_call(
        join_kernel,
        out_shape=jax.ShapeDtypeStruct((2 * size, width), first.dtype),
        in_specs=[pl.BlockSpec(memory_space=pl.ANY)] * 2,
        out_specs=pl.BlockSpec(memory_space=pl.ANY),
        scratch_shapes=[pltpu.SemaphoreType.DMA((2,))],
        compiler_params=pltpu.CompilerParams(vmem_limit_bytes=MIB),
        cost_estimate=pl.CostEstimate(flops=work, bytes_accessed=0, transcendentals=0),
    )(first, second)


def new_pass(chunk, news, count, size):
    group = 3
    groups = chunk * size // (group * BLK)
    tiles = -(-count * size // BLK)
    return (chunk, news, groups, group, False, tuple(range(groups * group, tiles)))


def late_pass(chunk, news, low, high, size):
    return (chunk, news, 0, 1, True, tuple(range(low * size // BLK, -(-high * size // BLK))))


def finish_kernel(size, order_ref, own_ref, other_ref, clusters_ref, best_ref, out_ref, acc):
    gram = lax.dot_general(own_ref[...], other_ref[...], NT, preferred_element_type=jnp.float32)
    left = as_column(clusters_ref, 14 * size, size)
    left = jnp.tile(left, (1, -(-size // LANES)))[:, :size]
    last = 15 * size
    values = jnp.where(left == clusters_ref[:, last : last + size], gram, jnp.float32(-1.0))
    acc[...] = jnp.full_like(acc, -1.0)
    acc[0:size, :] = jnp.broadcast_to(jnp.max(values, axis=1, keepdims=True), (size, LANES))
    for i in range(16):
        found = best_ref[:, i * size : (i + 1) * size]
        if i == 14:
            found = jnp.maximum(found, best_of_rows(acc[...], size))
        if i == 15:
            found = jnp.maximum(found, jnp.max(values, axis=0, keepdims=True))
        place = order_ref[i]
        source, half = place // 2, place % 2
        for rep in range(4):
            out_ref[source * 4 + rep, pl.ds(half, 1), :] = found


def finish(order, own, other, clusters, best):
    size = own.shape[0]
    padded = -(-size // LANES) * LANES
    return pl.pallas_call(
        functools.partial(finish_kernel, size),
        out_shape=jax.ShapeDtypeStruct((32, 2, size), jnp.float32),
        in_specs=[pl.BlockSpec(memory_space=pltpu.SMEM)]
        + [pl.BlockSpec(memory_space=pltpu.VMEM)] * 4,
        out_specs=pl.BlockSpec(memory_space=pltpu.VMEM),
        scratch_shapes=[pltpu.VMEM((padded, LANES), jnp.float32)],
        compiler_params=pltpu.CompilerParams(vmem_limit_bytes=16 * MIB),
    )(order, own, other, clusters, best)


def settle_kernel(sources, size, high, index_ref, values_ref, out_ref, left_ref, right_ref):
    wide = left_ref.shape[1] // len(sources)
    left_ref[...] = jnp.zeros_like(left_ref)
    right_ref[...] = jnp.zeros_like(right_ref)
    rows = lax.broadcasted_iota(jnp.int32, (high, size), 0)
    lanes = lax.broadcasted_iota(jnp.int32, (LANES, size), 0)
    for g, places in enumerate(sources):
        index = index_ref[g // 2, g % 2 : g % 2 + 1, :] if index_ref.ndim == 3 else index_ref[g : g + 1, :]
        value = values_ref[places[0][0], places[0][1] : places[0][1] + 1, :]
        for a, b in places[1:]:
            value = jnp.maximum(value, values_ref[a, b : b + 1, :])
        span = slice(g * wide, g * wide + size)
        here = rows == index // LANES
        for piece in range(3):
            head = value.astype(jnp.bfloat16).astype(jnp.float32)
            value = value - head
            left_ref[piece * high : (piece + 1) * high, span] = jnp.where(here, head, 0.0).astype(
                jnp.bfloat16
            )
        right_ref[:, span] = jnp.where(lanes == index % LANES, 1.0, 0.0).astype(jnp.bfloat16)
    total = lax.dot_general(left_ref[...], right_ref[...], NT, preferred_element_type=jnp.float32)
    total = total[2 * high : 3 * high] + total[high : 2 * high] + total[:high]
    out_ref[...] = total[: out_ref.shape[0]]


def settle(index, values, sources, documents):
    size = index.shape[-1]
    high = -(-documents // (16 * LANES)) * 16
    wide = -(-size // LANES) * LANES * len(sources)
    out = pl.pallas_call(
        functools.partial(settle_kernel, sources, size, high),
        out_shape=jax.ShapeDtypeStruct((documents // LANES, LANES), jnp.float32),
        scratch_shapes=[
            pltpu.VMEM((3 * high, wide), jnp.bfloat16),
            pltpu.VMEM((LANES, wide), jnp.bfloat16),
        ],
        compiler_params=pltpu.CompilerParams(vmem_limit_bytes=16 * MIB),
    )(index, values)
    return out.reshape(-1)


def hosted(embeddings, send_index, place_index, slot_cluster):
    documents = embeddings.shape[0]
    size = send_index.shape[0] // 16
    axes = ("shard", "rep")
    named = arrival_names(place_index, slot_cluster)
    embeddings = tie(embeddings, named)
    (early,) = gather_rows(embeddings, send_index, (0,), size)
    named = lax.ppermute(named, axes, metadata_pairs())
    early = tie(early, named)
    index = send_index.reshape(8, 2, size)

    def go(step, chunk):
        return lax.ppermute(chunk, axes, round_pairs(step - 1))

    def swap(chunk):
        return lax.ppermute(chunk, axes, SIBLINGS)

    own, other = [None] * 8, [None] * 8
    own[1], own[2] = go(1, early), go(2, early)
    late = gather_rows(tie(embeddings, early), send_index, (1, 2, 3, 4), size)
    own[0], other[0] = late[2:]
    own[3], own[4] = go(3, late[0]), go(4, late[0])
    own[1], own[2] = tie(own[1], late[0]), tie(own[2], late[0])
    own[5] = go(5, tie(late[1], own[1]))
    own[6] = go(6, tie(late[1], own[2]))

    named, table = tie(named, late[0]), tie(jnp.asarray(chunk_order()), late[0])
    order = table[lax.axis_index("shard"), lax.axis_index("rep")]
    flat = named.reshape(16, size)[order].reshape(1, 16 * size)

    def score(best, count, passes, carry=(), after=()):
        arrays, loads = [], []
        for r, side in CHUNKS[:count]:
            chunk = (own, other)[side][r]
            array, place = chunk if isinstance(chunk, tuple) else (chunk, 0)
            if not any(array is known for known in arrays):
                arrays.append(array)
            loads.append(([array is known for known in arrays].index(True), place))
        return gram_best(arrays, tuple(loads), size, flat, best, passes, carry, after)

    best = jnp.full((1, 16 * size), -1.0, jnp.float32)
    best, pair = score(best, 4, (new_pass(0, 3, 4, size),), (1, 2), (order, index))
    pair = swap(pair)
    other[1], other[2] = (pair, 0), (pair, 1)
    early_pair = join(tie(own[3], best), tie(own[4], best), LONG // 2)
    own[7] = go(7, tie(late[2], own[3]))
    pair = swap(early_pair)
    own[3], own[4] = (early_pair, 0), (early_pair, 1)
    best, _ = score(best, 8, (new_pass(6, 2, 8, size), late_pass(1, 2, 4, 6, size)))
    other[3], other[4] = (pair, 0), (pair, 1)
    late_pair = join(tie(own[5], best), tie(own[6], best), LONG // 2)
    pair = swap(late_pair)
    own[5], own[6] = (late_pair, 0), (late_pair, 1)
    best, _ = score(best, 12, (new_pass(10, 2, 12, size), late_pass(6, 2, 8, 10, size)))
    other[5], other[6] = (pair, 0), (pair, 1)
    own[7] = tie(own[7], best)
    other[7] = swap(own[7])
    best, _ = score(best, 15, (new_pass(14, 1, 15, size), late_pass(10, 2, 12, 14, size)))
    outbound = finish(order, own[7], other[7], flat, best)
    returned = lax.all_to_all(outbound, axes, split_axis=0, concat_axis=0, tiled=True)
    sources = []
    for owner in range(8):
        host, y = host_of(owner)
        for half in range(2):
            sources.append(tuple((host * 4 + y * 2 + core, half) for core in range(2)))
    return settle(index, returned, tuple(sources), documents)


def gathered(embeddings, send_index, place_index, slot_cluster):
    documents, width = embeddings.shape
    owners = lax.axis_size("shard")
    reps = lax.axis_size("rep")
    share = send_index.shape[0] // owners
    outgoing = normalize(embeddings.at[send_index].get(mode="promise_in_bounds"))
    arrived = lax.all_to_all(
        outgoing.reshape(owners, share, width), "shard", split_axis=0, concat_axis=0, tiled=True
    )
    parts = 16
    size = documents // parts
    news = parts // reps
    turn = lax.axis_index("rep") * news
    arrived = jnp.roll(arrived.reshape(parts, size, width), -turn, axis=0)
    clusters = arrival_names(place_index, slot_cluster).reshape(parts, size)
    clusters = jnp.roll(clusters, -turn, axis=0)
    best = jnp.full((1, documents), -1.0, jnp.float32)
    tiles = tuple(range(documents // BLK))
    passes = ((0, news, 0, 1, True, tiles),)
    chunks = [arrived[i] for i in range(parts)]
    loads = tuple((i, 0) for i in range(parts))
    best, _ = gram_best(chunks, loads, size, clusters.reshape(1, -1), best, passes)
    best = lax.all_gather(best[0, : news * size], "rep", axis=0, tiled=True)
    returned = lax.all_to_all(
        best.reshape(owners, share), "shard", split_axis=0, concat_axis=0, tiled=True
    )
    sources = tuple(((0, g),) for g in range(parts))
    return settle(send_index.reshape(parts, size), returned.reshape(1, parts, size), sources, documents)


def solution(mesh):
    planned = mesh.shape["shard"] == 8 and mesh.shape["rep"] == 4

    def shards(embeddings, send_index, place_index, slot_cluster, pair_list):
        del pair_list
        run = hosted if planned else gathered
        return run(embeddings, send_index, place_index, slot_cluster)

    return jax.shard_map(
        shards,
        mesh=mesh,
        in_specs=(P("shard", None), P("shard"), P("shard"), P("shard"), P(("shard", "rep"), None)),
        out_specs=P("shard"),
        check_vma=False,
    )
```

```python
import functools

import jax
import jax.numpy as jnp
import numpy as np
from jax import lax
from jax.experimental import pallas as pl
from jax.experimental.pallas import tpu as pltpu
from jax.sharding import PartitionSpec as P

BLK = 256
LANES = 128
NT = (((1,), (1,)), ((), ()))
MIB = 1024 * 1024
LONG = 40_000_000_000
SHORT = 2_000_000_000

HOSTS = (2, 3, 4, 5)
ROUNDS = ((2, 6, 3, 7, 4, 1, 5), (3, 7, 2, 6, 5, 1, 4))


CHUNKS = (
    (0, 1), (0, 0), (1, 0), (2, 0),
    (3, 0), (4, 0), (1, 1),
    (2, 1), (3, 1), (4, 1), (5, 0), (6, 0),
    (5, 1), (6, 1), (7, 0), (7, 1),
)


def host_of(owner):
    z, x = owner // 2, owner % 2
    return (1 if z < 2 else 2) * 2 + x, z % 2


def chunk_order():
    order = np.zeros((8, 4, 16), np.int32)
    for s in range(8):
        for rep in range(4):
            for i, (step, side) in enumerate(CHUNKS):
                half = rep % 2 ^ side
                order[s, rep, i] = (s ^ ((0,) + ROUNDS[half])[step]) * 2 + half
    return order


def round_pairs(step):
    pairs = []
    for rep in range(4):
        for host in HOSTS:
            pairs.append(((host ^ ROUNDS[rep % 2][step]) * 4 + rep, host * 4 + rep))
    return pairs


SIBLINGS = [(host * 4 + rep, host * 4 + (rep ^ 1)) for host in HOSTS for rep in range(4)]


def metadata_pairs():
    pairs = []
    for owner in range(8):
        host, y = host_of(owner)
        for core in range(2):
            pairs.append((owner * 4 + y * 2 + core, host * 4 + y * 2 + core))
    return pairs


def tie(value, *after):
    return lax.optimization_barrier((value, *after))[0]


def normalize(rows):
    wide = rows.astype(jnp.float32)
    return (wide * lax.rsqrt(jnp.sum(wide * wide, axis=1, keepdims=True) + 1e-06)).astype(
        jnp.bfloat16
    )


def names_kernel(place_ref, slots_ref, out_ref):
    block = place_ref[...] // BLK
    found = jnp.zeros_like(block)
    for i in range(slots_ref.shape[0] * LANES // BLK):
        row = i * BLK // LANES
        found = jnp.where(block == i, slots_ref[row : row + 1, 0:1], found)
    out_ref[...] = found


def arrival_names(place_index, slot_cluster):
    places = place_index.reshape(-1, LANES)
    return pl.pallas_call(
        names_kernel, out_shape=jax.ShapeDtypeStruct(places.shape, jnp.int32)
    )(places, slot_cluster.reshape(-1, LANES))


def chunk_start(slot, size):
    s, rep = lax.axis_index("shard"), lax.axis_index("rep")
    y, core = rep // 2, rep % 2
    inner = (s >= HOSTS[0]) & (s <= HOSTS[-1])
    turn = min(slot, 3)
    steps = [(order[2 * turn], (order + (0,))[2 * turn + 1]) for order in ROUNDS]
    outer_step = jnp.where(core == 0, steps[0][0], steps[1][0])
    inner_step = jnp.where(core == 0, steps[0][1], steps[1][1])
    target = s ^ jnp.where(inner, inner_step, outer_step)
    owner = (2 * (target // 2 - 1) + y) * 2 + target % 2
    half = 1 - core if slot == 4 else core
    return owner * (2 * size) + half * size


def gather_kernel(slots, size, group, sections, *refs):
    index_hbm, rows_ref = refs[:2]
    index_ref, raw, wide, picked, sems = refs[-5:]
    outs = refs[-5 - len(slots) : -5]
    listed = pltpu.make_async_copy(index_hbm, index_ref, sems.at[sections])
    listed.start()
    width = raw.shape[1]
    tiles = width // LANES
    part = raw.shape[0] // sections
    copies = []
    for i in range(sections):
        rows = pl.ds(i * part, part)
        copies.append(pltpu.make_async_copy(rows_ref.at[rows], raw.at[rows], sems.at[i]))
        copies[-1].start()
    step = 160
    for i in range(sections):
        copies[i].wait()

        def widen(j, _, i=i):
            first = i * part + j * step
            rows = raw[pl.ds(pl.multiple_of(first, step), step), :].astype(jnp.float32)
            for t in range(tiles):
                wide[pl.ds(first * tiles + t, step, stride=tiles), :] = rows[:, t * LANES : (t + 1) * LANES]
            return 0

        lax.fori_loop(0, part // step, widen, 0)
    listed.wait()
    for c, slot in enumerate(slots):
        base = chunk_start(slot, size)

        def pick(j, _, c=c, base=base):
            for t in range(group):
                source = pl.multiple_of(index_ref[base + j * group + t] * tiles, tiles)
                picked[t * tiles : (t + 1) * tiles, :] = wide[pl.ds(source, tiles), :]
            for first in range(0, group, 16):
                rows = jnp.concatenate(
                    [picked[pl.ds(first * tiles + t, 16, stride=tiles), :] for t in range(tiles)],
                    axis=1,
                )
                scale = lax.rsqrt(jnp.sum(rows * rows, axis=1, keepdims=True) + 1e-06)
                outs[c][pl.ds(pl.multiple_of(j * group + first, 16), 16), :] = (rows * scale).astype(
                    jnp.bfloat16
                )
            return 0

        lax.fori_loop(0, size // group, pick, 0)


def gather_rows(embeddings, index, slots, size):
    documents, width = embeddings.shape
    count = len(slots)
    sections = 10
    group = 80
    return pl.pallas_call(
        functools.partial(gather_kernel, slots, size, group, sections),
        out_shape=[jax.ShapeDtypeStruct((size, width), jnp.bfloat16)] * count,
        in_specs=[pl.BlockSpec(memory_space=pltpu.HBM)] * 2,
        out_specs=[pl.BlockSpec(memory_space=pltpu.VMEM)] * count,
        scratch_shapes=[
            pltpu.SMEM(index.shape, jnp.int32),
            pltpu.VMEM((documents, width), jnp.bfloat16),
            pltpu.VMEM((documents * width // LANES, LANES), jnp.float32),
            pltpu.VMEM((group * width // LANES, LANES), jnp.float32),
            pltpu.SemaphoreType.DMA((sections + 1,)),
        ],
        compiler_params=pltpu.CompilerParams(vmem_limit_bytes=45 * MIB),
        cost_estimate=pl.CostEstimate(flops=LONG, bytes_accessed=0, transcendentals=0),
    )(index, embeddings)


def best_of_rows(acc, size):
    return jnp.max(jnp.transpose(acc), axis=0, keepdims=True)[:, :size]


def as_column(row_ref, start, size):
    wide = -(-size // LANES) * LANES
    row = row_ref[:, start : start + wide]
    return jnp.transpose(jnp.broadcast_to(row, (LANES, wide)))[:size]


def gram_kernel(passes, loads, size, limit, *refs):
    cluster_row, before_ref, best_ref, held, acc, sems = refs[-6:]
    count = len(loads)
    first = range(passes[0][0], passes[0][0] + passes[0][1])

    def source(i):
        array, place = loads[i]
        return refs[array].at[pl.ds(place * size, size)]

    def copy(i):
        return pltpu.make_async_copy(source(i), held.at[pl.ds(i * size, size)], sems.at[i])

    def arrive(i):
        rows = held.at[pl.ds(0, size)]
        pltpu.make_async_copy(rows, rows, sems.at[i]).wait()

    for i in first:
        copy(i).start()
    for i in range(count):
        if i not in first:
            copy(i).start()
    best_ref[...] = before_ref[...]
    for i in first:
        copy(i).wait()
    for n, (chunk, news, groups, group, meets, last) in enumerate(passes):
        height = news * size
        acc[...] = jnp.full_like(acc, -1.0)
        rows = held[chunk * size : chunk * size + height, :]
        left = as_column(cluster_row, chunk * size, height)
        left = jnp.concatenate([left, left], axis=1)

        def tile(start, special, chunk=chunk, height=height, rows=rows, left=left):
            gram = lax.dot_general(
                rows, held[pl.ds(start, BLK), :], NT, preferred_element_type=jnp.float32
            )
            counts = left == cluster_row[:, pl.ds(start, BLK)]
            if special:
                column = start + lax.broadcasted_iota(jnp.int32, (height, BLK), 1)
                row = chunk * size + lax.broadcasted_iota(jnp.int32, (height, BLK), 0)
                counts = counts & (column != row) & (column < limit)
            values = jnp.where(counts, gram, jnp.float32(-1.0))
            top = jnp.max(values, axis=0, keepdims=True)
            best_ref[:, pl.ds(start, BLK)] = jnp.maximum(best_ref[:, pl.ds(start, BLK)], top)
            acc[0:height, :] = jnp.maximum(
                acc[0:height, :], jnp.maximum(values[:, :LANES], values[:, LANES:])
            )

        def visit(u, _, n=n, group=group, meets=meets, tile=tile):
            if n == 0:
                for i in (2 * u, 2 * u + 1):

                    @pl.when(i < first[0])
                    def _(i=i):
                        arrive(i)

            for t in range(group):
                tile(pl.multiple_of((u * group + t) * BLK, BLK), meets)
            return 0

        lax.fori_loop(0, groups, visit, 0)
        if n == 0:
            for i in range(count):
                if i not in first and not i < min(2 * groups, first[0]):
                    arrive(i)
        for t in last:
            tile(t * BLK, True)
        span = slice(chunk * size, chunk * size + height)
        best_ref[:, span] = jnp.maximum(best_ref[:, span], best_of_rows(acc[...], height))


def gram_best(arrays, loads, size, cluster_row, before, passes, after=()):
    width = arrays[0].shape[1]
    limit = len(loads) * size
    held = -(-limit // BLK) * BLK
    tall = max(news for _, news, *_ in passes) * size
    padded = -(-tall // LANES) * LANES
    return pl.pallas_call(
        functools.partial(gram_kernel, passes, loads, size, limit),
        out_shape=jax.ShapeDtypeStruct(before.shape, jnp.float32),
        in_specs=[pl.BlockSpec(memory_space=pl.ANY)] * (len(arrays) + len(after))
        + [pl.BlockSpec(memory_space=pltpu.VMEM)] * 2,
        out_specs=pl.BlockSpec(memory_space=pltpu.VMEM),
        scratch_shapes=[
            pltpu.VMEM((held, width), jnp.bfloat16),
            pltpu.VMEM((padded, LANES), jnp.float32),
            pltpu.SemaphoreType.DMA((len(loads),)),
        ],
        compiler_params=pltpu.CompilerParams(vmem_limit_bytes=24 * MIB),
        cost_estimate=pl.CostEstimate(flops=0, bytes_accessed=0, transcendentals=0),
    )(*arrays, *after, cluster_row, before)


def join_kernel(size, *refs):
    out_ref, sems = refs[-2:]
    copies = [
        pltpu.make_async_copy(ref, out_ref.at[pl.ds(i * size, size)], sems.at[i])
        for i, ref in enumerate(refs[:-2])
    ]
    for copy in copies:
        copy.start()
    for copy in copies:
        copy.wait()


def join(chunks, work):
    size, width = chunks[0].shape
    return pl.pallas_call(
        functools.partial(join_kernel, size),
        out_shape=jax.ShapeDtypeStruct((len(chunks) * size, width), chunks[0].dtype),
        in_specs=[pl.BlockSpec(memory_space=pl.ANY)] * len(chunks),
        out_specs=pl.BlockSpec(memory_space=pl.ANY),
        scratch_shapes=[pltpu.SemaphoreType.DMA((len(chunks),))],
        compiler_params=pltpu.CompilerParams(vmem_limit_bytes=MIB),
        cost_estimate=pl.CostEstimate(flops=work, bytes_accessed=0, transcendentals=0),
    )(*chunks)


def new_pass(chunk, news, count, size):
    group = 3
    groups = chunk * size // (group * BLK)
    tiles = -(-count * size // BLK)
    return (chunk, news, groups, group, False, tuple(range(groups * group, tiles)))


def late_pass(chunk, news, low, high, size):
    return (chunk, news, 0, 1, True, tuple(range(low * size // BLK, -(-high * size // BLK))))


def finish_kernel(size, order_ref, own_ref, other_ref, clusters_ref, best_ref, out_ref, acc):
    gram = lax.dot_general(own_ref[...], other_ref[...], NT, preferred_element_type=jnp.float32)
    left = as_column(clusters_ref, 14 * size, size)
    left = jnp.tile(left, (1, -(-size // LANES)))[:, :size]
    last = 15 * size
    values = jnp.where(left == clusters_ref[:, last : last + size], gram, jnp.float32(-1.0))
    acc[...] = jnp.full_like(acc, -1.0)
    acc[0:size, :] = jnp.broadcast_to(jnp.max(values, axis=1, keepdims=True), (size, LANES))
    for i in range(16):
        found = best_ref[:, i * size : (i + 1) * size]
        if i == 14:
            found = jnp.maximum(found, best_of_rows(acc[...], size))
        if i == 15:
            found = jnp.maximum(found, jnp.max(values, axis=0, keepdims=True))
        place = order_ref[i]
        source, half = place // 2, place % 2
        for rep in range(4):
            out_ref[source * 4 + rep, pl.ds(half, 1), :] = found


def finish(order, own, other, clusters, best):
    size = own.shape[0]
    padded = -(-size // LANES) * LANES
    return pl.pallas_call(
        functools.partial(finish_kernel, size),
        out_shape=jax.ShapeDtypeStruct((32, 2, size), jnp.float32),
        in_specs=[pl.BlockSpec(memory_space=pltpu.SMEM)]
        + [pl.BlockSpec(memory_space=pltpu.VMEM)] * 4,
        out_specs=pl.BlockSpec(memory_space=pltpu.VMEM),
        scratch_shapes=[pltpu.VMEM((padded, LANES), jnp.float32)],
        compiler_params=pltpu.CompilerParams(vmem_limit_bytes=16 * MIB),
    )(order, own, other, clusters, best)


def settle_kernel(sources, size, high, index_ref, values_ref, out_ref, left_ref, right_ref):
    wide = left_ref.shape[1] // len(sources)
    left_ref[...] = jnp.zeros_like(left_ref)
    right_ref[...] = jnp.zeros_like(right_ref)
    rows = lax.broadcasted_iota(jnp.int32, (high, size), 0)
    lanes = lax.broadcasted_iota(jnp.int32, (LANES, size), 0)
    for g, places in enumerate(sources):
        index = index_ref[g // 2, g % 2 : g % 2 + 1, :] if index_ref.ndim == 3 else index_ref[g : g + 1, :]
        value = values_ref[places[0][0], places[0][1] : places[0][1] + 1, :]
        for a, b in places[1:]:
            value = jnp.maximum(value, values_ref[a, b : b + 1, :])
        span = slice(g * wide, g * wide + size)
        here = rows == index // LANES
        for piece in range(3):
            head = value.astype(jnp.bfloat16).astype(jnp.float32)
            value = value - head
            left_ref[piece * high : (piece + 1) * high, span] = jnp.where(here, head, 0.0).astype(
                jnp.bfloat16
            )
        right_ref[:, span] = jnp.where(lanes == index % LANES, 1.0, 0.0).astype(jnp.bfloat16)
    total = lax.dot_general(left_ref[...], right_ref[...], NT, preferred_element_type=jnp.float32)
    total = total[2 * high : 3 * high] + total[high : 2 * high] + total[:high]
    out_ref[...] = total[: out_ref.shape[0]]


def settle(index, values, sources, documents):
    size = index.shape[-1]
    high = -(-documents // (16 * LANES)) * 16
    wide = -(-size // LANES) * LANES * len(sources)
    out = pl.pallas_call(
        functools.partial(settle_kernel, sources, size, high),
        out_shape=jax.ShapeDtypeStruct((documents // LANES, LANES), jnp.float32),
        scratch_shapes=[
            pltpu.VMEM((3 * high, wide), jnp.bfloat16),
            pltpu.VMEM((LANES, wide), jnp.bfloat16),
        ],
        compiler_params=pltpu.CompilerParams(vmem_limit_bytes=16 * MIB),
    )(index, values)
    return out.reshape(-1)


def hosted(embeddings, send_index, place_index, slot_cluster):
    documents = embeddings.shape[0]
    size = send_index.shape[0] // 16
    axes = ("shard", "rep")
    named = arrival_names(place_index, slot_cluster)
    embeddings = tie(embeddings, named)
    (early,) = gather_rows(embeddings, send_index, (0,), size)
    named = lax.ppermute(named, axes, metadata_pairs())
    early = tie(early, named)
    index = send_index.reshape(8, 2, size)

    def go(step, chunk):
        return lax.ppermute(chunk, axes, round_pairs(step - 1))

    def swap(chunk):
        return lax.ppermute(chunk, axes, SIBLINGS)

    own, other = [None] * 8, [None] * 8
    own[1], own[2] = go(1, early), go(2, early)
    late = gather_rows(tie(embeddings, early), send_index, (1, 2, 3, 4), size)
    own[0], other[0] = late[2:]
    own[3], own[4] = go(3, late[0]), go(4, late[0])
    own[1], own[2] = tie(own[1], late[0]), tie(own[2], late[0])
    own[5] = go(5, tie(late[1], own[1]))
    own[6] = go(6, tie(late[1], own[2]))

    named, table = tie(named, late[0]), tie(jnp.asarray(chunk_order()), late[0])
    order = table[lax.axis_index("shard"), lax.axis_index("rep")]
    flat = named.reshape(16, size)[order].reshape(1, 16 * size)

    def score(best, count, passes, after=()):
        arrays, loads = [], []
        for r, side in CHUNKS[:count]:
            chunk = (own, other)[side][r]
            array, place = chunk if isinstance(chunk, tuple) else (chunk, 0)
            if not any(array is known for known in arrays):
                arrays.append(array)
            loads.append(([array is known for known in arrays].index(True), place))
        return gram_best(arrays, tuple(loads), size, flat, best, passes, after)

    best = jnp.full((1, 16 * size), -1.0, jnp.float32)
    best = score(best, 4, (new_pass(1, 3, 4, size),), (order, index))
    other[1] = swap(tie(own[1], best))
    joined = join([own[2], tie(own[3], best), tie(own[4], best)], SHORT)
    own[7] = go(7, tie(late[2], own[3]))
    swapped = swap(joined)
    own[3], own[4] = (joined, 1), (joined, 2)
    best = score(best, 7, (new_pass(4, 2, 7, size), late_pass(2, 2, 6, 7, size)))
    other[2], other[3], other[4] = (swapped, 0), (swapped, 1), (swapped, 2)
    joined = join([tie(own[5], best), tie(own[6], best)], LONG)
    swapped = swap(joined)
    own[5], own[6] = (joined, 0), (joined, 1)
    best = score(best, 12, (new_pass(10, 2, 12, size), late_pass(3, 3, 7, 10, size)))
    other[5], other[6] = (swapped, 0), (swapped, 1)
    own[7] = tie(own[7], best)
    other[7] = swap(own[7])
    best = score(best, 15, (new_pass(14, 1, 15, size), late_pass(10, 2, 12, 14, size)))
    outbound = finish(order, own[7], other[7], flat, best)
    returned = lax.all_to_all(outbound, axes, split_axis=0, concat_axis=0, tiled=True)
    sources = []
    for owner in range(8):
        host, y = host_of(owner)
        for half in range(2):
            sources.append(tuple((host * 4 + y * 2 + core, half) for core in range(2)))
    return settle(index, returned, tuple(sources), documents)


def gathered(embeddings, send_index, place_index, slot_cluster):
    documents, width = embeddings.shape
    owners = lax.axis_size("shard")
    reps = lax.axis_size("rep")
    share = send_index.shape[0] // owners
    outgoing = normalize(embeddings.at[send_index].get(mode="promise_in_bounds"))
    arrived = lax.all_to_all(
        outgoing.reshape(owners, share, width), "shard", split_axis=0, concat_axis=0, tiled=True
    )
    parts = 16
    size = documents // parts
    news = parts // reps
    turn = lax.axis_index("rep") * news
    arrived = jnp.roll(arrived.reshape(parts, size, width), -turn, axis=0)
    clusters = arrival_names(place_index, slot_cluster).reshape(parts, size)
    clusters = jnp.roll(clusters, -turn, axis=0)
    best = jnp.full((1, documents), -1.0, jnp.float32)
    tiles = tuple(range(documents // BLK))
    passes = ((0, news, 0, 1, True, tiles),)
    chunks = [arrived[i] for i in range(parts)]
    loads = tuple((i, 0) for i in range(parts))
    best = gram_best(chunks, loads, size, clusters.reshape(1, -1), best, passes)
    best = lax.all_gather(best[0, : news * size], "rep", axis=0, tiled=True)
    returned = lax.all_to_all(
        best.reshape(owners, share), "shard", split_axis=0, concat_axis=0, tiled=True
    )
    sources = tuple(((0, g),) for g in range(parts))
    return settle(send_index.reshape(parts, size), returned.reshape(1, parts, size), sources, documents)


def solution(mesh):
    planned = mesh.shape["shard"] == 8 and mesh.shape["rep"] == 4

    def shards(embeddings, send_index, place_index, slot_cluster, pair_list):
        del pair_list
        run = hosted if planned else gathered
        return run(embeddings, send_index, place_index, slot_cluster)

    return jax.shard_map(
        shards,
        mesh=mesh,
        in_specs=(P("shard", None), P("shard"), P("shard"), P("shard"), P(("shard", "rep"), None)),
        out_specs=P("shard"),
        check_vma=False,
    )
```

```python
import functools

import jax
import jax.numpy as jnp
import numpy as np
from jax import lax
from jax.experimental import pallas as pl
from jax.experimental.pallas import tpu as pltpu
from jax.sharding import PartitionSpec as P

BLK = 256
LANES = 128
NT = (((1,), (1,)), ((), ()))
MIB = 1024 * 1024
LONG = 40_000_000_000
SHORT = 2_000_000_000

HOSTS = (2, 3, 4, 5)
ROUNDS = ((2, 6, 3, 7, 4, 1, 5), (3, 7, 2, 6, 5, 1, 4))


CHUNKS = (
    (0, 1), (0, 0), (1, 0), (2, 0),
    (3, 0), (4, 0), (1, 1),
    (2, 1), (3, 1), (4, 1), (5, 0), (6, 0),
    (5, 1), (6, 1), (7, 0), (7, 1),
)


def host_of(owner):
    z, x = owner // 2, owner % 2
    return (1 if z < 2 else 2) * 2 + x, z % 2


def chunk_order():
    order = np.zeros((8, 4, 16), np.int32)
    for s in range(8):
        for rep in range(4):
            for i, (step, side) in enumerate(CHUNKS):
                half = rep % 2 ^ side
                order[s, rep, i] = (s ^ ((0,) + ROUNDS[half])[step]) * 2 + half
    return order


def round_pairs(step):
    pairs = []
    for rep in range(4):
        for host in HOSTS:
            pairs.append(((host ^ ROUNDS[rep % 2][step]) * 4 + rep, host * 4 + rep))
    return pairs


SIBLINGS = [(host * 4 + rep, host * 4 + (rep ^ 1)) for host in HOSTS for rep in range(4)]


def metadata_pairs():
    pairs = []
    for owner in range(8):
        host, y = host_of(owner)
        for core in range(2):
            pairs.append((owner * 4 + y * 2 + core, host * 4 + y * 2 + core))
    return pairs


def tie(value, *after):
    return lax.optimization_barrier((value, *after))[0]


def normalize(rows):
    wide = rows.astype(jnp.float32)
    return (wide * lax.rsqrt(jnp.sum(wide * wide, axis=1, keepdims=True) + 1e-06)).astype(
        jnp.bfloat16
    )


def names_kernel(place_ref, slots_ref, out_ref):
    block = place_ref[...] // BLK
    found = jnp.zeros_like(block)
    for i in range(slots_ref.shape[0] * LANES // BLK):
        row = i * BLK // LANES
        found = jnp.where(block == i, slots_ref[row : row + 1, 0:1], found)
    out_ref[...] = found


def arrival_names(place_index, slot_cluster):
    places = place_index.reshape(-1, LANES)
    return pl.pallas_call(
        names_kernel, out_shape=jax.ShapeDtypeStruct(places.shape, jnp.int32)
    )(places, slot_cluster.reshape(-1, LANES))


def chunk_start(slot, size):
    s, rep = lax.axis_index("shard"), lax.axis_index("rep")
    y, core = rep // 2, rep % 2
    inner = (s >= HOSTS[0]) & (s <= HOSTS[-1])
    turn = min(slot, 3)
    steps = [(order[2 * turn], (order + (0,))[2 * turn + 1]) for order in ROUNDS]
    outer_step = jnp.where(core == 0, steps[0][0], steps[1][0])
    inner_step = jnp.where(core == 0, steps[0][1], steps[1][1])
    target = s ^ jnp.where(inner, inner_step, outer_step)
    owner = (2 * (target // 2 - 1) + y) * 2 + target % 2
    half = 1 - core if slot == 4 else core
    return owner * (2 * size) + half * size


def gather_kernel(slots, size, group, sections, *refs):
    index_hbm, rows_ref = refs[:2]
    index_ref, raw, wide, picked, sems = refs[-5:]
    outs = refs[-5 - len(slots) : -5]
    listed = pltpu.make_async_copy(index_hbm, index_ref, sems.at[sections])
    listed.start()
    width = raw.shape[1]
    tiles = width // LANES
    part = raw.shape[0] // sections
    copies = []
    for i in range(sections):
        rows = pl.ds(i * part, part)
        copies.append(pltpu.make_async_copy(rows_ref.at[rows], raw.at[rows], sems.at[i]))
        copies[-1].start()
    step = 160
    for i in range(sections):
        copies[i].wait()

        def widen(j, _, i=i):
            first = i * part + j * step
            rows = raw[pl.ds(pl.multiple_of(first, step), step), :].astype(jnp.float32)
            for t in range(tiles):
                wide[pl.ds(first * tiles + t, step, stride=tiles), :] = rows[:, t * LANES : (t + 1) * LANES]
            return 0

        lax.fori_loop(0, part // step, widen, 0)
    listed.wait()
    for c, slot in enumerate(slots):
        base = chunk_start(slot, size)

        def pick(j, _, c=c, base=base):
            for t in range(group):
                source = pl.multiple_of(index_ref[base + j * group + t] * tiles, tiles)
                picked[t * tiles : (t + 1) * tiles, :] = wide[pl.ds(source, tiles), :]
            for first in range(0, group, 16):
                rows = jnp.concatenate(
                    [picked[pl.ds(first * tiles + t, 16, stride=tiles), :] for t in range(tiles)],
                    axis=1,
                )
                scale = lax.rsqrt(jnp.sum(rows * rows, axis=1, keepdims=True) + 1e-06)
                outs[c][pl.ds(pl.multiple_of(j * group + first, 16), 16), :] = (rows * scale).astype(
                    jnp.bfloat16
                )
            return 0

        lax.fori_loop(0, size // group, pick, 0)


def gather_rows(embeddings, index, slots, size):
    documents, width = embeddings.shape
    count = len(slots)
    sections = 10
    group = 80
    return pl.pallas_call(
        functools.partial(gather_kernel, slots, size, group, sections),
        out_shape=[jax.ShapeDtypeStruct((size, width), jnp.bfloat16)] * count,
        in_specs=[pl.BlockSpec(memory_space=pltpu.HBM)] * 2,
        out_specs=[pl.BlockSpec(memory_space=pltpu.VMEM)] * count,
        scratch_shapes=[
            pltpu.SMEM(index.shape, jnp.int32),
            pltpu.VMEM((documents, width), jnp.bfloat16),
            pltpu.VMEM((documents * width // LANES, LANES), jnp.float32),
            pltpu.VMEM((group * width // LANES, LANES), jnp.float32),
            pltpu.SemaphoreType.DMA((sections + 1,)),
        ],
        compiler_params=pltpu.CompilerParams(vmem_limit_bytes=45 * MIB),
        cost_estimate=pl.CostEstimate(flops=LONG, bytes_accessed=0, transcendentals=0),
    )(index, embeddings)


def best_of_rows(acc, size):
    return jnp.max(jnp.transpose(acc), axis=0, keepdims=True)[:, :size]


def as_column(row_ref, start, size):
    wide = -(-size // LANES) * LANES
    row = row_ref[:, start : start + wide]
    return jnp.transpose(jnp.broadcast_to(row, (LANES, wide)))[:size]


def gram_kernel(passes, loads, size, limit, *refs):
    cluster_row, before_ref, best_ref, held, acc, sems = refs[-6:]
    count = len(loads)
    first = range(passes[0][0], passes[0][0] + passes[0][1])

    def source(i):
        array, place = loads[i]
        return refs[array].at[pl.ds(place * size, size)]

    def copy(i):
        return pltpu.make_async_copy(source(i), held.at[pl.ds(i * size, size)], sems.at[i])

    def arrive(i):
        rows = held.at[pl.ds(0, size)]
        pltpu.make_async_copy(rows, rows, sems.at[i]).wait()

    for i in first:
        copy(i).start()
    for i in range(count):
        if i not in first:
            copy(i).start()
    best_ref[...] = before_ref[...]
    for i in first:
        copy(i).wait()
    for n, (chunk, news, groups, group, meets, last) in enumerate(passes):
        height = news * size
        acc[...] = jnp.full_like(acc, -1.0)
        rows = held[chunk * size : chunk * size + height, :]
        left = as_column(cluster_row, chunk * size, height)
        left = jnp.concatenate([left, left], axis=1)

        def tile(start, special, chunk=chunk, height=height, rows=rows, left=left):
            gram = lax.dot_general(
                rows, held[pl.ds(start, BLK), :], NT, preferred_element_type=jnp.float32
            )
            counts = left == cluster_row[:, pl.ds(start, BLK)]
            if special:
                column = start + lax.broadcasted_iota(jnp.int32, (height, BLK), 1)
                row = chunk * size + lax.broadcasted_iota(jnp.int32, (height, BLK), 0)
                counts = counts & (column != row) & (column < limit)
            values = jnp.where(counts, gram, jnp.float32(-1.0))
            top = jnp.max(values, axis=0, keepdims=True)
            best_ref[:, pl.ds(start, BLK)] = jnp.maximum(best_ref[:, pl.ds(start, BLK)], top)
            acc[0:height, :] = jnp.maximum(
                acc[0:height, :], jnp.maximum(values[:, :LANES], values[:, LANES:])
            )

        def visit(u, _, n=n, group=group, meets=meets, tile=tile):
            if n == 0:
                for i in (2 * u, 2 * u + 1):

                    @pl.when(i < first[0])
                    def _(i=i):
                        arrive(i)

            for t in range(group):
                tile(pl.multiple_of((u * group + t) * BLK, BLK), meets)
            return 0

        lax.fori_loop(0, groups, visit, 0)
        if n == 0:
            for i in range(count):
                if i not in first and not i < min(2 * groups, first[0]):
                    arrive(i)
        for t in last:
            tile(t * BLK, True)
        span = slice(chunk * size, chunk * size + height)
        best_ref[:, span] = jnp.maximum(best_ref[:, span], best_of_rows(acc[...], height))


def gram_best(arrays, loads, size, cluster_row, before, passes, after=()):
    width = arrays[0].shape[1]
    limit = len(loads) * size
    held = -(-limit // BLK) * BLK
    tall = max(news for _, news, *_ in passes) * size
    padded = -(-tall // LANES) * LANES
    return pl.pallas_call(
        functools.partial(gram_kernel, passes, loads, size, limit),
        out_shape=jax.ShapeDtypeStruct(before.shape, jnp.float32),
        in_specs=[pl.BlockSpec(memory_space=pl.ANY)] * (len(arrays) + len(after))
        + [pl.BlockSpec(memory_space=pltpu.VMEM)] * 2,
        out_specs=pl.BlockSpec(memory_space=pltpu.VMEM),
        scratch_shapes=[
            pltpu.VMEM((held, width), jnp.bfloat16),
            pltpu.VMEM((padded, LANES), jnp.float32),
            pltpu.SemaphoreType.DMA((len(loads),)),
        ],
        compiler_params=pltpu.CompilerParams(vmem_limit_bytes=24 * MIB),
        cost_estimate=pl.CostEstimate(flops=0, bytes_accessed=0, transcendentals=0),
    )(*arrays, *after, cluster_row, before)


def join_kernel(size, *refs):
    out_ref, sems = refs[-2:]
    copies = [
        pltpu.make_async_copy(ref, out_ref.at[pl.ds(i * size, size)], sems.at[i])
        for i, ref in enumerate(refs[:-2])
    ]
    for copy in copies:
        copy.start()
    for copy in copies:
        copy.wait()


def join(chunks, work):
    size, width = chunks[0].shape
    return pl.pallas_call(
        functools.partial(join_kernel, size),
        out_shape=jax.ShapeDtypeStruct((len(chunks) * size, width), chunks[0].dtype),
        in_specs=[pl.BlockSpec(memory_space=pl.ANY)] * len(chunks),
        out_specs=pl.BlockSpec(memory_space=pl.ANY),
        scratch_shapes=[pltpu.SemaphoreType.DMA((len(chunks),))],
        compiler_params=pltpu.CompilerParams(vmem_limit_bytes=MIB),
        cost_estimate=pl.CostEstimate(flops=work, bytes_accessed=0, transcendentals=0),
    )(*chunks)


def new_pass(chunk, news, count, size):
    group = 3
    groups = chunk * size // (group * BLK)
    tiles = -(-count * size // BLK)
    return (chunk, news, groups, group, False, tuple(range(groups * group, tiles)))


def late_pass(chunk, news, low, high, size):
    return (chunk, news, 0, 1, True, tuple(range(low * size // BLK, -(-high * size // BLK))))


def finish_kernel(size, order_ref, own_ref, other_ref, clusters_ref, best_ref, out_ref, acc):
    gram = lax.dot_general(own_ref[...], other_ref[...], NT, preferred_element_type=jnp.float32)
    left = as_column(clusters_ref, 14 * size, size)
    left = jnp.tile(left, (1, -(-size // LANES)))[:, :size]
    last = 15 * size
    values = jnp.where(left == clusters_ref[:, last : last + size], gram, jnp.float32(-1.0))
    acc[...] = jnp.full_like(acc, -1.0)
    acc[0:size, :] = jnp.broadcast_to(jnp.max(values, axis=1, keepdims=True), (size, LANES))
    for i in range(16):
        found = best_ref[:, i * size : (i + 1) * size]
        if i == 14:
            found = jnp.maximum(found, best_of_rows(acc[...], size))
        if i == 15:
            found = jnp.maximum(found, jnp.max(values, axis=0, keepdims=True))
        place = order_ref[i]
        source, half = place // 2, place % 2
        for rep in range(4):
            out_ref[source * 4 + rep, pl.ds(half, 1), :] = found


def finish(order, own, other, clusters, best):
    size = own.shape[0]
    padded = -(-size // LANES) * LANES
    return pl.pallas_call(
        functools.partial(finish_kernel, size),
        out_shape=jax.ShapeDtypeStruct((32, 2, size), jnp.float32),
        in_specs=[pl.BlockSpec(memory_space=pltpu.SMEM)]
        + [pl.BlockSpec(memory_space=pltpu.VMEM)] * 4,
        out_specs=pl.BlockSpec(memory_space=pltpu.VMEM),
        scratch_shapes=[pltpu.VMEM((padded, LANES), jnp.float32)],
        compiler_params=pltpu.CompilerParams(vmem_limit_bytes=16 * MIB),
    )(order, own, other, clusters, best)


def settle_kernel(sources, size, high, index_ref, values_ref, out_ref, left_ref, right_ref):
    wide = left_ref.shape[1] // len(sources)
    left_ref[...] = jnp.zeros_like(left_ref)
    right_ref[...] = jnp.zeros_like(right_ref)
    rows = lax.broadcasted_iota(jnp.int32, (high, size), 0)
    lanes = lax.broadcasted_iota(jnp.int32, (LANES, size), 0)
    for g, places in enumerate(sources):
        index = index_ref[g // 2, g % 2 : g % 2 + 1, :] if index_ref.ndim == 3 else index_ref[g : g + 1, :]
        value = values_ref[places[0][0], places[0][1] : places[0][1] + 1, :]
        for a, b in places[1:]:
            value = jnp.maximum(value, values_ref[a, b : b + 1, :])
        span = slice(g * wide, g * wide + size)
        here = rows == index // LANES
        for piece in range(3):
            head = value.astype(jnp.bfloat16).astype(jnp.float32)
            value = value - head
            left_ref[piece * high : (piece + 1) * high, span] = jnp.where(here, head, 0.0).astype(
                jnp.bfloat16
            )
        right_ref[:, span] = jnp.where(lanes == index % LANES, 1.0, 0.0).astype(jnp.bfloat16)
    total = lax.dot_general(left_ref[...], right_ref[...], NT, preferred_element_type=jnp.float32)
    total = total[2 * high : 3 * high] + total[high : 2 * high] + total[:high]
    out_ref[...] = total[: out_ref.shape[0]]


def settle(index, values, sources, documents):
    size = index.shape[-1]
    high = -(-documents // (16 * LANES)) * 16
    wide = -(-size // LANES) * LANES * len(sources)
    out = pl.pallas_call(
        functools.partial(settle_kernel, sources, size, high),
        out_shape=jax.ShapeDtypeStruct((documents // LANES, LANES), jnp.float32),
        scratch_shapes=[
            pltpu.VMEM((3 * high, wide), jnp.bfloat16),
            pltpu.VMEM((LANES, wide), jnp.bfloat16),
        ],
        compiler_params=pltpu.CompilerParams(vmem_limit_bytes=16 * MIB),
    )(index, values)
    return out.reshape(-1)


def hosted(embeddings, send_index, place_index, slot_cluster):
    documents = embeddings.shape[0]
    size = send_index.shape[0] // 16
    axes = ("shard", "rep")
    named = arrival_names(place_index, slot_cluster)
    embeddings = tie(embeddings, named)
    (early,) = gather_rows(embeddings, send_index, (0,), size)
    named = lax.ppermute(named, axes, metadata_pairs())
    early = tie(early, named)
    index = send_index.reshape(8, 2, size)

    def go(step, chunk):
        return lax.ppermute(chunk, axes, round_pairs(step - 1))

    def swap(chunk):
        return lax.ppermute(chunk, axes, SIBLINGS)

    own, other = [None] * 8, [None] * 8
    own[1], own[2] = go(1, early), go(2, early)
    late = gather_rows(tie(embeddings, early), send_index, (1, 2, 3, 4), size)
    own[0], other[0] = late[2:]
    own[3], own[4] = go(3, late[0]), go(4, late[0])
    own[1], own[2] = tie(own[1], late[0]), tie(own[2], late[0])
    own[5] = go(5, tie(late[1], own[1]))
    own[6] = go(6, tie(late[1], own[2]))

    named, table = tie(named, late[0]), tie(jnp.asarray(chunk_order()), late[0])
    order = table[lax.axis_index("shard"), lax.axis_index("rep")]
    flat = named.reshape(16, size)[order].reshape(1, 16 * size)

    def score(best, count, passes, after=()):
        arrays, loads = [], []
        for r, side in CHUNKS[:count]:
            chunk = (own, other)[side][r]
            array, place = chunk if isinstance(chunk, tuple) else (chunk, 0)
            if not any(array is known for known in arrays):
                arrays.append(array)
            loads.append(([array is known for known in arrays].index(True), place))
        return gram_best(arrays, tuple(loads), size, flat, best, passes, after)

    best = jnp.full((1, 16 * size), -1.0, jnp.float32)
    best = score(best, 4, (new_pass(1, 3, 4, size),), (order, index))
    other[1] = swap(tie(own[1], best))
    joined = join([own[2], tie(own[3], best), tie(own[4], best)], SHORT)
    swapped = swap(joined)
    own[3], own[4] = (joined, 1), (joined, 2)
    best = score(best, 7, (new_pass(4, 2, 7, size), late_pass(2, 2, 6, 7, size)))
    own[7] = go(7, tie(late[2], best))
    other[2], other[3], other[4] = (swapped, 0), (swapped, 1), (swapped, 2)
    joined = join([tie(own[5], best), tie(own[6], best)], LONG)
    swapped = swap(joined)
    own[5], own[6] = (joined, 0), (joined, 1)
    best = score(best, 12, (new_pass(10, 2, 12, size), late_pass(3, 3, 7, 10, size)))
    other[5], other[6] = (swapped, 0), (swapped, 1)
    own[7] = tie(own[7], best)
    other[7] = swap(own[7])
    best = score(best, 15, (new_pass(14, 1, 15, size), late_pass(10, 2, 12, 14, size)))
    outbound = finish(order, own[7], other[7], flat, best)
    returned = lax.all_to_all(outbound, axes, split_axis=0, concat_axis=0, tiled=True)
    sources = []
    for owner in range(8):
        host, y = host_of(owner)
        for half in range(2):
            sources.append(tuple((host * 4 + y * 2 + core, half) for core in range(2)))
    return settle(index, returned, tuple(sources), documents)


def gathered(embeddings, send_index, place_index, slot_cluster):
    documents, width = embeddings.shape
    owners = lax.axis_size("shard")
    reps = lax.axis_size("rep")
    share = send_index.shape[0] // owners
    outgoing = normalize(embeddings.at[send_index].get(mode="promise_in_bounds"))
    arrived = lax.all_to_all(
        outgoing.reshape(owners, share, width), "shard", split_axis=0, concat_axis=0, tiled=True
    )
    parts = 16
    size = documents // parts
    news = parts // reps
    turn = lax.axis_index("rep") * news
    arrived = jnp.roll(arrived.reshape(parts, size, width), -turn, axis=0)
    clusters = arrival_names(place_index, slot_cluster).reshape(parts, size)
    clusters = jnp.roll(clusters, -turn, axis=0)
    best = jnp.full((1, documents), -1.0, jnp.float32)
    tiles = tuple(range(documents // BLK))
    passes = ((0, news, 0, 1, True, tiles),)
    chunks = [arrived[i] for i in range(parts)]
    loads = tuple((i, 0) for i in range(parts))
    best = gram_best(chunks, loads, size, clusters.reshape(1, -1), best, passes)
    best = lax.all_gather(best[0, : news * size], "rep", axis=0, tiled=True)
    returned = lax.all_to_all(
        best.reshape(owners, share), "shard", split_axis=0, concat_axis=0, tiled=True
    )
    sources = tuple(((0, g),) for g in range(parts))
    return settle(send_index.reshape(parts, size), returned.reshape(1, parts, size), sources, documents)


def solution(mesh):
    planned = mesh.shape["shard"] == 8 and mesh.shape["rep"] == 4

    def shards(embeddings, send_index, place_index, slot_cluster, pair_list):
        del pair_list
        run = hosted if planned else gathered
        return run(embeddings, send_index, place_index, slot_cluster)

    return jax.shard_map(
        shards,
        mesh=mesh,
        in_specs=(P("shard", None), P("shard"), P("shard"), P("shard"), P(("shard", "rep"), None)),
        out_specs=P("shard"),
        check_vma=False,
    )
```

```python
import functools

import jax
import jax.numpy as jnp
import numpy as np
from jax import lax
from jax.experimental import pallas as pl
from jax.experimental.pallas import tpu as pltpu
from jax.sharding import PartitionSpec as P

BLK = 256
LANES = 128
NT = (((1,), (1,)), ((), ()))
MIB = 1024 * 1024
LONG = 40_000_000_000
SHORT = 2_000_000_000

HOSTS = (2, 3, 4, 5)
ROUNDS = ((2, 6, 3, 7, 4, 1, 5), (3, 7, 2, 6, 4, 1, 5))


CHUNKS = (
    (0, 1), (0, 0), (1, 0), (2, 0),
    (3, 0), (4, 0), (1, 1),
    (2, 1), (3, 1), (4, 1), (5, 0), (6, 0),
    (5, 1), (6, 1), (7, 0), (7, 1),
)


def host_of(owner):
    z, x = owner // 2, owner % 2
    return (1 if z < 2 else 2) * 2 + x, z % 2


def chunk_order():
    order = np.zeros((8, 4, 16), np.int32)
    for s in range(8):
        for rep in range(4):
            for i, (step, side) in enumerate(CHUNKS):
                half = rep % 2 ^ side
                order[s, rep, i] = (s ^ ((0,) + ROUNDS[half])[step]) * 2 + half
    return order


def round_pairs(step):
    pairs = []
    for rep in range(4):
        for host in HOSTS:
            pairs.append(((host ^ ROUNDS[rep % 2][step]) * 4 + rep, host * 4 + rep))
    return pairs


SIBLINGS = [(host * 4 + rep, host * 4 + (rep ^ 1)) for host in HOSTS for rep in range(4)]


def metadata_pairs():
    pairs = []
    for owner in range(8):
        host, y = host_of(owner)
        for core in range(2):
            pairs.append((owner * 4 + y * 2 + core, host * 4 + y * 2 + core))
    return pairs


def tie(value, *after):
    return lax.optimization_barrier((value, *after))[0]


def normalize(rows):
    wide = rows.astype(jnp.float32)
    return (wide * lax.rsqrt(jnp.sum(wide * wide, axis=1, keepdims=True) + 1e-06)).astype(
        jnp.bfloat16
    )


def names_kernel(place_ref, slots_ref, out_ref):
    block = place_ref[...] // BLK
    found = jnp.zeros_like(block)
    for i in range(slots_ref.shape[0] * LANES // BLK):
        row = i * BLK // LANES
        found = jnp.where(block == i, slots_ref[row : row + 1, 0:1], found)
    out_ref[...] = found


def arrival_names(place_index, slot_cluster):
    places = place_index.reshape(-1, LANES)
    return pl.pallas_call(
        names_kernel, out_shape=jax.ShapeDtypeStruct(places.shape, jnp.int32)
    )(places, slot_cluster.reshape(-1, LANES))


def chunk_start(slot, size):
    s, rep = lax.axis_index("shard"), lax.axis_index("rep")
    y, core = rep // 2, rep % 2
    inner = (s >= HOSTS[0]) & (s <= HOSTS[-1])
    turn = min(slot, 3)
    steps = [(order[2 * turn], (order + (0,))[2 * turn + 1]) for order in ROUNDS]
    outer_step = jnp.where(core == 0, steps[0][0], steps[1][0])
    inner_step = jnp.where(core == 0, steps[0][1], steps[1][1])
    target = s ^ jnp.where(inner, inner_step, outer_step)
    owner = (2 * (target // 2 - 1) + y) * 2 + target % 2
    half = 1 - core if slot == 4 else core
    return owner * (2 * size) + half * size


def gather_kernel(slots, size, group, sections, *refs):
    index_hbm, rows_ref = refs[:2]
    index_ref, raw, wide, picked, sems = refs[-5:]
    outs = refs[-5 - len(slots) : -5]
    listed = pltpu.make_async_copy(index_hbm, index_ref, sems.at[sections])
    listed.start()
    width = raw.shape[1]
    tiles = width // LANES
    part = raw.shape[0] // sections
    copies = []
    for i in range(sections):
        rows = pl.ds(i * part, part)
        copies.append(pltpu.make_async_copy(rows_ref.at[rows], raw.at[rows], sems.at[i]))
        copies[-1].start()
    step = 160
    for i in range(sections):
        copies[i].wait()

        def widen(j, _, i=i):
            first = i * part + j * step
            rows = raw[pl.ds(pl.multiple_of(first, step), step), :].astype(jnp.float32)
            for t in range(tiles):
                wide[pl.ds(first * tiles + t, step, stride=tiles), :] = rows[:, t * LANES : (t + 1) * LANES]
            return 0

        lax.fori_loop(0, part // step, widen, 0)
    listed.wait()
    for c, slot in enumerate(slots):
        base = chunk_start(slot, size)

        def pick(j, _, c=c, base=base):
            for t in range(group):
                source = pl.multiple_of(index_ref[base + j * group + t] * tiles, tiles)
                picked[t * tiles : (t + 1) * tiles, :] = wide[pl.ds(source, tiles), :]
            for first in range(0, group, 16):
                rows = jnp.concatenate(
                    [picked[pl.ds(first * tiles + t, 16, stride=tiles), :] for t in range(tiles)],
                    axis=1,
                )
                scale = lax.rsqrt(jnp.sum(rows * rows, axis=1, keepdims=True) + 1e-06)
                outs[c][pl.ds(pl.multiple_of(j * group + first, 16), 16), :] = (rows * scale).astype(
                    jnp.bfloat16
                )
            return 0

        lax.fori_loop(0, size // group, pick, 0)


def gather_rows(embeddings, index, slots, size):
    documents, width = embeddings.shape
    count = len(slots)
    sections = 10
    group = 80
    return pl.pallas_call(
        functools.partial(gather_kernel, slots, size, group, sections),
        out_shape=[jax.ShapeDtypeStruct((size, width), jnp.bfloat16)] * count,
        in_specs=[pl.BlockSpec(memory_space=pltpu.HBM)] * 2,
        out_specs=[pl.BlockSpec(memory_space=pltpu.VMEM)] * count,
        scratch_shapes=[
            pltpu.SMEM(index.shape, jnp.int32),
            pltpu.VMEM((documents, width), jnp.bfloat16),
            pltpu.VMEM((documents * width // LANES, LANES), jnp.float32),
            pltpu.VMEM((group * width // LANES, LANES), jnp.float32),
            pltpu.SemaphoreType.DMA((sections + 1,)),
        ],
        compiler_params=pltpu.CompilerParams(vmem_limit_bytes=45 * MIB),
        cost_estimate=pl.CostEstimate(flops=LONG, bytes_accessed=0, transcendentals=0),
    )(index, embeddings)


def best_of_rows(acc, size):
    return jnp.max(jnp.transpose(acc), axis=0, keepdims=True)[:, :size]


def as_column(row_ref, start, size):
    wide = -(-size // LANES) * LANES
    row = row_ref[:, start : start + wide]
    return jnp.transpose(jnp.broadcast_to(row, (LANES, wide)))[:size]


def gram_kernel(passes, loads, size, limit, *refs):
    cluster_row, before_ref, best_ref, held, acc, sems = refs[-6:]
    count = len(loads)
    first = range(passes[0][0], passes[0][0] + passes[0][1])

    def source(i):
        array, place = loads[i]
        return refs[array].at[pl.ds(place * size, size)]

    def copy(i):
        return pltpu.make_async_copy(source(i), held.at[pl.ds(i * size, size)], sems.at[i])

    def arrive(i):
        rows = held.at[pl.ds(0, size)]
        pltpu.make_async_copy(rows, rows, sems.at[i]).wait()

    for i in first:
        copy(i).start()
    for i in range(count):
        if i not in first:
            copy(i).start()
    best_ref[...] = before_ref[...]
    for i in first:
        copy(i).wait()
    for n, (chunk, news, groups, group, meets, last) in enumerate(passes):
        height = news * size
        acc[...] = jnp.full_like(acc, -1.0)
        rows = held[chunk * size : chunk * size + height, :]
        left = as_column(cluster_row, chunk * size, height)
        left = jnp.concatenate([left, left], axis=1)

        def tile(start, special, chunk=chunk, height=height, rows=rows, left=left):
            gram = lax.dot_general(
                rows, held[pl.ds(start, BLK), :], NT, preferred_element_type=jnp.float32
            )
            counts = left == cluster_row[:, pl.ds(start, BLK)]
            if special:
                column = start + lax.broadcasted_iota(jnp.int32, (height, BLK), 1)
                row = chunk * size + lax.broadcasted_iota(jnp.int32, (height, BLK), 0)
                counts = counts & (column != row) & (column < limit)
            values = jnp.where(counts, gram, jnp.float32(-1.0))
            top = jnp.max(values, axis=0, keepdims=True)
            best_ref[:, pl.ds(start, BLK)] = jnp.maximum(best_ref[:, pl.ds(start, BLK)], top)
            acc[0:height, :] = jnp.maximum(
                acc[0:height, :], jnp.maximum(values[:, :LANES], values[:, LANES:])
            )

        def visit(u, _, n=n, group=group, meets=meets, tile=tile):
            if n == 0:
                for i in (2 * u, 2 * u + 1):

                    @pl.when(i < first[0])
                    def _(i=i):
                        arrive(i)

            for t in range(group):
                tile(pl.multiple_of((u * group + t) * BLK, BLK), meets)
            return 0

        lax.fori_loop(0, groups, visit, 0)
        if n == 0:
            for i in range(count):
                if i not in first and not i < min(2 * groups, first[0]):
                    arrive(i)
        for t in last:
            tile(t * BLK, True)
        span = slice(chunk * size, chunk * size + height)
        best_ref[:, span] = jnp.maximum(best_ref[:, span], best_of_rows(acc[...], height))


def gram_best(arrays, loads, size, cluster_row, before, passes, after=()):
    width = arrays[0].shape[1]
    limit = len(loads) * size
    held = -(-limit // BLK) * BLK
    tall = max(news for _, news, *_ in passes) * size
    padded = -(-tall // LANES) * LANES
    return pl.pallas_call(
        functools.partial(gram_kernel, passes, loads, size, limit),
        out_shape=jax.ShapeDtypeStruct(before.shape, jnp.float32),
        in_specs=[pl.BlockSpec(memory_space=pl.ANY)] * (len(arrays) + len(after))
        + [pl.BlockSpec(memory_space=pltpu.VMEM)] * 2,
        out_specs=pl.BlockSpec(memory_space=pltpu.VMEM),
        scratch_shapes=[
            pltpu.VMEM((held, width), jnp.bfloat16),
            pltpu.VMEM((padded, LANES), jnp.float32),
            pltpu.SemaphoreType.DMA((len(loads),)),
        ],
        compiler_params=pltpu.CompilerParams(vmem_limit_bytes=24 * MIB),
        cost_estimate=pl.CostEstimate(flops=0, bytes_accessed=0, transcendentals=0),
    )(*arrays, *after, cluster_row, before)


def join_kernel(size, *refs):
    out_ref, sems = refs[-2:]
    copies = [
        pltpu.make_async_copy(ref, out_ref.at[pl.ds(i * size, size)], sems.at[i])
        for i, ref in enumerate(refs[:-2])
    ]
    for copy in copies:
        copy.start()
    for copy in copies:
        copy.wait()


def join(chunks, work):
    size, width = chunks[0].shape
    return pl.pallas_call(
        functools.partial(join_kernel, size),
        out_shape=jax.ShapeDtypeStruct((len(chunks) * size, width), chunks[0].dtype),
        in_specs=[pl.BlockSpec(memory_space=pl.ANY)] * len(chunks),
        out_specs=pl.BlockSpec(memory_space=pl.ANY),
        scratch_shapes=[pltpu.SemaphoreType.DMA((len(chunks),))],
        compiler_params=pltpu.CompilerParams(vmem_limit_bytes=MIB),
        cost_estimate=pl.CostEstimate(flops=work, bytes_accessed=0, transcendentals=0),
    )(*chunks)


def new_pass(chunk, news, count, size):
    group = 3
    groups = chunk * size // (group * BLK)
    tiles = -(-count * size // BLK)
    return (chunk, news, groups, group, False, tuple(range(groups * group, tiles)))


def late_pass(chunk, news, low, high, size):
    return (chunk, news, 0, 1, True, tuple(range(low * size // BLK, -(-high * size // BLK))))


def finish_kernel(size, order_ref, own_ref, other_ref, clusters_ref, best_ref, out_ref, acc):
    gram = lax.dot_general(own_ref[...], other_ref[...], NT, preferred_element_type=jnp.float32)
    left = as_column(clusters_ref, 14 * size, size)
    left = jnp.tile(left, (1, -(-size // LANES)))[:, :size]
    last = 15 * size
    values = jnp.where(left == clusters_ref[:, last : last + size], gram, jnp.float32(-1.0))
    acc[...] = jnp.full_like(acc, -1.0)
    acc[0:size, :] = jnp.broadcast_to(jnp.max(values, axis=1, keepdims=True), (size, LANES))
    for i in range(16):
        found = best_ref[:, i * size : (i + 1) * size]
        if i == 14:
            found = jnp.maximum(found, best_of_rows(acc[...], size))
        if i == 15:
            found = jnp.maximum(found, jnp.max(values, axis=0, keepdims=True))
        place = order_ref[i]
        source, half = place // 2, place % 2
        for rep in range(4):
            out_ref[source * 4 + rep, pl.ds(half, 1), :] = found


def finish(order, own, other, clusters, best):
    size = own.shape[0]
    padded = -(-size // LANES) * LANES
    return pl.pallas_call(
        functools.partial(finish_kernel, size),
        out_shape=jax.ShapeDtypeStruct((32, 2, size), jnp.float32),
        in_specs=[pl.BlockSpec(memory_space=pltpu.SMEM)]
        + [pl.BlockSpec(memory_space=pltpu.VMEM)] * 4,
        out_specs=pl.BlockSpec(memory_space=pltpu.VMEM),
        scratch_shapes=[pltpu.VMEM((padded, LANES), jnp.float32)],
        compiler_params=pltpu.CompilerParams(vmem_limit_bytes=16 * MIB),
    )(order, own, other, clusters, best)


def settle_kernel(sources, size, high, index_ref, values_ref, out_ref, left_ref, right_ref):
    wide = left_ref.shape[1] // len(sources)
    left_ref[...] = jnp.zeros_like(left_ref)
    right_ref[...] = jnp.zeros_like(right_ref)
    rows = lax.broadcasted_iota(jnp.int32, (high, size), 0)
    lanes = lax.broadcasted_iota(jnp.int32, (LANES, size), 0)
    for g, places in enumerate(sources):
        index = index_ref[g // 2, g % 2 : g % 2 + 1, :] if index_ref.ndim == 3 else index_ref[g : g + 1, :]
        value = values_ref[places[0][0], places[0][1] : places[0][1] + 1, :]
        for a, b in places[1:]:
            value = jnp.maximum(value, values_ref[a, b : b + 1, :])
        span = slice(g * wide, g * wide + size)
        here = rows == index // LANES
        for piece in range(3):
            head = value.astype(jnp.bfloat16).astype(jnp.float32)
            value = value - head
            left_ref[piece * high : (piece + 1) * high, span] = jnp.where(here, head, 0.0).astype(
                jnp.bfloat16
            )
        right_ref[:, span] = jnp.where(lanes == index % LANES, 1.0, 0.0).astype(jnp.bfloat16)
    total = lax.dot_general(left_ref[...], right_ref[...], NT, preferred_element_type=jnp.float32)
    total = total[2 * high : 3 * high] + total[high : 2 * high] + total[:high]
    out_ref[...] = total[: out_ref.shape[0]]


def settle(index, values, sources, documents):
    size = index.shape[-1]
    high = -(-documents // (16 * LANES)) * 16
    wide = -(-size // LANES) * LANES * len(sources)
    out = pl.pallas_call(
        functools.partial(settle_kernel, sources, size, high),
        out_shape=jax.ShapeDtypeStruct((documents // LANES, LANES), jnp.float32),
        scratch_shapes=[
            pltpu.VMEM((3 * high, wide), jnp.bfloat16),
            pltpu.VMEM((LANES, wide), jnp.bfloat16),
        ],
        compiler_params=pltpu.CompilerParams(vmem_limit_bytes=16 * MIB),
    )(index, values)
    return out.reshape(-1)


def hosted(embeddings, send_index, place_index, slot_cluster):
    documents = embeddings.shape[0]
    size = send_index.shape[0] // 16
    axes = ("shard", "rep")
    named = arrival_names(place_index, slot_cluster)
    embeddings = tie(embeddings, named)
    (early,) = gather_rows(embeddings, send_index, (0,), size)
    named = lax.ppermute(named, axes, metadata_pairs())
    early = tie(early, named)
    index = send_index.reshape(8, 2, size)

    def go(step, chunk):
        return lax.ppermute(chunk, axes, round_pairs(step - 1))

    def swap(chunk):
        return lax.ppermute(chunk, axes, SIBLINGS)

    own, other = [None] * 8, [None] * 8
    own[1], own[2] = go(1, early), go(2, early)
    late = gather_rows(tie(embeddings, early), send_index, (1, 2, 3, 4), size)
    own[0], other[0] = late[2:]
    own[3], own[4] = go(3, late[0]), go(4, late[0])
    own[1], own[2] = tie(own[1], late[0]), tie(own[2], late[0])
    own[5] = go(5, tie(late[1], own[1]))
    own[6] = go(6, tie(late[1], own[2]))

    named, table = tie(named, late[0]), tie(jnp.asarray(chunk_order()), late[0])
    order = table[lax.axis_index("shard"), lax.axis_index("rep")]
    flat = named.reshape(16, size)[order].reshape(1, 16 * size)

    def score(best, count, passes, after=()):
        arrays, loads = [], []
        for r, side in CHUNKS[:count]:
            chunk = (own, other)[side][r]
            array, place = chunk if isinstance(chunk, tuple) else (chunk, 0)
            if not any(array is known for known in arrays):
                arrays.append(array)
            loads.append(([array is known for known in arrays].index(True), place))
        return gram_best(arrays, tuple(loads), size, flat, best, passes, after)

    best = jnp.full((1, 16 * size), -1.0, jnp.float32)
    best = score(best, 4, (new_pass(1, 3, 4, size),), (order, index))
    other[1] = swap(tie(own[1], best))
    joined = join([own[2], tie(own[3], best), tie(own[4], best)], SHORT)
    swapped = swap(joined)
    own[3], own[4] = (joined, 1), (joined, 2)
    best = score(best, 7, (new_pass(4, 2, 7, size), late_pass(2, 2, 6, 7, size)))
    own[7] = go(7, tie(late[2], best))
    other[2], other[3], other[4] = (swapped, 0), (swapped, 1), (swapped, 2)
    joined = join([tie(own[5], best), tie(own[6], best)], LONG)
    swapped = swap(joined)
    own[5], own[6] = (joined, 0), (joined, 1)
    best = score(best, 12, (new_pass(10, 2, 12, size), late_pass(3, 3, 7, 10, size)))
    other[5], other[6] = (swapped, 0), (swapped, 1)
    own[7] = tie(own[7], best)
    other[7] = swap(own[7])
    best = score(best, 15, (new_pass(14, 1, 15, size), late_pass(10, 2, 12, 14, size)))
    outbound = finish(order, own[7], other[7], flat, best)
    returned = lax.all_to_all(outbound, axes, split_axis=0, concat_axis=0, tiled=True)
    sources = []
    for owner in range(8):
        host, y = host_of(owner)
        for half in range(2):
            sources.append(tuple((host * 4 + y * 2 + core, half) for core in range(2)))
    return settle(index, returned, tuple(sources), documents)


def gathered(embeddings, send_index, place_index, slot_cluster):
    documents, width = embeddings.shape
    owners = lax.axis_size("shard")
    reps = lax.axis_size("rep")
    share = send_index.shape[0] // owners
    outgoing = normalize(embeddings.at[send_index].get(mode="promise_in_bounds"))
    arrived = lax.all_to_all(
        outgoing.reshape(owners, share, width), "shard", split_axis=0, concat_axis=0, tiled=True
    )
    parts = 16
    size = documents // parts
    news = parts // reps
    turn = lax.axis_index("rep") * news
    arrived = jnp.roll(arrived.reshape(parts, size, width), -turn, axis=0)
    clusters = arrival_names(place_index, slot_cluster).reshape(parts, size)
    clusters = jnp.roll(clusters, -turn, axis=0)
    best = jnp.full((1, documents), -1.0, jnp.float32)
    tiles = tuple(range(documents // BLK))
    passes = ((0, news, 0, 1, True, tiles),)
    chunks = [arrived[i] for i in range(parts)]
    loads = tuple((i, 0) for i in range(parts))
    best = gram_best(chunks, loads, size, clusters.reshape(1, -1), best, passes)
    best = lax.all_gather(best[0, : news * size], "rep", axis=0, tiled=True)
    returned = lax.all_to_all(
        best.reshape(owners, share), "shard", split_axis=0, concat_axis=0, tiled=True
    )
    sources = tuple(((0, g),) for g in range(parts))
    return settle(send_index.reshape(parts, size), returned.reshape(1, parts, size), sources, documents)


def solution(mesh):
    planned = mesh.shape["shard"] == 8 and mesh.shape["rep"] == 4

    def shards(embeddings, send_index, place_index, slot_cluster, pair_list):
        del pair_list
        run = hosted if planned else gathered
        return run(embeddings, send_index, place_index, slot_cluster)

    return jax.shard_map(
        shards,
        mesh=mesh,
        in_specs=(P("shard", None), P("shard"), P("shard"), P("shard"), P(("shard", "rep"), None)),
        out_specs=P("shard"),
        check_vma=False,
    )
```

```python
import functools

import jax
import jax.numpy as jnp
import numpy as np
from jax import lax
from jax.experimental import pallas as pl
from jax.experimental.pallas import tpu as pltpu
from jax.sharding import PartitionSpec as P

BLK = 256
LANES = 128
NT = (((1,), (1,)), ((), ()))
MIB = 1024 * 1024
LONG = 40_000_000_000
SHORT = 2_000_000_000

HOSTS = (2, 3, 4, 5)
ROUNDS = ((2, 6, 3, 7, 4, 1, 5), (3, 7, 2, 6, 4, 1, 5))


CHUNKS = (
    (0, 1), (0, 0), (1, 0), (2, 0),
    (3, 0), (4, 0), (1, 1),
    (2, 1), (3, 1), (4, 1), (5, 0), (6, 0),
    (5, 1), (6, 1), (7, 0), (7, 1),
)


def host_of(owner):
    z, x = owner // 2, owner % 2
    return (1 if z < 2 else 2) * 2 + x, z % 2


def chunk_order():
    order = np.zeros((8, 4, 16), np.int32)
    for s in range(8):
        for rep in range(4):
            for i, (step, side) in enumerate(CHUNKS):
                half = rep % 2 ^ side
                order[s, rep, i] = (s ^ ((0,) + ROUNDS[half])[step]) * 2 + half
    return order


def round_pairs(step):
    pairs = []
    for rep in range(4):
        for host in HOSTS:
            pairs.append(((host ^ ROUNDS[rep % 2][step]) * 4 + rep, host * 4 + rep))
    return pairs


SIBLINGS = [(host * 4 + rep, host * 4 + (rep ^ 1)) for host in HOSTS for rep in range(4)]


def metadata_pairs():
    pairs = []
    for owner in range(8):
        host, y = host_of(owner)
        for core in range(2):
            pairs.append((owner * 4 + y * 2 + core, host * 4 + y * 2 + core))
    return pairs


def tie(value, *after):
    return lax.optimization_barrier((value, *after))[0]


def normalize(rows):
    wide = rows.astype(jnp.float32)
    return (wide * lax.rsqrt(jnp.sum(wide * wide, axis=1, keepdims=True) + 1e-06)).astype(
        jnp.bfloat16
    )


def names_kernel(place_ref, slots_ref, out_ref):
    block = place_ref[...] // BLK
    found = jnp.zeros_like(block)
    for i in range(slots_ref.shape[0] * LANES // BLK):
        row = i * BLK // LANES
        found = jnp.where(block == i, slots_ref[row : row + 1, 0:1], found)
    out_ref[...] = found


def arrival_names(place_index, slot_cluster):
    places = place_index.reshape(-1, LANES)
    return pl.pallas_call(
        names_kernel, out_shape=jax.ShapeDtypeStruct(places.shape, jnp.int32)
    )(places, slot_cluster.reshape(-1, LANES))


def chunk_start(slot, size):
    s, rep = lax.axis_index("shard"), lax.axis_index("rep")
    y, core = rep // 2, rep % 2
    inner = (s >= HOSTS[0]) & (s <= HOSTS[-1])
    turn = min(slot, 3)
    steps = [(order[2 * turn], (order + (0,))[2 * turn + 1]) for order in ROUNDS]
    outer_step = jnp.where(core == 0, steps[0][0], steps[1][0])
    inner_step = jnp.where(core == 0, steps[0][1], steps[1][1])
    target = s ^ jnp.where(inner, inner_step, outer_step)
    owner = (2 * (target // 2 - 1) + y) * 2 + target % 2
    half = 1 - core if slot == 4 else core
    return owner * (2 * size) + half * size


def gather_kernel(slots, size, group, sections, *refs):
    index_hbm, rows_ref = refs[:2]
    index_ref, raw, wide, picked, sems = refs[-5:]
    outs = refs[-5 - len(slots) : -5]
    listed = pltpu.make_async_copy(index_hbm, index_ref, sems.at[sections])
    listed.start()
    width = raw.shape[1]
    tiles = width // LANES
    part = raw.shape[0] // sections
    copies = []
    for i in range(sections):
        rows = pl.ds(i * part, part)
        copies.append(pltpu.make_async_copy(rows_ref.at[rows], raw.at[rows], sems.at[i]))
        copies[-1].start()
    step = 160
    for i in range(sections):
        copies[i].wait()

        def widen(j, _, i=i):
            first = i * part + j * step
            rows = raw[pl.ds(pl.multiple_of(first, step), step), :].astype(jnp.float32)
            for t in range(tiles):
                wide[pl.ds(first * tiles + t, step, stride=tiles), :] = rows[:, t * LANES : (t + 1) * LANES]
            return 0

        lax.fori_loop(0, part // step, widen, 0)
    listed.wait()
    for c, slot in enumerate(slots):
        base = chunk_start(slot, size)

        def pick(j, _, c=c, base=base):
            for t in range(group):
                source = pl.multiple_of(index_ref[base + j * group + t] * tiles, tiles)
                picked[t * tiles : (t + 1) * tiles, :] = wide[pl.ds(source, tiles), :]
            for first in range(0, group, 16):
                rows = jnp.concatenate(
                    [picked[pl.ds(first * tiles + t, 16, stride=tiles), :] for t in range(tiles)],
                    axis=1,
                )
                scale = lax.rsqrt(jnp.sum(rows * rows, axis=1, keepdims=True) + 1e-06)
                outs[c][pl.ds(pl.multiple_of(j * group + first, 16), 16), :] = (rows * scale).astype(
                    jnp.bfloat16
                )
            return 0

        lax.fori_loop(0, size // group, pick, 0)


def gather_rows(embeddings, index, slots, size):
    documents, width = embeddings.shape
    count = len(slots)
    sections = 10
    group = 80
    return pl.pallas_call(
        functools.partial(gather_kernel, slots, size, group, sections),
        out_shape=[jax.ShapeDtypeStruct((size, width), jnp.bfloat16)] * count,
        in_specs=[pl.BlockSpec(memory_space=pltpu.HBM)] * 2,
        out_specs=[pl.BlockSpec(memory_space=pltpu.VMEM)] * count,
        scratch_shapes=[
            pltpu.SMEM(index.shape, jnp.int32),
            pltpu.VMEM((documents, width), jnp.bfloat16),
            pltpu.VMEM((documents * width // LANES, LANES), jnp.float32),
            pltpu.VMEM((group * width // LANES, LANES), jnp.float32),
            pltpu.SemaphoreType.DMA((sections + 1,)),
        ],
        compiler_params=pltpu.CompilerParams(vmem_limit_bytes=45 * MIB),
        cost_estimate=pl.CostEstimate(flops=LONG, bytes_accessed=0, transcendentals=0),
    )(index, embeddings)


def best_of_rows(acc, size):
    return jnp.max(jnp.transpose(acc), axis=0, keepdims=True)[:, :size]


def as_column(row_ref, start, size):
    wide = -(-size // LANES) * LANES
    row = row_ref[:, start : start + wide]
    return jnp.transpose(jnp.broadcast_to(row, (LANES, wide)))[:size]


def gram_kernel(passes, loads, size, limit, *refs):
    cluster_row, before_ref, best_ref, held, acc, sems = refs[-6:]
    count = len(loads)
    first = range(passes[0][0], passes[0][0] + passes[0][1])

    def source(i):
        array, place = loads[i]
        return refs[array].at[pl.ds(place * size, size)]

    def copy(i):
        return pltpu.make_async_copy(source(i), held.at[pl.ds(i * size, size)], sems.at[i])

    def arrive(i):
        rows = held.at[pl.ds(0, size)]
        pltpu.make_async_copy(rows, rows, sems.at[i]).wait()

    for i in first:
        copy(i).start()
    for i in range(count):
        if i not in first:
            copy(i).start()
    best_ref[...] = before_ref[...]
    for i in first:
        copy(i).wait()
    for n, (chunk, news, groups, group, meets, last) in enumerate(passes):
        height = news * size
        acc[...] = jnp.full_like(acc, -1.0)
        rows = held[chunk * size : chunk * size + height, :]
        left = as_column(cluster_row, chunk * size, height)
        left = jnp.concatenate([left, left], axis=1)

        def tile(start, special, chunk=chunk, height=height, rows=rows, left=left):
            gram = lax.dot_general(
                rows, held[pl.ds(start, BLK), :], NT, preferred_element_type=jnp.float32
            )
            counts = left == cluster_row[:, pl.ds(start, BLK)]
            if special:
                column = start + lax.broadcasted_iota(jnp.int32, (height, BLK), 1)
                row = chunk * size + lax.broadcasted_iota(jnp.int32, (height, BLK), 0)
                counts = counts & (column != row) & (column < limit)
            values = jnp.where(counts, gram, jnp.float32(-1.0))
            top = jnp.max(values, axis=0, keepdims=True)
            best_ref[:, pl.ds(start, BLK)] = jnp.maximum(best_ref[:, pl.ds(start, BLK)], top)
            acc[0:height, :] = jnp.maximum(
                acc[0:height, :], jnp.maximum(values[:, :LANES], values[:, LANES:])
            )

        def visit(u, _, n=n, group=group, meets=meets, tile=tile):
            if n == 0:
                for i in (2 * u, 2 * u + 1):

                    @pl.when(i < first[0])
                    def _(i=i):
                        arrive(i)

            for t in range(group):
                tile(pl.multiple_of((u * group + t) * BLK, BLK), meets)
            return 0

        lax.fori_loop(0, groups, visit, 0)
        if n == 0:
            for i in range(count):
                if i not in first and not i < min(2 * groups, first[0]):
                    arrive(i)
        for t in last:
            start, stop = t * BLK, (t + 1) * BLK
            meets = start < chunk * size + height and stop > chunk * size
            tile(start, meets or stop > limit)
        span = slice(chunk * size, chunk * size + height)
        best_ref[:, span] = jnp.maximum(best_ref[:, span], best_of_rows(acc[...], height))


def gram_best(arrays, loads, size, cluster_row, before, passes, after=()):
    width = arrays[0].shape[1]
    limit = len(loads) * size
    held = -(-limit // BLK) * BLK
    tall = max(news for _, news, *_ in passes) * size
    padded = -(-tall // LANES) * LANES
    return pl.pallas_call(
        functools.partial(gram_kernel, passes, loads, size, limit),
        out_shape=jax.ShapeDtypeStruct(before.shape, jnp.float32),
        in_specs=[pl.BlockSpec(memory_space=pl.ANY)] * (len(arrays) + len(after))
        + [pl.BlockSpec(memory_space=pltpu.VMEM)] * 2,
        out_specs=pl.BlockSpec(memory_space=pltpu.VMEM),
        scratch_shapes=[
            pltpu.VMEM((held, width), jnp.bfloat16),
            pltpu.VMEM((padded, LANES), jnp.float32),
            pltpu.SemaphoreType.DMA((len(loads),)),
        ],
        compiler_params=pltpu.CompilerParams(vmem_limit_bytes=24 * MIB),
        cost_estimate=pl.CostEstimate(flops=0, bytes_accessed=0, transcendentals=0),
    )(*arrays, *after, cluster_row, before)


def join_kernel(size, *refs):
    out_ref, sems = refs[-2:]
    copies = [
        pltpu.make_async_copy(ref, out_ref.at[pl.ds(i * size, size)], sems.at[i])
        for i, ref in enumerate(refs[:-2])
    ]
    for copy in copies:
        copy.start()
    for copy in copies:
        copy.wait()


def join(chunks, work):
    size, width = chunks[0].shape
    return pl.pallas_call(
        functools.partial(join_kernel, size),
        out_shape=jax.ShapeDtypeStruct((len(chunks) * size, width), chunks[0].dtype),
        in_specs=[pl.BlockSpec(memory_space=pl.ANY)] * len(chunks),
        out_specs=pl.BlockSpec(memory_space=pl.ANY),
        scratch_shapes=[pltpu.SemaphoreType.DMA((len(chunks),))],
        compiler_params=pltpu.CompilerParams(vmem_limit_bytes=MIB),
        cost_estimate=pl.CostEstimate(flops=work, bytes_accessed=0, transcendentals=0),
    )(*chunks)


def new_pass(chunk, news, count, size):
    group = 3
    groups = chunk * size // (group * BLK)
    tiles = -(-count * size // BLK)
    return (chunk, news, groups, group, False, tuple(range(groups * group, tiles)))


def late_pass(chunk, news, low, high, size):
    return (chunk, news, 0, 1, True, tuple(range(low * size // BLK, -(-high * size // BLK))))


def finish_kernel(size, order_ref, own_ref, other_ref, clusters_ref, best_ref, out_ref, acc):
    gram = lax.dot_general(own_ref[...], other_ref[...], NT, preferred_element_type=jnp.float32)
    left = as_column(clusters_ref, 14 * size, size)
    left = jnp.tile(left, (1, -(-size // LANES)))[:, :size]
    last = 15 * size
    values = jnp.where(left == clusters_ref[:, last : last + size], gram, jnp.float32(-1.0))
    acc[...] = jnp.full_like(acc, -1.0)
    acc[0:size, :] = jnp.broadcast_to(jnp.max(values, axis=1, keepdims=True), (size, LANES))
    for i in range(16):
        found = best_ref[:, i * size : (i + 1) * size]
        if i == 14:
            found = jnp.maximum(found, best_of_rows(acc[...], size))
        if i == 15:
            found = jnp.maximum(found, jnp.max(values, axis=0, keepdims=True))
        place = order_ref[i]
        source, half = place // 2, place % 2
        for rep in range(4):
            out_ref[source * 4 + rep, pl.ds(half, 1), :] = found


def finish(order, own, other, clusters, best):
    size = own.shape[0]
    padded = -(-size // LANES) * LANES
    return pl.pallas_call(
        functools.partial(finish_kernel, size),
        out_shape=jax.ShapeDtypeStruct((32, 2, size), jnp.float32),
        in_specs=[pl.BlockSpec(memory_space=pltpu.SMEM)]
        + [pl.BlockSpec(memory_space=pltpu.VMEM)] * 4,
        out_specs=pl.BlockSpec(memory_space=pltpu.VMEM),
        scratch_shapes=[pltpu.VMEM((padded, LANES), jnp.float32)],
        compiler_params=pltpu.CompilerParams(vmem_limit_bytes=16 * MIB),
    )(order, own, other, clusters, best)


def settle_kernel(sources, size, high, index_ref, values_ref, out_ref, left_ref, right_ref):
    wide = left_ref.shape[1] // len(sources)
    left_ref[...] = jnp.zeros_like(left_ref)
    right_ref[...] = jnp.zeros_like(right_ref)
    rows = lax.broadcasted_iota(jnp.int32, (high, size), 0)
    lanes = lax.broadcasted_iota(jnp.int32, (LANES, size), 0)
    for g, places in enumerate(sources):
        index = index_ref[g // 2, g % 2 : g % 2 + 1, :] if index_ref.ndim == 3 else index_ref[g : g + 1, :]
        value = values_ref[places[0][0], places[0][1] : places[0][1] + 1, :]
        for a, b in places[1:]:
            value = jnp.maximum(value, values_ref[a, b : b + 1, :])
        span = slice(g * wide, g * wide + size)
        here = rows == index // LANES
        for piece in range(3):
            head = value.astype(jnp.bfloat16).astype(jnp.float32)
            value = value - head
            left_ref[piece * high : (piece + 1) * high, span] = jnp.where(here, head, 0.0).astype(
                jnp.bfloat16
            )
        right_ref[:, span] = jnp.where(lanes == index % LANES, 1.0, 0.0).astype(jnp.bfloat16)
    total = lax.dot_general(left_ref[...], right_ref[...], NT, preferred_element_type=jnp.float32)
    total = total[2 * high : 3 * high] + total[high : 2 * high] + total[:high]
    out_ref[...] = total[: out_ref.shape[0]]


def settle(index, values, sources, documents):
    size = index.shape[-1]
    high = -(-documents // (16 * LANES)) * 16
    wide = -(-size // LANES) * LANES * len(sources)
    out = pl.pallas_call(
        functools.partial(settle_kernel, sources, size, high),
        out_shape=jax.ShapeDtypeStruct((documents // LANES, LANES), jnp.float32),
        scratch_shapes=[
            pltpu.VMEM((3 * high, wide), jnp.bfloat16),
            pltpu.VMEM((LANES, wide), jnp.bfloat16),
        ],
        compiler_params=pltpu.CompilerParams(vmem_limit_bytes=16 * MIB),
    )(index, values)
    return out.reshape(-1)


def hosted(embeddings, send_index, place_index, slot_cluster):
    documents = embeddings.shape[0]
    size = send_index.shape[0] // 16
    axes = ("shard", "rep")
    (early,) = gather_rows(embeddings, send_index, (0,), size)
    named = arrival_names(tie(place_index, early), slot_cluster)
    named = lax.ppermute(named, axes, metadata_pairs())
    index = send_index.reshape(8, 2, size)

    def go(step, chunk):
        return lax.ppermute(chunk, axes, round_pairs(step - 1))

    def swap(chunk):
        return lax.ppermute(chunk, axes, SIBLINGS)

    own, other = [None] * 8, [None] * 8
    own[1], own[2] = go(1, early), go(2, early)
    late = gather_rows(tie(embeddings, early), send_index, (1, 2, 3, 4), size)
    own[0], other[0] = late[2:]
    own[3], own[4] = go(3, late[0]), go(4, tie(late[0], named))
    own[1], own[2] = tie(own[1], late[0]), tie(own[2], late[0])
    own[5] = go(5, tie(late[1], own[1]))
    own[6] = go(6, tie(late[1], own[2]))

    named, table = tie(named, late[0]), tie(jnp.asarray(chunk_order()), late[0])
    order = table[lax.axis_index("shard"), lax.axis_index("rep")]
    flat = named.reshape(16, size)[order].reshape(1, 16 * size)

    def score(best, count, passes, after=()):
        arrays, loads = [], []
        for r, side in CHUNKS[:count]:
            chunk = (own, other)[side][r]
            array, place = chunk if isinstance(chunk, tuple) else (chunk, 0)
            if not any(array is known for known in arrays):
                arrays.append(array)
            loads.append(([array is known for known in arrays].index(True), place))
        return gram_best(arrays, tuple(loads), size, flat, best, passes, after)

    best = jnp.full((1, 16 * size), -1.0, jnp.float32)
    best = score(best, 4, (new_pass(1, 3, 4, size),), (order, index))
    other[1] = swap(tie(own[1], best))
    joined = join([own[2], tie(own[3], best), tie(own[4], best)], SHORT)
    own[7] = go(7, tie(late[2], own[3]))
    swapped = swap(joined)
    own[3], own[4] = (joined, 1), (joined, 2)
    best = score(best, 7, (new_pass(4, 2, 7, size), late_pass(2, 2, 6, 7, size)))
    other[2], other[3], other[4] = (swapped, 0), (swapped, 1), (swapped, 2)
    joined = join([tie(own[5], best), tie(own[6], best)], LONG)
    swapped = swap(joined)
    own[5], own[6] = (joined, 0), (joined, 1)
    best = score(best, 12, (new_pass(10, 2, 12, size), late_pass(3, 3, 7, 10, size)))
    other[5], other[6] = (swapped, 0), (swapped, 1)
    own[7] = tie(own[7], best)
    other[7] = swap(own[7])
    best = score(best, 15, (new_pass(14, 1, 15, size), late_pass(10, 2, 12, 14, size)))
    outbound = finish(order, own[7], other[7], flat, best)
    returned = lax.all_to_all(outbound, axes, split_axis=0, concat_axis=0, tiled=True)
    sources = []
    for owner in range(8):
        host, y = host_of(owner)
        for half in range(2):
            sources.append(tuple((host * 4 + y * 2 + core, half) for core in range(2)))
    return settle(index, returned, tuple(sources), documents)


def gathered(embeddings, send_index, place_index, slot_cluster):
    documents, width = embeddings.shape
    owners = lax.axis_size("shard")
    reps = lax.axis_size("rep")
    share = send_index.shape[0] // owners
    outgoing = normalize(embeddings.at[send_index].get(mode="promise_in_bounds"))
    arrived = lax.all_to_all(
        outgoing.reshape(owners, share, width), "shard", split_axis=0, concat_axis=0, tiled=True
    )
    parts = 16
    size = documents // parts
    news = parts // reps
    turn = lax.axis_index("rep") * news
    arrived = jnp.roll(arrived.reshape(parts, size, width), -turn, axis=0)
    clusters = arrival_names(place_index, slot_cluster).reshape(parts, size)
    clusters = jnp.roll(clusters, -turn, axis=0)
    best = jnp.full((1, documents), -1.0, jnp.float32)
    tiles = tuple(range(documents // BLK))
    passes = ((0, news, 0, 1, True, tiles),)
    chunks = [arrived[i] for i in range(parts)]
    loads = tuple((i, 0) for i in range(parts))
    best = gram_best(chunks, loads, size, clusters.reshape(1, -1), best, passes)
    best = lax.all_gather(best[0, : news * size], "rep", axis=0, tiled=True)
    returned = lax.all_to_all(
        best.reshape(owners, share), "shard", split_axis=0, concat_axis=0, tiled=True
    )
    sources = tuple(((0, g),) for g in range(parts))
    return settle(send_index.reshape(parts, size), returned.reshape(1, parts, size), sources, documents)


def solution(mesh):
    planned = mesh.shape["shard"] == 8 and mesh.shape["rep"] == 4

    def shards(embeddings, send_index, place_index, slot_cluster, pair_list):
        del pair_list
        run = hosted if planned else gathered
        return run(embeddings, send_index, place_index, slot_cluster)

    return jax.shard_map(
        shards,
        mesh=mesh,
        in_specs=(P("shard", None), P("shard"), P("shard"), P("shard"), P(("shard", "rep"), None)),
        out_specs=P("shard"),
        check_vma=False,
    )
```

```python
import functools

import jax
import jax.numpy as jnp
import numpy as np
from jax import lax
from jax.experimental import pallas as pl
from jax.experimental.pallas import tpu as pltpu
from jax.sharding import PartitionSpec as P

BLK = 256
LANES = 128
NT = (((1,), (1,)), ((), ()))
MIB = 1024 * 1024
LONG = 40_000_000_000
SHORT = 2_000_000_000

HOSTS = (2, 3, 4, 5)
ROUNDS = ((2, 6, 3, 7, 4, 1, 5), (3, 7, 2, 6, 4, 1, 5))


CHUNKS = (
    (0, 1), (0, 0), (1, 0), (2, 0),
    (3, 0), (4, 0), (1, 1),
    (2, 1), (3, 1), (4, 1), (5, 0), (6, 0),
    (5, 1), (6, 1), (7, 0), (7, 1),
)


def host_of(owner):
    z, x = owner // 2, owner % 2
    return (1 if z < 2 else 2) * 2 + x, z % 2


def chunk_order():
    order = np.zeros((8, 4, 16), np.int32)
    for s in range(8):
        for rep in range(4):
            for i, (step, side) in enumerate(CHUNKS):
                half = rep % 2 ^ side
                order[s, rep, i] = (s ^ ((0,) + ROUNDS[half])[step]) * 2 + half
    return order


def round_pairs(step):
    pairs = []
    for rep in range(4):
        for host in HOSTS:
            pairs.append(((host ^ ROUNDS[rep % 2][step]) * 4 + rep, host * 4 + rep))
    return pairs


SIBLINGS = [(host * 4 + rep, host * 4 + (rep ^ 1)) for host in HOSTS for rep in range(4)]


def metadata_pairs():
    pairs = []
    for owner in range(8):
        host, y = host_of(owner)
        for core in range(2):
            pairs.append((owner * 4 + y * 2 + core, host * 4 + y * 2 + core))
    return pairs


def tie(value, *after):
    return lax.optimization_barrier((value, *after))[0]


def normalize(rows):
    wide = rows.astype(jnp.float32)
    return (wide * lax.rsqrt(jnp.sum(wide * wide, axis=1, keepdims=True) + 1e-06)).astype(
        jnp.bfloat16
    )


def names_kernel(place_ref, slots_ref, out_ref):
    block = place_ref[...] // BLK
    found = jnp.zeros_like(block)
    for i in range(slots_ref.shape[0] * LANES // BLK):
        row = i * BLK // LANES
        found = jnp.where(block == i, slots_ref[row : row + 1, 0:1], found)
    out_ref[...] = found


def arrival_names(place_index, slot_cluster):
    places = place_index.reshape(-1, LANES)
    return pl.pallas_call(
        names_kernel, out_shape=jax.ShapeDtypeStruct(places.shape, jnp.int32)
    )(places, slot_cluster.reshape(-1, LANES))


def chunk_start(slot, size):
    s, rep = lax.axis_index("shard"), lax.axis_index("rep")
    y, core = rep // 2, rep % 2
    inner = (s >= HOSTS[0]) & (s <= HOSTS[-1])
    turn = min(slot, 3)
    steps = [(order[2 * turn], (order + (0,))[2 * turn + 1]) for order in ROUNDS]
    outer_step = jnp.where(core == 0, steps[0][0], steps[1][0])
    inner_step = jnp.where(core == 0, steps[0][1], steps[1][1])
    target = s ^ jnp.where(inner, inner_step, outer_step)
    owner = (2 * (target // 2 - 1) + y) * 2 + target % 2
    half = 1 - core if slot == 4 else core
    return owner * (2 * size) + half * size


def gather_kernel(slots, size, group, sections, *refs):
    index_hbm, rows_ref = refs[:2]
    index_ref, raw, wide, picked, sems = refs[-5:]
    outs = refs[-5 - len(slots) : -5]
    listed = pltpu.make_async_copy(index_hbm, index_ref, sems.at[sections])
    listed.start()
    width = raw.shape[1]
    tiles = width // LANES
    part = raw.shape[0] // sections
    copies = []
    for i in range(sections):
        rows = pl.ds(i * part, part)
        copies.append(pltpu.make_async_copy(rows_ref.at[rows], raw.at[rows], sems.at[i]))
        copies[-1].start()
    step = 160
    for i in range(sections):
        copies[i].wait()

        def widen(j, _, i=i):
            first = i * part + j * step
            rows = raw[pl.ds(pl.multiple_of(first, step), step), :].astype(jnp.float32)
            for t in range(tiles):
                wide[pl.ds(first * tiles + t, step, stride=tiles), :] = rows[:, t * LANES : (t + 1) * LANES]
            return 0

        lax.fori_loop(0, part // step, widen, 0)
    listed.wait()
    for c, slot in enumerate(slots):
        base = chunk_start(slot, size)

        def pick(j, _, c=c, base=base):
            for t in range(group):
                source = pl.multiple_of(index_ref[base + j * group + t] * tiles, tiles)
                picked[t * tiles : (t + 1) * tiles, :] = wide[pl.ds(source, tiles), :]
            for first in range(0, group, 16):
                rows = jnp.concatenate(
                    [picked[pl.ds(first * tiles + t, 16, stride=tiles), :] for t in range(tiles)],
                    axis=1,
                )
                scale = lax.rsqrt(jnp.sum(rows * rows, axis=1, keepdims=True) + 1e-06)
                outs[c][pl.ds(pl.multiple_of(j * group + first, 16), 16), :] = (rows * scale).astype(
                    jnp.bfloat16
                )
            return 0

        lax.fori_loop(0, size // group, pick, 0)


def gather_rows(embeddings, index, slots, size):
    documents, width = embeddings.shape
    count = len(slots)
    sections = 10
    group = 80
    return pl.pallas_call(
        functools.partial(gather_kernel, slots, size, group, sections),
        out_shape=[jax.ShapeDtypeStruct((size, width), jnp.bfloat16)] * count,
        in_specs=[pl.BlockSpec(memory_space=pltpu.HBM)] * 2,
        out_specs=[pl.BlockSpec(memory_space=pltpu.VMEM)] * count,
        scratch_shapes=[
            pltpu.SMEM(index.shape, jnp.int32),
            pltpu.VMEM((documents, width), jnp.bfloat16),
            pltpu.VMEM((documents * width // LANES, LANES), jnp.float32),
            pltpu.VMEM((group * width // LANES, LANES), jnp.float32),
            pltpu.SemaphoreType.DMA((sections + 1,)),
        ],
        compiler_params=pltpu.CompilerParams(vmem_limit_bytes=45 * MIB),
        cost_estimate=pl.CostEstimate(flops=LONG, bytes_accessed=0, transcendentals=0),
    )(index, embeddings)


def best_of_rows(acc, size):
    return jnp.max(jnp.transpose(acc), axis=0, keepdims=True)[:, :size]


def as_column(row_ref, start, size):
    wide = -(-size // LANES) * LANES
    row = row_ref[:, start : start + wide]
    return jnp.transpose(jnp.broadcast_to(row, (LANES, wide)))[:size]


def gram_kernel(passes, loads, size, limit, *refs):
    cluster_row, before_ref, best_ref, held, acc, sems = refs[-6:]
    count = len(loads)
    first = range(passes[0][0], passes[0][0] + passes[0][1])

    def source(i):
        array, place = loads[i]
        return refs[array].at[pl.ds(place * size, size)]

    def copy(i):
        return pltpu.make_async_copy(source(i), held.at[pl.ds(i * size, size)], sems.at[i])

    def arrive(i):
        rows = held.at[pl.ds(0, size)]
        pltpu.make_async_copy(rows, rows, sems.at[i]).wait()

    for i in first:
        copy(i).start()
    for i in range(count):
        if i not in first:
            copy(i).start()
    best_ref[...] = before_ref[...]
    for i in first:
        copy(i).wait()
    for n, (chunk, news, groups, group, meets, last) in enumerate(passes):
        height = news * size
        acc[...] = jnp.full_like(acc, -1.0)
        rows = held[chunk * size : chunk * size + height, :]
        left = as_column(cluster_row, chunk * size, height)
        left = jnp.concatenate([left, left], axis=1)

        def tile(start, special, chunk=chunk, height=height, rows=rows, left=left):
            gram = lax.dot_general(
                rows, held[pl.ds(start, BLK), :], NT, preferred_element_type=jnp.float32
            )
            counts = left == cluster_row[:, pl.ds(start, BLK)]
            if special:
                column = start + lax.broadcasted_iota(jnp.int32, (height, BLK), 1)
                row = chunk * size + lax.broadcasted_iota(jnp.int32, (height, BLK), 0)
                counts = counts & (column != row) & (column < limit)
            values = jnp.where(counts, gram, jnp.float32(-1.0))
            top = jnp.max(values, axis=0, keepdims=True)
            best_ref[:, pl.ds(start, BLK)] = jnp.maximum(best_ref[:, pl.ds(start, BLK)], top)
            acc[0:height, :] = jnp.maximum(
                acc[0:height, :], jnp.maximum(values[:, :LANES], values[:, LANES:])
            )

        def visit(u, _, n=n, group=group, meets=meets, tile=tile):
            if n == 0:
                for i in (2 * u, 2 * u + 1):

                    @pl.when(i < first[0])
                    def _(i=i):
                        arrive(i)

            for t in range(group):
                tile(pl.multiple_of((u * group + t) * BLK, BLK), meets)
            return 0

        lax.fori_loop(0, groups, visit, 0)
        if n == 0:
            for i in range(count):
                if i not in first and not i < min(2 * groups, first[0]):
                    arrive(i)
        for t in last:
            start, stop = t * BLK, (t + 1) * BLK
            meets = start < chunk * size + height and stop > chunk * size
            tile(start, meets or stop > limit)
        span = slice(chunk * size, chunk * size + height)
        best_ref[:, span] = jnp.maximum(best_ref[:, span], best_of_rows(acc[...], height))


def gram_best(arrays, loads, size, cluster_row, before, passes, after=()):
    width = arrays[0].shape[1]
    limit = len(loads) * size
    held = -(-limit // BLK) * BLK
    tall = max(news for _, news, *_ in passes) * size
    padded = -(-tall // LANES) * LANES
    return pl.pallas_call(
        functools.partial(gram_kernel, passes, loads, size, limit),
        out_shape=jax.ShapeDtypeStruct(before.shape, jnp.float32),
        in_specs=[pl.BlockSpec(memory_space=pl.ANY)] * (len(arrays) + len(after))
        + [pl.BlockSpec(memory_space=pltpu.VMEM)] * 2,
        out_specs=pl.BlockSpec(memory_space=pltpu.VMEM),
        scratch_shapes=[
            pltpu.VMEM((held, width), jnp.bfloat16),
            pltpu.VMEM((padded, LANES), jnp.float32),
            pltpu.SemaphoreType.DMA((len(loads),)),
        ],
        compiler_params=pltpu.CompilerParams(vmem_limit_bytes=24 * MIB),
        cost_estimate=pl.CostEstimate(flops=0, bytes_accessed=0, transcendentals=0),
    )(*arrays, *after, cluster_row, before)


def join_kernel(size, *refs):
    out_ref, sems = refs[-2:]
    copies = [
        pltpu.make_async_copy(ref, out_ref.at[pl.ds(i * size, size)], sems.at[i])
        for i, ref in enumerate(refs[:-2])
    ]
    for copy in copies:
        copy.start()
    for copy in copies:
        copy.wait()


def join(chunks, work):
    size, width = chunks[0].shape
    return pl.pallas_call(
        functools.partial(join_kernel, size),
        out_shape=jax.ShapeDtypeStruct((len(chunks) * size, width), chunks[0].dtype),
        in_specs=[pl.BlockSpec(memory_space=pl.ANY)] * len(chunks),
        out_specs=pl.BlockSpec(memory_space=pl.ANY),
        scratch_shapes=[pltpu.SemaphoreType.DMA((len(chunks),))],
        compiler_params=pltpu.CompilerParams(vmem_limit_bytes=MIB),
        cost_estimate=pl.CostEstimate(flops=work, bytes_accessed=0, transcendentals=0),
    )(*chunks)


def new_pass(chunk, news, count, size):
    group = 3
    groups = chunk * size // (group * BLK)
    tiles = -(-count * size // BLK)
    return (chunk, news, groups, group, False, tuple(range(groups * group, tiles)))


def late_pass(chunk, news, low, high, size):
    return (chunk, news, 0, 1, True, tuple(range(low * size // BLK, -(-high * size // BLK))))


def finish_kernel(size, order_ref, own_ref, other_ref, clusters_ref, best_ref, out_ref, acc):
    gram = lax.dot_general(own_ref[...], other_ref[...], NT, preferred_element_type=jnp.float32)
    left = as_column(clusters_ref, 14 * size, size)
    left = jnp.tile(left, (1, -(-size // LANES)))[:, :size]
    last = 15 * size
    values = jnp.where(left == clusters_ref[:, last : last + size], gram, jnp.float32(-1.0))
    acc[...] = jnp.full_like(acc, -1.0)
    acc[0:size, :] = jnp.broadcast_to(jnp.max(values, axis=1, keepdims=True), (size, LANES))
    for i in range(16):
        found = best_ref[:, i * size : (i + 1) * size]
        if i == 14:
            found = jnp.maximum(found, best_of_rows(acc[...], size))
        if i == 15:
            found = jnp.maximum(found, jnp.max(values, axis=0, keepdims=True))
        place = order_ref[i]
        source, half = place // 2, place % 2
        for rep in range(4):
            out_ref[source * 4 + rep, pl.ds(half, 1), :] = found


def finish(order, own, other, clusters, best):
    size = own.shape[0]
    padded = -(-size // LANES) * LANES
    return pl.pallas_call(
        functools.partial(finish_kernel, size),
        out_shape=jax.ShapeDtypeStruct((32, 2, size), jnp.float32),
        in_specs=[pl.BlockSpec(memory_space=pltpu.SMEM)]
        + [pl.BlockSpec(memory_space=pltpu.VMEM)] * 4,
        out_specs=pl.BlockSpec(memory_space=pltpu.VMEM),
        scratch_shapes=[pltpu.VMEM((padded, LANES), jnp.float32)],
        compiler_params=pltpu.CompilerParams(vmem_limit_bytes=16 * MIB),
    )(order, own, other, clusters, best)


def settle_kernel(sources, size, high, index_ref, values_ref, out_ref, left_ref, right_ref):
    wide = left_ref.shape[1] // len(sources)
    left_ref[...] = jnp.zeros_like(left_ref)
    right_ref[...] = jnp.zeros_like(right_ref)
    rows = lax.broadcasted_iota(jnp.int32, (high, size), 0)
    lanes = lax.broadcasted_iota(jnp.int32, (LANES, size), 0)
    for g, places in enumerate(sources):
        index = index_ref[g // 2, g % 2 : g % 2 + 1, :] if index_ref.ndim == 3 else index_ref[g : g + 1, :]
        value = values_ref[places[0][0], places[0][1] : places[0][1] + 1, :]
        for a, b in places[1:]:
            value = jnp.maximum(value, values_ref[a, b : b + 1, :])
        span = slice(g * wide, g * wide + size)
        here = rows == index // LANES
        for piece in range(3):
            head = value.astype(jnp.bfloat16).astype(jnp.float32)
            value = value - head
            left_ref[piece * high : (piece + 1) * high, span] = jnp.where(here, head, 0.0).astype(
                jnp.bfloat16
            )
        right_ref[:, span] = jnp.where(lanes == index % LANES, 1.0, 0.0).astype(jnp.bfloat16)
    total = lax.dot_general(left_ref[...], right_ref[...], NT, preferred_element_type=jnp.float32)
    total = total[2 * high : 3 * high] + total[high : 2 * high] + total[:high]
    out_ref[...] = total[: out_ref.shape[0]]


def settle(index, values, sources, documents):
    size = index.shape[-1]
    high = -(-documents // (16 * LANES)) * 16
    wide = -(-size // LANES) * LANES * len(sources)
    out = pl.pallas_call(
        functools.partial(settle_kernel, sources, size, high),
        out_shape=jax.ShapeDtypeStruct((documents // LANES, LANES), jnp.float32),
        scratch_shapes=[
            pltpu.VMEM((3 * high, wide), jnp.bfloat16),
            pltpu.VMEM((LANES, wide), jnp.bfloat16),
        ],
        compiler_params=pltpu.CompilerParams(vmem_limit_bytes=16 * MIB),
    )(index, values)
    return out.reshape(-1)


def hosted(embeddings, send_index, place_index, slot_cluster):
    documents = embeddings.shape[0]
    size = send_index.shape[0] // 16
    axes = ("shard", "rep")
    named = arrival_names(place_index, slot_cluster)
    embeddings = tie(embeddings, named)
    (early,) = gather_rows(embeddings, send_index, (0,), size)
    named = lax.ppermute(named, axes, metadata_pairs())
    early = tie(early, named)
    index = send_index.reshape(8, 2, size)

    def go(step, chunk):
        return lax.ppermute(chunk, axes, round_pairs(step - 1))

    def swap(chunk):
        return lax.ppermute(chunk, axes, SIBLINGS)

    own, other = [None] * 8, [None] * 8
    own[1], own[2] = go(1, early), go(2, early)
    late = gather_rows(tie(embeddings, early), send_index, (1, 2, 3, 4), size)
    own[0], other[0] = late[2:]
    own[3], own[4] = go(3, late[0]), go(4, late[0])
    own[1], own[2] = tie(own[1], late[0]), tie(own[2], late[0])
    own[5] = go(5, tie(late[1], own[4]))
    own[6] = go(6, tie(late[1], own[2]))

    named, table = tie(named, late[0]), tie(jnp.asarray(chunk_order()), late[0])
    order = table[lax.axis_index("shard"), lax.axis_index("rep")]
    flat = named.reshape(16, size)[order].reshape(1, 16 * size)

    def score(best, count, passes, after=()):
        arrays, loads = [], []
        for r, side in CHUNKS[:count]:
            chunk = (own, other)[side][r]
            array, place = chunk if isinstance(chunk, tuple) else (chunk, 0)
            if not any(array is known for known in arrays):
                arrays.append(array)
            loads.append(([array is known for known in arrays].index(True), place))
        return gram_best(arrays, tuple(loads), size, flat, best, passes, after)

    best = jnp.full((1, 16 * size), -1.0, jnp.float32)
    best = score(best, 4, (new_pass(1, 3, 4, size),), (order, index))
    other[1] = swap(tie(own[1], best))
    joined = join([own[2], tie(own[3], best), tie(own[4], best)], SHORT)
    own[7] = go(7, tie(late[2], own[3]))
    swapped = swap(joined)
    own[3], own[4] = (joined, 1), (joined, 2)
    best = score(best, 7, (new_pass(4, 2, 7, size), late_pass(2, 2, 6, 7, size)))
    other[2], other[3], other[4] = (swapped, 0), (swapped, 1), (swapped, 2)
    joined = join([tie(own[5], best), tie(own[6], best)], LONG)
    swapped = swap(joined)
    own[5], own[6] = (joined, 0), (joined, 1)
    best = score(best, 12, (new_pass(10, 2, 12, size), late_pass(3, 3, 7, 10, size)))
    other[5], other[6] = (swapped, 0), (swapped, 1)
    own[7] = tie(own[7], best)
    other[7] = swap(own[7])
    best = score(best, 15, (new_pass(14, 1, 15, size), late_pass(10, 2, 12, 14, size)))
    outbound = finish(order, own[7], other[7], flat, best)
    returned = lax.all_to_all(outbound, axes, split_axis=0, concat_axis=0, tiled=True)
    sources = []
    for owner in range(8):
        host, y = host_of(owner)
        for half in range(2):
            sources.append(tuple((host * 4 + y * 2 + core, half) for core in range(2)))
    return settle(index, returned, tuple(sources), documents)


def gathered(embeddings, send_index, place_index, slot_cluster):
    documents, width = embeddings.shape
    owners = lax.axis_size("shard")
    reps = lax.axis_size("rep")
    share = send_index.shape[0] // owners
    outgoing = normalize(embeddings.at[send_index].get(mode="promise_in_bounds"))
    arrived = lax.all_to_all(
        outgoing.reshape(owners, share, width), "shard", split_axis=0, concat_axis=0, tiled=True
    )
    parts = 16
    size = documents // parts
    news = parts // reps
    turn = lax.axis_index("rep") * news
    arrived = jnp.roll(arrived.reshape(parts, size, width), -turn, axis=0)
    clusters = arrival_names(place_index, slot_cluster).reshape(parts, size)
    clusters = jnp.roll(clusters, -turn, axis=0)
    best = jnp.full((1, documents), -1.0, jnp.float32)
    tiles = tuple(range(documents // BLK))
    passes = ((0, news, 0, 1, True, tiles),)
    chunks = [arrived[i] for i in range(parts)]
    loads = tuple((i, 0) for i in range(parts))
    best = gram_best(chunks, loads, size, clusters.reshape(1, -1), best, passes)
    best = lax.all_gather(best[0, : news * size], "rep", axis=0, tiled=True)
    returned = lax.all_to_all(
        best.reshape(owners, share), "shard", split_axis=0, concat_axis=0, tiled=True
    )
    sources = tuple(((0, g),) for g in range(parts))
    return settle(send_index.reshape(parts, size), returned.reshape(1, parts, size), sources, documents)


def solution(mesh):
    planned = mesh.shape["shard"] == 8 and mesh.shape["rep"] == 4

    def shards(embeddings, send_index, place_index, slot_cluster, pair_list):
        del pair_list
        run = hosted if planned else gathered
        return run(embeddings, send_index, place_index, slot_cluster)

    return jax.shard_map(
        shards,
        mesh=mesh,
        in_specs=(P("shard", None), P("shard"), P("shard"), P("shard"), P(("shard", "rep"), None)),
        out_specs=P("shard"),
        check_vma=False,
    )
```

```python
import functools

import jax
import jax.numpy as jnp
import numpy as np
from jax import lax
from jax.experimental import pallas as pl
from jax.experimental.pallas import tpu as pltpu
from jax.sharding import PartitionSpec as P

BLK = 256
LANES = 128
NT = (((1,), (1,)), ((), ()))
MIB = 1024 * 1024
LONG = 40_000_000_000
SHORT = 2_000_000_000

HOSTS = (2, 3, 4, 5)
ROUNDS = ((2, 6, 3, 7, 4, 1, 5), (3, 7, 2, 6, 4, 1, 5))


CHUNKS = (
    (0, 1), (0, 0), (1, 0), (2, 0),
    (3, 0), (4, 0), (1, 1),
    (2, 1), (3, 1), (4, 1), (5, 0), (6, 0),
    (5, 1), (6, 1), (7, 0), (7, 1),
)


def host_of(owner):
    z, x = owner // 2, owner % 2
    return (1 if z < 2 else 2) * 2 + x, z % 2


def chunk_order():
    order = np.zeros((8, 4, 16), np.int32)
    for s in range(8):
        for rep in range(4):
            for i, (step, side) in enumerate(CHUNKS):
                half = rep % 2 ^ side
                order[s, rep, i] = (s ^ ((0,) + ROUNDS[half])[step]) * 2 + half
    return order


def round_pairs(step):
    pairs = []
    for rep in range(4):
        for host in HOSTS:
            pairs.append(((host ^ ROUNDS[rep % 2][step]) * 4 + rep, host * 4 + rep))
    return pairs


SIBLINGS = [(host * 4 + rep, host * 4 + (rep ^ 1)) for host in HOSTS for rep in range(4)]


def metadata_pairs():
    pairs = []
    for owner in range(8):
        host, y = host_of(owner)
        for core in range(2):
            pairs.append((owner * 4 + y * 2 + core, host * 4 + y * 2 + core))
    return pairs


def tie(value, *after):
    return lax.optimization_barrier((value, *after))[0]


def normalize(rows):
    wide = rows.astype(jnp.float32)
    return (wide * lax.rsqrt(jnp.sum(wide * wide, axis=1, keepdims=True) + 1e-06)).astype(
        jnp.bfloat16
    )


def names_kernel(place_ref, slots_ref, out_ref):
    block = place_ref[...] // BLK
    found = jnp.zeros_like(block)
    for i in range(slots_ref.shape[0] * LANES // BLK):
        row = i * BLK // LANES
        found = jnp.where(block == i, slots_ref[row : row + 1, 0:1], found)
    out_ref[...] = found


def arrival_names(place_index, slot_cluster):
    places = place_index.reshape(-1, LANES)
    return pl.pallas_call(
        names_kernel, out_shape=jax.ShapeDtypeStruct(places.shape, jnp.int32)
    )(places, slot_cluster.reshape(-1, LANES))


def chunk_start(slot, size):
    s, rep = lax.axis_index("shard"), lax.axis_index("rep")
    y, core = rep // 2, rep % 2
    inner = (s >= HOSTS[0]) & (s <= HOSTS[-1])
    turn = min(slot, 3)
    steps = [(order[2 * turn], (order + (0,))[2 * turn + 1]) for order in ROUNDS]
    outer_step = jnp.where(core == 0, steps[0][0], steps[1][0])
    inner_step = jnp.where(core == 0, steps[0][1], steps[1][1])
    target = s ^ jnp.where(inner, inner_step, outer_step)
    owner = (2 * (target // 2 - 1) + y) * 2 + target % 2
    half = 1 - core if slot == 4 else core
    return owner * (2 * size) + half * size


def gather_kernel(slots, size, group, sections, *refs):
    index_hbm, rows_ref = refs[:2]
    index_ref, raw, wide, picked, sems = refs[-5:]
    outs = refs[-5 - len(slots) : -5]
    listed = pltpu.make_async_copy(index_hbm, index_ref, sems.at[sections])
    listed.start()
    width = raw.shape[1]
    tiles = width // LANES
    part = raw.shape[0] // sections

    def load(i):
        rows = pl.ds(pl.multiple_of(i * part, part), part)
        return pltpu.make_async_copy(rows_ref.at[rows], raw.at[rows], sems.at[i])

    for i in range(sections):
        load(i).start()

    def widen(i, _):
        load(i).wait()
        first = pl.multiple_of(i * part, part)
        rows = raw[pl.ds(first, part), :].astype(jnp.float32)
        for t in range(tiles):
            wide[pl.ds(first * tiles + t, part, stride=tiles), :] = rows[:, t * LANES : (t + 1) * LANES]
        return 0

    lax.fori_loop(0, sections, widen, 0)
    listed.wait()
    for c, slot in enumerate(slots):
        base = chunk_start(slot, size)

        def pick(j, _, c=c, base=base):
            for t in range(group):
                source = pl.multiple_of(index_ref[base + j * group + t] * tiles, tiles)
                picked[t * tiles : (t + 1) * tiles, :] = wide[pl.ds(source, tiles), :]
            for first in range(0, group, 16):
                rows = jnp.concatenate(
                    [picked[pl.ds(first * tiles + t, 16, stride=tiles), :] for t in range(tiles)],
                    axis=1,
                )
                scale = lax.rsqrt(jnp.sum(rows * rows, axis=1, keepdims=True) + 1e-06)
                outs[c][pl.ds(pl.multiple_of(j * group + first, 16), 16), :] = (rows * scale).astype(
                    jnp.bfloat16
                )
            return 0

        lax.fori_loop(0, size // group, pick, 0)


def gather_rows(embeddings, index, slots, size):
    documents, width = embeddings.shape
    count = len(slots)
    sections = 20
    group = 80
    return pl.pallas_call(
        functools.partial(gather_kernel, slots, size, group, sections),
        out_shape=[jax.ShapeDtypeStruct((size, width), jnp.bfloat16)] * count,
        in_specs=[pl.BlockSpec(memory_space=pltpu.HBM)] * 2,
        out_specs=[pl.BlockSpec(memory_space=pltpu.VMEM)] * count,
        scratch_shapes=[
            pltpu.SMEM(index.shape, jnp.int32),
            pltpu.VMEM((documents, width), jnp.bfloat16),
            pltpu.VMEM((documents * width // LANES, LANES), jnp.float32),
            pltpu.VMEM((group * width // LANES, LANES), jnp.float32),
            pltpu.SemaphoreType.DMA((sections + 1,)),
        ],
        compiler_params=pltpu.CompilerParams(vmem_limit_bytes=45 * MIB),
        cost_estimate=pl.CostEstimate(flops=LONG, bytes_accessed=0, transcendentals=0),
    )(index, embeddings)


def best_of_rows(acc, size):
    return jnp.max(jnp.transpose(acc), axis=0, keepdims=True)[:, :size]


def as_column(row_ref, start, size):
    wide = -(-size // LANES) * LANES
    row = row_ref[:, start : start + wide]
    return jnp.transpose(jnp.broadcast_to(row, (LANES, wide)))[:size]


def gram_kernel(passes, loads, size, limit, *refs):
    cluster_row, before_ref, best_ref, held, acc, sems = refs[-6:]
    count = len(loads)
    first = range(passes[0][0], passes[0][0] + passes[0][1])

    def source(i):
        array, place = loads[i]
        return refs[array].at[pl.ds(place * size, size)]

    def copy(i):
        return pltpu.make_async_copy(source(i), held.at[pl.ds(i * size, size)], sems.at[i])

    def arrive(i):
        rows = held.at[pl.ds(0, size)]
        pltpu.make_async_copy(rows, rows, sems.at[i]).wait()

    for i in first:
        copy(i).start()
    for i in range(count):
        if i not in first:
            copy(i).start()
    best_ref[...] = before_ref[...]
    for i in first:
        copy(i).wait()
    for n, (chunk, news, groups, group, meets, last) in enumerate(passes):
        height = news * size
        acc[...] = jnp.full_like(acc, -1.0)
        rows = held[chunk * size : chunk * size + height, :]
        left = as_column(cluster_row, chunk * size, height)
        left = jnp.concatenate([left, left], axis=1)

        def tile(start, special, chunk=chunk, height=height, rows=rows, left=left):
            gram = lax.dot_general(
                rows, held[pl.ds(start, BLK), :], NT, preferred_element_type=jnp.float32
            )
            counts = left == cluster_row[:, pl.ds(start, BLK)]
            if special:
                column = start + lax.broadcasted_iota(jnp.int32, (height, BLK), 1)
                row = chunk * size + lax.broadcasted_iota(jnp.int32, (height, BLK), 0)
                counts = counts & (column != row) & (column < limit)
            values = jnp.where(counts, gram, jnp.float32(-1.0))
            top = jnp.max(values, axis=0, keepdims=True)
            best_ref[:, pl.ds(start, BLK)] = jnp.maximum(best_ref[:, pl.ds(start, BLK)], top)
            acc[0:height, :] = jnp.maximum(
                acc[0:height, :], jnp.maximum(values[:, :LANES], values[:, LANES:])
            )

        def visit(u, _, n=n, group=group, meets=meets, tile=tile):
            if n == 0:
                for i in (2 * u, 2 * u + 1):

                    @pl.when(i < first[0])
                    def _(i=i):
                        arrive(i)

            for t in range(group):
                tile(pl.multiple_of((u * group + t) * BLK, BLK), meets)
            return 0

        lax.fori_loop(0, groups, visit, 0)
        if n == 0:
            for i in range(count):
                if i not in first and not i < min(2 * groups, first[0]):
                    arrive(i)
        for t in last:
            start, stop = t * BLK, (t + 1) * BLK
            meets = start < chunk * size + height and stop > chunk * size
            tile(start, meets or stop > limit)
        span = slice(chunk * size, chunk * size + height)
        best_ref[:, span] = jnp.maximum(best_ref[:, span], best_of_rows(acc[...], height))


def gram_best(arrays, loads, size, cluster_row, before, passes, after=()):
    width = arrays[0].shape[1]
    limit = len(loads) * size
    held = -(-limit // BLK) * BLK
    tall = max(news for _, news, *_ in passes) * size
    padded = -(-tall // LANES) * LANES
    return pl.pallas_call(
        functools.partial(gram_kernel, passes, loads, size, limit),
        out_shape=jax.ShapeDtypeStruct(before.shape, jnp.float32),
        in_specs=[pl.BlockSpec(memory_space=pl.ANY)] * (len(arrays) + len(after))
        + [pl.BlockSpec(memory_space=pltpu.VMEM)] * 2,
        out_specs=pl.BlockSpec(memory_space=pltpu.VMEM),
        scratch_shapes=[
            pltpu.VMEM((held, width), jnp.bfloat16),
            pltpu.VMEM((padded, LANES), jnp.float32),
            pltpu.SemaphoreType.DMA((len(loads),)),
        ],
        compiler_params=pltpu.CompilerParams(vmem_limit_bytes=24 * MIB),
        cost_estimate=pl.CostEstimate(flops=0, bytes_accessed=0, transcendentals=0),
    )(*arrays, *after, cluster_row, before)


def join_kernel(size, *refs):
    out_ref, sems = refs[-2:]
    copies = [
        pltpu.make_async_copy(ref, out_ref.at[pl.ds(i * size, size)], sems.at[i])
        for i, ref in enumerate(refs[:-2])
    ]
    for copy in copies:
        copy.start()
    for copy in copies:
        copy.wait()


def join(chunks, work):
    size, width = chunks[0].shape
    return pl.pallas_call(
        functools.partial(join_kernel, size),
        out_shape=jax.ShapeDtypeStruct((len(chunks) * size, width), chunks[0].dtype),
        in_specs=[pl.BlockSpec(memory_space=pl.ANY)] * len(chunks),
        out_specs=pl.BlockSpec(memory_space=pl.ANY),
        scratch_shapes=[pltpu.SemaphoreType.DMA((len(chunks),))],
        compiler_params=pltpu.CompilerParams(vmem_limit_bytes=MIB),
        cost_estimate=pl.CostEstimate(flops=work, bytes_accessed=0, transcendentals=0),
    )(*chunks)


def new_pass(chunk, news, count, size):
    group = 3
    groups = chunk * size // (group * BLK)
    tiles = -(-count * size // BLK)
    return (chunk, news, groups, group, False, tuple(range(groups * group, tiles)))


def late_pass(chunk, news, low, high, size):
    return (chunk, news, 0, 1, True, tuple(range(low * size // BLK, -(-high * size // BLK))))


def finish_kernel(size, order_ref, own_ref, other_ref, clusters_ref, best_ref, out_ref, acc):
    gram = lax.dot_general(own_ref[...], other_ref[...], NT, preferred_element_type=jnp.float32)
    left = as_column(clusters_ref, 14 * size, size)
    left = jnp.tile(left, (1, -(-size // LANES)))[:, :size]
    last = 15 * size
    values = jnp.where(left == clusters_ref[:, last : last + size], gram, jnp.float32(-1.0))
    acc[...] = jnp.full_like(acc, -1.0)
    acc[0:size, :] = jnp.broadcast_to(jnp.max(values, axis=1, keepdims=True), (size, LANES))
    for i in range(16):
        found = best_ref[:, i * size : (i + 1) * size]
        if i == 14:
            found = jnp.maximum(found, best_of_rows(acc[...], size))
        if i == 15:
            found = jnp.maximum(found, jnp.max(values, axis=0, keepdims=True))
        place = order_ref[i]
        source, half = place // 2, place % 2
        for rep in range(4):
            out_ref[source * 4 + rep, pl.ds(half, 1), :] = found


def finish(order, own, other, clusters, best):
    size = own.shape[0]
    padded = -(-size // LANES) * LANES
    return pl.pallas_call(
        functools.partial(finish_kernel, size),
        out_shape=jax.ShapeDtypeStruct((32, 2, size), jnp.float32),
        in_specs=[pl.BlockSpec(memory_space=pltpu.SMEM)]
        + [pl.BlockSpec(memory_space=pltpu.VMEM)] * 4,
        out_specs=pl.BlockSpec(memory_space=pltpu.VMEM),
        scratch_shapes=[pltpu.VMEM((padded, LANES), jnp.float32)],
        compiler_params=pltpu.CompilerParams(vmem_limit_bytes=16 * MIB),
    )(order, own, other, clusters, best)


def settle_kernel(sources, size, high, index_ref, values_ref, out_ref, left_ref, right_ref):
    wide = left_ref.shape[1] // len(sources)
    left_ref[...] = jnp.zeros_like(left_ref)
    right_ref[...] = jnp.zeros_like(right_ref)
    rows = lax.broadcasted_iota(jnp.int32, (high, size), 0)
    lanes = lax.broadcasted_iota(jnp.int32, (LANES, size), 0)
    for g, places in enumerate(sources):
        index = index_ref[g // 2, g % 2 : g % 2 + 1, :] if index_ref.ndim == 3 else index_ref[g : g + 1, :]
        value = values_ref[places[0][0], places[0][1] : places[0][1] + 1, :]
        for a, b in places[1:]:
            value = jnp.maximum(value, values_ref[a, b : b + 1, :])
        span = slice(g * wide, g * wide + size)
        here = rows == index // LANES
        for piece in range(3):
            head = value.astype(jnp.bfloat16).astype(jnp.float32)
            value = value - head
            left_ref[piece * high : (piece + 1) * high, span] = jnp.where(here, head, 0.0).astype(
                jnp.bfloat16
            )
        right_ref[:, span] = jnp.where(lanes == index % LANES, 1.0, 0.0).astype(jnp.bfloat16)
    total = lax.dot_general(left_ref[...], right_ref[...], NT, preferred_element_type=jnp.float32)
    total = total[2 * high : 3 * high] + total[high : 2 * high] + total[:high]
    out_ref[...] = total[: out_ref.shape[0]]


def settle(index, values, sources, documents):
    size = index.shape[-1]
    high = -(-documents // (16 * LANES)) * 16
    wide = -(-size // LANES) * LANES * len(sources)
    out = pl.pallas_call(
        functools.partial(settle_kernel, sources, size, high),
        out_shape=jax.ShapeDtypeStruct((documents // LANES, LANES), jnp.float32),
        scratch_shapes=[
            pltpu.VMEM((3 * high, wide), jnp.bfloat16),
            pltpu.VMEM((LANES, wide), jnp.bfloat16),
        ],
        compiler_params=pltpu.CompilerParams(vmem_limit_bytes=16 * MIB),
    )(index, values)
    return out.reshape(-1)


def hosted(embeddings, send_index, place_index, slot_cluster):
    documents = embeddings.shape[0]
    size = send_index.shape[0] // 16
    axes = ("shard", "rep")
    named = arrival_names(place_index, slot_cluster)
    embeddings = tie(embeddings, named)
    (early,) = gather_rows(embeddings, send_index, (0,), size)
    named = lax.ppermute(named, axes, metadata_pairs())
    early = tie(early, named)
    index = send_index.reshape(8, 2, size)

    def go(step, chunk):
        return lax.ppermute(chunk, axes, round_pairs(step - 1))

    def swap(chunk):
        return lax.ppermute(chunk, axes, SIBLINGS)

    own, other = [None] * 8, [None] * 8
    own[1], own[2] = go(1, early), go(2, early)
    late = gather_rows(tie(embeddings, early), send_index, (1, 2, 3, 4), size)
    own[0], other[0] = late[2:]
    own[3], own[4] = go(3, late[0]), go(4, late[0])
    own[1], own[2] = tie(own[1], late[0]), tie(own[2], late[0])
    own[5] = go(5, tie(late[1], own[1]))
    own[6] = go(6, tie(late[1], own[2]))

    named, table = tie(named, late[0]), tie(jnp.asarray(chunk_order()), late[0])
    order = table[lax.axis_index("shard"), lax.axis_index("rep")]
    flat = named.reshape(16, size)[order].reshape(1, 16 * size)

    def score(best, count, passes, after=()):
        arrays, loads = [], []
        for r, side in CHUNKS[:count]:
            chunk = (own, other)[side][r]
            array, place = chunk if isinstance(chunk, tuple) else (chunk, 0)
            if not any(array is known for known in arrays):
                arrays.append(array)
            loads.append(([array is known for known in arrays].index(True), place))
        return gram_best(arrays, tuple(loads), size, flat, best, passes, after)

    best = jnp.full((1, 16 * size), -1.0, jnp.float32)
    best = score(best, 4, (new_pass(1, 3, 4, size),), (order, index))
    other[1] = swap(tie(own[1], best))
    joined = join([own[2], tie(own[3], best), tie(own[4], best)], SHORT)
    own[7] = go(7, tie(late[2], own[3]))
    swapped = swap(joined)
    own[3], own[4] = (joined, 1), (joined, 2)
    best = score(best, 7, (new_pass(4, 2, 7, size), late_pass(2, 2, 6, 7, size)))
    other[2], other[3], other[4] = (swapped, 0), (swapped, 1), (swapped, 2)
    joined = join([tie(own[5], best), tie(own[6], best)], LONG)
    swapped = swap(joined)
    own[5], own[6] = (joined, 0), (joined, 1)
    best = score(best, 12, (new_pass(10, 2, 12, size), late_pass(3, 3, 7, 10, size)))
    other[5], other[6] = (swapped, 0), (swapped, 1)
    own[7] = tie(own[7], best)
    other[7] = swap(own[7])
    best = score(best, 15, (new_pass(14, 1, 15, size), late_pass(10, 2, 12, 14, size)))
    outbound = finish(order, own[7], other[7], flat, best)
    returned = lax.all_to_all(outbound, axes, split_axis=0, concat_axis=0, tiled=True)
    sources = []
    for owner in range(8):
        host, y = host_of(owner)
        for half in range(2):
            sources.append(tuple((host * 4 + y * 2 + core, half) for core in range(2)))
    return settle(index, returned, tuple(sources), documents)


def gathered(embeddings, send_index, place_index, slot_cluster):
    documents, width = embeddings.shape
    owners = lax.axis_size("shard")
    reps = lax.axis_size("rep")
    share = send_index.shape[0] // owners
    outgoing = normalize(embeddings.at[send_index].get(mode="promise_in_bounds"))
    arrived = lax.all_to_all(
        outgoing.reshape(owners, share, width), "shard", split_axis=0, concat_axis=0, tiled=True
    )
    parts = 16
    size = documents // parts
    news = parts // reps
    turn = lax.axis_index("rep") * news
    arrived = jnp.roll(arrived.reshape(parts, size, width), -turn, axis=0)
    clusters = arrival_names(place_index, slot_cluster).reshape(parts, size)
    clusters = jnp.roll(clusters, -turn, axis=0)
    best = jnp.full((1, documents), -1.0, jnp.float32)
    tiles = tuple(range(documents // BLK))
    passes = ((0, news, 0, 1, True, tiles),)
    chunks = [arrived[i] for i in range(parts)]
    loads = tuple((i, 0) for i in range(parts))
    best = gram_best(chunks, loads, size, clusters.reshape(1, -1), best, passes)
    best = lax.all_gather(best[0, : news * size], "rep", axis=0, tiled=True)
    returned = lax.all_to_all(
        best.reshape(owners, share), "shard", split_axis=0, concat_axis=0, tiled=True
    )
    sources = tuple(((0, g),) for g in range(parts))
    return settle(send_index.reshape(parts, size), returned.reshape(1, parts, size), sources, documents)


def solution(mesh):
    planned = mesh.shape["shard"] == 8 and mesh.shape["rep"] == 4

    def shards(embeddings, send_index, place_index, slot_cluster, pair_list):
        del pair_list
        run = hosted if planned else gathered
        return run(embeddings, send_index, place_index, slot_cluster)

    return jax.shard_map(
        shards,
        mesh=mesh,
        in_specs=(P("shard", None), P("shard"), P("shard"), P("shard"), P(("shard", "rep"), None)),
        out_specs=P("shard"),
        check_vma=False,
    )
```

```python
import functools

import jax
import jax.numpy as jnp
import numpy as np
from jax import lax
from jax.experimental import pallas as pl
from jax.experimental.pallas import tpu as pltpu
from jax.sharding import PartitionSpec as P

BLK = 256
LANES = 128
NT = (((1,), (1,)), ((), ()))
MIB = 1024 * 1024
LONG = 40_000_000_000
SHORT = 2_000_000_000

HOSTS = (2, 3, 4, 5)
ROUNDS = ((2, 6, 3, 7, 4, 1, 5), (3, 7, 2, 6, 4, 1, 5))


CHUNKS = (
    (0, 1), (0, 0), (1, 0), (2, 0),
    (3, 0), (4, 0), (1, 1),
    (2, 1), (3, 1), (4, 1), (5, 0), (6, 0),
    (5, 1), (6, 1), (7, 0), (7, 1),
)


def host_of(owner):
    z, x = owner // 2, owner % 2
    return (1 if z < 2 else 2) * 2 + x, z % 2


def chunk_order():
    order = np.zeros((8, 4, 16), np.int32)
    for s in range(8):
        for rep in range(4):
            for i, (step, side) in enumerate(CHUNKS):
                half = rep % 2 ^ side
                order[s, rep, i] = (s ^ ((0,) + ROUNDS[half])[step]) * 2 + half
    return order


def round_pairs(step):
    pairs = []
    for rep in range(4):
        for host in HOSTS:
            pairs.append(((host ^ ROUNDS[rep % 2][step]) * 4 + rep, host * 4 + rep))
    return pairs


SIBLINGS = [(host * 4 + rep, host * 4 + (rep ^ 1)) for host in HOSTS for rep in range(4)]


def metadata_pairs():
    pairs = []
    for owner in range(8):
        host, y = host_of(owner)
        for core in range(2):
            pairs.append((owner * 4 + y * 2 + core, host * 4 + y * 2 + core))
    return pairs


def tie(value, *after):
    return lax.optimization_barrier((value, *after))[0]


def normalize(rows):
    wide = rows.astype(jnp.float32)
    return (wide * lax.rsqrt(jnp.sum(wide * wide, axis=1, keepdims=True) + 1e-06)).astype(
        jnp.bfloat16
    )


def names_kernel(place_ref, slots_ref, out_ref):
    block = place_ref[...] // BLK
    found = jnp.zeros_like(block)
    for i in range(slots_ref.shape[0] * LANES // BLK):
        row = i * BLK // LANES
        found = jnp.where(block == i, slots_ref[row : row + 1, 0:1], found)
    out_ref[...] = found


def arrival_names(place_index, slot_cluster):
    places = place_index.reshape(-1, LANES)
    return pl.pallas_call(
        names_kernel, out_shape=jax.ShapeDtypeStruct(places.shape, jnp.int32)
    )(places, slot_cluster.reshape(-1, LANES))


def chunk_start(slot, size):
    s, rep = lax.axis_index("shard"), lax.axis_index("rep")
    y, core = rep // 2, rep % 2
    inner = (s >= HOSTS[0]) & (s <= HOSTS[-1])
    turn = min(slot, 3)
    steps = [(order[2 * turn], (order + (0,))[2 * turn + 1]) for order in ROUNDS]
    outer_step = jnp.where(core == 0, steps[0][0], steps[1][0])
    inner_step = jnp.where(core == 0, steps[0][1], steps[1][1])
    target = s ^ jnp.where(inner, inner_step, outer_step)
    owner = (2 * (target // 2 - 1) + y) * 2 + target % 2
    half = 1 - core if slot == 4 else core
    return owner * (2 * size) + half * size


def gather_kernel(slots, size, group, sections, *refs):
    index_hbm, rows_ref = refs[:2]
    index_ref, raw, wide, picked, sems = refs[-5:]
    outs = refs[-5 - len(slots) : -5]
    listed = pltpu.make_async_copy(index_hbm, index_ref, sems.at[sections])
    listed.start()
    width = raw.shape[1]
    tiles = width // LANES
    part = raw.shape[0] // sections
    copies = []
    for i in range(sections):
        rows = pl.ds(i * part, part)
        copies.append(pltpu.make_async_copy(rows_ref.at[rows], raw.at[rows], sems.at[i]))
        copies[-1].start()
    step = 160
    for i in range(sections):
        copies[i].wait()

        def widen(j, _, i=i):
            first = i * part + j * step
            rows = raw[pl.ds(pl.multiple_of(first, step), step), :].astype(jnp.float32)
            for t in range(tiles):
                wide[pl.ds(first * tiles + t, step, stride=tiles), :] = rows[:, t * LANES : (t + 1) * LANES]
            return 0

        lax.fori_loop(0, part // step, widen, 0)
    listed.wait()
    for c, slot in enumerate(slots):
        base = chunk_start(slot, size)

        def pick(j, _, c=c, base=base):
            for t in range(group):
                source = pl.multiple_of(index_ref[base + j * group + t] * tiles, tiles)
                picked[t * tiles : (t + 1) * tiles, :] = wide[pl.ds(source, tiles), :]
            for first in range(0, group, 16):
                rows = jnp.concatenate(
                    [picked[pl.ds(first * tiles + t, 16, stride=tiles), :] for t in range(tiles)],
                    axis=1,
                )
                scale = lax.rsqrt(jnp.sum(rows * rows, axis=1, keepdims=True) + 1e-06)
                outs[c][pl.ds(pl.multiple_of(j * group + first, 16), 16), :] = (rows * scale).astype(
                    jnp.bfloat16
                )
            return 0

        lax.fori_loop(0, size // group, pick, 0)


def gather_rows(embeddings, index, slots, size):
    documents, width = embeddings.shape
    count = len(slots)
    sections = 10
    group = 80
    return pl.pallas_call(
        functools.partial(gather_kernel, slots, size, group, sections),
        out_shape=[jax.ShapeDtypeStruct((size, width), jnp.bfloat16)] * count,
        in_specs=[pl.BlockSpec(memory_space=pltpu.HBM)] * 2,
        out_specs=[pl.BlockSpec(memory_space=pltpu.VMEM)] * count,
        scratch_shapes=[
            pltpu.SMEM(index.shape, jnp.int32),
            pltpu.VMEM((documents, width), jnp.bfloat16),
            pltpu.VMEM((documents * width // LANES, LANES), jnp.float32),
            pltpu.VMEM((group * width // LANES, LANES), jnp.float32),
            pltpu.SemaphoreType.DMA((sections + 1,)),
        ],
        compiler_params=pltpu.CompilerParams(vmem_limit_bytes=45 * MIB),
        cost_estimate=pl.CostEstimate(flops=LONG, bytes_accessed=0, transcendentals=0),
    )(index, embeddings)


def best_of_rows(acc, size):
    return jnp.max(jnp.transpose(acc), axis=0, keepdims=True)[:, :size]


def as_column(row_ref, start, size):
    wide = -(-size // LANES) * LANES
    row = row_ref[:, start : start + wide]
    return jnp.transpose(jnp.broadcast_to(row, (LANES, wide)))[:size]


def gram_kernel(passes, loads, size, limit, *refs):
    cluster_row, before_ref, best_ref, held, acc, sems = refs[-6:]
    count = len(loads)

    def source(i):
        array, place = loads[i]
        return refs[array].at[pl.ds(place * size, size)]

    def copy(i):
        return pltpu.make_async_copy(source(i), held.at[pl.ds(i * size, size)], sems.at[i])

    def arrive(i):
        rows = held.at[pl.ds(0, size)]
        pltpu.make_async_copy(rows, rows, sems.at[i]).wait()

    low = passes[0][5][0] * BLK // size
    for i in (*range(low, count), *range(low)):
        copy(i).start()
    best_ref[...] = before_ref[...]
    for i in range(low, count):
        copy(i).wait()
    for n, (chunk, news, groups, group, meets, last) in enumerate(passes):
        height = news * size
        acc[...] = jnp.full_like(acc, -1.0)
        rows = held[chunk * size : chunk * size + height, :]
        left = as_column(cluster_row, chunk * size, height)
        left = jnp.concatenate([left, left], axis=1)

        def tile(start, special, chunk=chunk, height=height, rows=rows, left=left):
            gram = lax.dot_general(
                rows, held[pl.ds(start, BLK), :], NT, preferred_element_type=jnp.float32
            )
            counts = left == cluster_row[:, pl.ds(start, BLK)]
            if special:
                column = start + lax.broadcasted_iota(jnp.int32, (height, BLK), 1)
                row = chunk * size + lax.broadcasted_iota(jnp.int32, (height, BLK), 0)
                counts = counts & (column != row) & (column < limit)
            values = jnp.where(counts, gram, jnp.float32(-1.0))
            top = jnp.max(values, axis=0, keepdims=True)
            best_ref[:, pl.ds(start, BLK)] = jnp.maximum(best_ref[:, pl.ds(start, BLK)], top)
            acc[0:height, :] = jnp.maximum(
                acc[0:height, :], jnp.maximum(values[:, :LANES], values[:, LANES:])
            )

        for t in last:
            start, stop = t * BLK, (t + 1) * BLK
            own = start < chunk * size + height and stop > chunk * size
            tile(start, own or stop > limit)
        step = -(-group * BLK // size)

        def visit(u, _, n=n, group=group, meets=meets, tile=tile, step=step):
            for i in range(step) if n == 0 else ():

                @pl.when(u * step + i < low)
                def _(i=i):
                    arrive(u * step + i)

            for t in range(group):
                tile(pl.multiple_of((u * group + t) * BLK, BLK), meets)
            return 0

        lax.fori_loop(0, groups, visit, 0)
        span = slice(chunk * size, chunk * size + height)
        best_ref[:, span] = jnp.maximum(best_ref[:, span], best_of_rows(acc[...], height))


def gram_best(arrays, loads, size, cluster_row, before, passes, after=()):
    width = arrays[0].shape[1]
    limit = len(loads) * size
    held = -(-limit // BLK) * BLK
    tall = max(news for _, news, *_ in passes) * size
    padded = -(-tall // LANES) * LANES
    return pl.pallas_call(
        functools.partial(gram_kernel, passes, loads, size, limit),
        out_shape=jax.ShapeDtypeStruct(before.shape, jnp.float32),
        in_specs=[pl.BlockSpec(memory_space=pl.ANY)] * (len(arrays) + len(after))
        + [pl.BlockSpec(memory_space=pltpu.VMEM)] * 2,
        out_specs=pl.BlockSpec(memory_space=pltpu.VMEM),
        scratch_shapes=[
            pltpu.VMEM((held, width), jnp.bfloat16),
            pltpu.VMEM((padded, LANES), jnp.float32),
            pltpu.SemaphoreType.DMA((len(loads),)),
        ],
        compiler_params=pltpu.CompilerParams(vmem_limit_bytes=24 * MIB),
        cost_estimate=pl.CostEstimate(flops=0, bytes_accessed=0, transcendentals=0),
    )(*arrays, *after, cluster_row, before)


def join_kernel(size, *refs):
    out_ref, sems = refs[-2:]
    copies = [
        pltpu.make_async_copy(ref, out_ref.at[pl.ds(i * size, size)], sems.at[i])
        for i, ref in enumerate(refs[:-2])
    ]
    for copy in copies:
        copy.start()
    for copy in copies:
        copy.wait()


def join(chunks, work):
    size, width = chunks[0].shape
    return pl.pallas_call(
        functools.partial(join_kernel, size),
        out_shape=jax.ShapeDtypeStruct((len(chunks) * size, width), chunks[0].dtype),
        in_specs=[pl.BlockSpec(memory_space=pl.ANY)] * len(chunks),
        out_specs=pl.BlockSpec(memory_space=pl.ANY),
        scratch_shapes=[pltpu.SemaphoreType.DMA((len(chunks),))],
        compiler_params=pltpu.CompilerParams(vmem_limit_bytes=MIB),
        cost_estimate=pl.CostEstimate(flops=work, bytes_accessed=0, transcendentals=0),
    )(*chunks)


def new_pass(chunk, news, count, size):
    plain = chunk * size // BLK
    group = max(n for n in range(1, 8) if plain % n == 0)
    groups = plain // group
    tiles = -(-count * size // BLK)
    return (chunk, news, groups, group, False, tuple(range(groups * group, tiles)))


def late_pass(chunk, news, low, high, size):
    return (chunk, news, 0, 1, True, tuple(range(low * size // BLK, -(-high * size // BLK))))


def finish_kernel(size, order_ref, own_ref, other_ref, clusters_ref, best_ref, out_ref, acc):
    gram = lax.dot_general(own_ref[...], other_ref[...], NT, preferred_element_type=jnp.float32)
    left = as_column(clusters_ref, 14 * size, size)
    left = jnp.tile(left, (1, -(-size // LANES)))[:, :size]
    last = 15 * size
    values = jnp.where(left == clusters_ref[:, last : last + size], gram, jnp.float32(-1.0))
    acc[...] = jnp.full_like(acc, -1.0)
    acc[0:size, :] = jnp.broadcast_to(jnp.max(values, axis=1, keepdims=True), (size, LANES))
    for i in range(16):
        found = best_ref[:, i * size : (i + 1) * size]
        if i == 14:
            found = jnp.maximum(found, best_of_rows(acc[...], size))
        if i == 15:
            found = jnp.maximum(found, jnp.max(values, axis=0, keepdims=True))
        place = order_ref[i]
        source, half = place // 2, place % 2
        for rep in range(4):
            out_ref[source * 4 + rep, pl.ds(half, 1), :] = found


def finish(order, own, other, clusters, best):
    size = own.shape[0]
    padded = -(-size // LANES) * LANES
    return pl.pallas_call(
        functools.partial(finish_kernel, size),
        out_shape=jax.ShapeDtypeStruct((32, 2, size), jnp.float32),
        in_specs=[pl.BlockSpec(memory_space=pltpu.SMEM)]
        + [pl.BlockSpec(memory_space=pltpu.VMEM)] * 4,
        out_specs=pl.BlockSpec(memory_space=pltpu.VMEM),
        scratch_shapes=[pltpu.VMEM((padded, LANES), jnp.float32)],
        compiler_params=pltpu.CompilerParams(vmem_limit_bytes=16 * MIB),
    )(order, own, other, clusters, best)


def settle_kernel(sources, size, high, index_ref, values_ref, out_ref, left_ref, right_ref):
    wide = left_ref.shape[1] // len(sources)
    left_ref[...] = jnp.zeros_like(left_ref)
    right_ref[...] = jnp.zeros_like(right_ref)
    rows = lax.broadcasted_iota(jnp.int32, (high, size), 0)
    lanes = lax.broadcasted_iota(jnp.int32, (LANES, size), 0)
    for g, places in enumerate(sources):
        index = index_ref[g // 2, g % 2 : g % 2 + 1, :] if index_ref.ndim == 3 else index_ref[g : g + 1, :]
        value = values_ref[places[0][0], places[0][1] : places[0][1] + 1, :]
        for a, b in places[1:]:
            value = jnp.maximum(value, values_ref[a, b : b + 1, :])
        span = slice(g * wide, g * wide + size)
        here = rows == index // LANES
        for piece in range(3):
            head = value.astype(jnp.bfloat16).astype(jnp.float32)
            value = value - head
            left_ref[piece * high : (piece + 1) * high, span] = jnp.where(here, head, 0.0).astype(
                jnp.bfloat16
            )
        right_ref[:, span] = jnp.where(lanes == index % LANES, 1.0, 0.0).astype(jnp.bfloat16)
    total = lax.dot_general(left_ref[...], right_ref[...], NT, preferred_element_type=jnp.float32)
    total = total[2 * high : 3 * high] + total[high : 2 * high] + total[:high]
    out_ref[...] = total[: out_ref.shape[0]]


def settle(index, values, sources, documents):
    size = index.shape[-1]
    high = -(-documents // (16 * LANES)) * 16
    wide = -(-size // LANES) * LANES * len(sources)
    out = pl.pallas_call(
        functools.partial(settle_kernel, sources, size, high),
        out_shape=jax.ShapeDtypeStruct((documents // LANES, LANES), jnp.float32),
        scratch_shapes=[
            pltpu.VMEM((3 * high, wide), jnp.bfloat16),
            pltpu.VMEM((LANES, wide), jnp.bfloat16),
        ],
        compiler_params=pltpu.CompilerParams(vmem_limit_bytes=16 * MIB),
    )(index, values)
    return out.reshape(-1)


def hosted(embeddings, send_index, place_index, slot_cluster):
    documents = embeddings.shape[0]
    size = send_index.shape[0] // 16
    axes = ("shard", "rep")
    named = arrival_names(place_index, slot_cluster)
    embeddings = tie(embeddings, named)
    (early,) = gather_rows(embeddings, send_index, (0,), size)
    named = lax.ppermute(named, axes, metadata_pairs())
    early = tie(early, named)
    index = send_index.reshape(8, 2, size)

    def go(step, chunk):
        return lax.ppermute(chunk, axes, round_pairs(step - 1))

    def swap(chunk):
        return lax.ppermute(chunk, axes, SIBLINGS)

    own, other = [None] * 8, [None] * 8
    own[1], own[2] = go(1, early), go(2, early)
    late = gather_rows(tie(embeddings, early), send_index, (1, 2, 3, 4), size)
    own[0], other[0] = late[2:]
    own[3], own[4] = go(3, late[0]), go(4, late[0])
    own[1], own[2] = tie(own[1], late[0]), tie(own[2], late[0])
    own[5] = go(5, tie(late[1], own[4]))
    own[6] = go(6, tie(late[1], own[2]))

    named, table = tie(named, late[0]), tie(jnp.asarray(chunk_order()), late[0])
    order = table[lax.axis_index("shard"), lax.axis_index("rep")]
    flat = named.reshape(16, size)[order].reshape(1, 16 * size)

    def score(best, count, passes, after=()):
        arrays, loads = [], []
        for r, side in CHUNKS[:count]:
            chunk = (own, other)[side][r]
            array, place = chunk if isinstance(chunk, tuple) else (chunk, 0)
            if not any(array is known for known in arrays):
                arrays.append(array)
            loads.append(([array is known for known in arrays].index(True), place))
        return gram_best(arrays, tuple(loads), size, flat, best, passes, after)

    best = jnp.full((1, 16 * size), -1.0, jnp.float32)
    best = score(best, 4, (new_pass(1, 3, 4, size),), (order, index))
    other[1] = swap(tie(own[1], best))
    joined = join([own[2], tie(own[3], best), tie(own[4], best)], SHORT)
    own[7] = go(7, tie(late[2], own[3]))
    swapped = swap(joined)
    own[3], own[4] = (joined, 1), (joined, 2)
    best = score(best, 7, (new_pass(4, 2, 7, size), late_pass(2, 2, 6, 7, size)))
    other[2], other[3], other[4] = (swapped, 0), (swapped, 1), (swapped, 2)
    joined = join([tie(own[5], best), tie(own[6], best)], LONG)
    swapped = swap(joined)
    own[5], own[6] = (joined, 0), (joined, 1)
    best = score(best, 12, (new_pass(10, 2, 12, size), late_pass(3, 3, 7, 10, size)))
    other[5], other[6] = (swapped, 0), (swapped, 1)
    own[7] = tie(own[7], best)
    other[7] = swap(own[7])
    best = score(best, 15, (new_pass(14, 1, 15, size), late_pass(10, 2, 12, 14, size)))
    outbound = finish(order, own[7], other[7], flat, best)
    returned = lax.all_to_all(outbound, axes, split_axis=0, concat_axis=0, tiled=True)
    sources = []
    for owner in range(8):
        host, y = host_of(owner)
        for half in range(2):
            sources.append(tuple((host * 4 + y * 2 + core, half) for core in range(2)))
    return settle(index, returned, tuple(sources), documents)


def gathered(embeddings, send_index, place_index, slot_cluster):
    documents, width = embeddings.shape
    owners = lax.axis_size("shard")
    reps = lax.axis_size("rep")
    share = send_index.shape[0] // owners
    outgoing = normalize(embeddings.at[send_index].get(mode="promise_in_bounds"))
    arrived = lax.all_to_all(
        outgoing.reshape(owners, share, width), "shard", split_axis=0, concat_axis=0, tiled=True
    )
    parts = 16
    size = documents // parts
    news = parts // reps
    turn = lax.axis_index("rep") * news
    arrived = jnp.roll(arrived.reshape(parts, size, width), -turn, axis=0)
    clusters = arrival_names(place_index, slot_cluster).reshape(parts, size)
    clusters = jnp.roll(clusters, -turn, axis=0)
    best = jnp.full((1, documents), -1.0, jnp.float32)
    tiles = tuple(range(documents // BLK))
    passes = ((0, news, 0, 1, True, tiles),)
    chunks = [arrived[i] for i in range(parts)]
    loads = tuple((i, 0) for i in range(parts))
    best = gram_best(chunks, loads, size, clusters.reshape(1, -1), best, passes)
    best = lax.all_gather(best[0, : news * size], "rep", axis=0, tiled=True)
    returned = lax.all_to_all(
        best.reshape(owners, share), "shard", split_axis=0, concat_axis=0, tiled=True
    )
    sources = tuple(((0, g),) for g in range(parts))
    return settle(send_index.reshape(parts, size), returned.reshape(1, parts, size), sources, documents)


def solution(mesh):
    planned = mesh.shape["shard"] == 8 and mesh.shape["rep"] == 4

    def shards(embeddings, send_index, place_index, slot_cluster, pair_list):
        del pair_list
        run = hosted if planned else gathered
        return run(embeddings, send_index, place_index, slot_cluster)

    return jax.shard_map(
        shards,
        mesh=mesh,
        in_specs=(P("shard", None), P("shard"), P("shard"), P("shard"), P(("shard", "rep"), None)),
        out_specs=P("shard"),
        check_vma=False,
    )
```

```python
import functools

import jax
import jax.numpy as jnp
import numpy as np
from jax import lax
from jax.experimental import pallas as pl
from jax.experimental.pallas import tpu as pltpu
from jax.sharding import PartitionSpec as P

BLK = 256
LANES = 128
NT = (((1,), (1,)), ((), ()))
MIB = 1024 * 1024
LONG = 40_000_000_000
SHORT = 2_000_000_000

HOSTS = (2, 3, 4, 5)
ROUNDS = ((2, 6, 3, 7, 4, 1, 5), (3, 7, 2, 6, 4, 1, 5))


CHUNKS = (
    (0, 1), (0, 0), (1, 0), (2, 0),
    (3, 0), (4, 0), (1, 1),
    (2, 1), (3, 1), (4, 1), (5, 0), (6, 0),
    (5, 1), (6, 1), (7, 0), (7, 1),
)


def host_of(owner):
    z, x = owner // 2, owner % 2
    return (1 if z < 2 else 2) * 2 + x, z % 2


def chunk_order():
    order = np.zeros((8, 4, 16), np.int32)
    for s in range(8):
        for rep in range(4):
            for i, (step, side) in enumerate(CHUNKS):
                half = rep % 2 ^ side
                order[s, rep, i] = (s ^ ((0,) + ROUNDS[half])[step]) * 2 + half
    return order


def round_pairs(step):
    pairs = []
    for rep in range(4):
        for host in HOSTS:
            pairs.append(((host ^ ROUNDS[rep % 2][step]) * 4 + rep, host * 4 + rep))
    return pairs


SIBLINGS = [(host * 4 + rep, host * 4 + (rep ^ 1)) for host in HOSTS for rep in range(4)]


def metadata_pairs():
    pairs = []
    for owner in range(8):
        host, y = host_of(owner)
        for core in range(2):
            pairs.append((owner * 4 + y * 2 + core, host * 4 + y * 2 + core))
    return pairs


def tie(value, *after):
    return lax.optimization_barrier((value, *after))[0]


def normalize(rows):
    wide = rows.astype(jnp.float32)
    return (wide * lax.rsqrt(jnp.sum(wide * wide, axis=1, keepdims=True) + 1e-06)).astype(
        jnp.bfloat16
    )


def names_kernel(place_ref, slots_ref, out_ref):
    block = place_ref[...] // BLK
    found = jnp.zeros_like(block)
    for i in range(slots_ref.shape[0] * LANES // BLK):
        row = i * BLK // LANES
        found = jnp.where(block == i, slots_ref[row : row + 1, 0:1], found)
    out_ref[...] = found


def arrival_names(place_index, slot_cluster):
    places = place_index.reshape(-1, LANES)
    return pl.pallas_call(
        names_kernel, out_shape=jax.ShapeDtypeStruct(places.shape, jnp.int32)
    )(places, slot_cluster.reshape(-1, LANES))


def chunk_start(slot, size):
    s, rep = lax.axis_index("shard"), lax.axis_index("rep")
    y, core = rep // 2, rep % 2
    inner = (s >= HOSTS[0]) & (s <= HOSTS[-1])
    turn = min(slot, 3)
    steps = [(order[2 * turn], (order + (0,))[2 * turn + 1]) for order in ROUNDS]
    outer_step = jnp.where(core == 0, steps[0][0], steps[1][0])
    inner_step = jnp.where(core == 0, steps[0][1], steps[1][1])
    target = s ^ jnp.where(inner, inner_step, outer_step)
    owner = (2 * (target // 2 - 1) + y) * 2 + target % 2
    half = 1 - core if slot == 4 else core
    return owner * (2 * size) + half * size


def gather_kernel(slots, size, group, sections, *refs):
    index_hbm, rows_ref = refs[:2]
    index_ref, raw, wide, picked, sems = refs[-5:]
    outs = refs[-5 - len(slots) : -5]
    listed = pltpu.make_async_copy(index_hbm, index_ref, sems.at[sections])
    listed.start()
    width = raw.shape[1]
    tiles = width // LANES
    part = raw.shape[0] // sections
    copies = []
    for i in range(sections):
        rows = pl.ds(i * part, part)
        copies.append(pltpu.make_async_copy(rows_ref.at[rows], raw.at[rows], sems.at[i]))
        copies[-1].start()
    step = 160
    for i in range(sections):
        copies[i].wait()

        def widen(j, _, i=i):
            first = i * part + j * step
            rows = raw[pl.ds(pl.multiple_of(first, step), step), :].astype(jnp.float32)
            for t in range(tiles):
                wide[pl.ds(first * tiles + t, step, stride=tiles), :] = rows[:, t * LANES : (t + 1) * LANES]
            return 0

        lax.fori_loop(0, part // step, widen, 0)
    listed.wait()
    for c, slot in enumerate(slots):
        base = chunk_start(slot, size)

        def pick(j, _, c=c, base=base):
            for t in range(group):
                source = pl.multiple_of(index_ref[base + j * group + t] * tiles, tiles)
                picked[t * tiles : (t + 1) * tiles, :] = wide[pl.ds(source, tiles), :]
            for first in range(0, group, 16):
                rows = jnp.concatenate(
                    [picked[pl.ds(first * tiles + t, 16, stride=tiles), :] for t in range(tiles)],
                    axis=1,
                )
                scale = lax.rsqrt(jnp.sum(rows * rows, axis=1, keepdims=True) + 1e-06)
                outs[c][pl.ds(pl.multiple_of(j * group + first, 16), 16), :] = (rows * scale).astype(
                    jnp.bfloat16
                )
            return 0

        lax.fori_loop(0, size // group, pick, 0)


def gather_rows(embeddings, index, slots, size):
    documents, width = embeddings.shape
    count = len(slots)
    sections = 10
    group = 80
    return pl.pallas_call(
        functools.partial(gather_kernel, slots, size, group, sections),
        out_shape=[jax.ShapeDtypeStruct((size, width), jnp.bfloat16)] * count,
        in_specs=[pl.BlockSpec(memory_space=pltpu.HBM)] * 2,
        out_specs=[pl.BlockSpec(memory_space=pltpu.VMEM)] * count,
        scratch_shapes=[
            pltpu.SMEM(index.shape, jnp.int32),
            pltpu.VMEM((documents, width), jnp.bfloat16),
            pltpu.VMEM((documents * width // LANES, LANES), jnp.float32),
            pltpu.VMEM((group * width // LANES, LANES), jnp.float32),
            pltpu.SemaphoreType.DMA((sections + 1,)),
        ],
        compiler_params=pltpu.CompilerParams(vmem_limit_bytes=45 * MIB),
        cost_estimate=pl.CostEstimate(flops=LONG, bytes_accessed=0, transcendentals=0),
    )(index, embeddings)


def best_of_rows(acc, size):
    return jnp.max(jnp.transpose(acc), axis=0, keepdims=True)[:, :size]


def as_column(row_ref, start, size):
    wide = -(-size // LANES) * LANES
    row = row_ref[:, start : start + wide]
    return jnp.transpose(jnp.broadcast_to(row, (LANES, wide)))[:size]


def gram_kernel(passes, loads, size, limit, *refs):
    cluster_row, before_ref, best_ref, held, acc, sems = refs[-6:]
    count = len(loads)

    def source(i):
        array, place = loads[i]
        return refs[array].at[pl.ds(place * size, size)]

    def copy(i):
        return pltpu.make_async_copy(source(i), held.at[pl.ds(i * size, size)], sems.at[i])

    def arrive(i):
        rows = held.at[pl.ds(0, size)]
        pltpu.make_async_copy(rows, rows, sems.at[i]).wait()

    low = passes[0][5][0] * BLK // size
    for i in (*range(low, count), *range(low)):
        copy(i).start()
    best_ref[...] = before_ref[...]
    for i in range(low, count):
        copy(i).wait()

    def sweep(first, height, work):
        acc[...] = jnp.full_like(acc, -1.0)
        rows = held[first : first + height, :]
        left = as_column(cluster_row, first, height)
        left = jnp.concatenate([left, left], axis=1)

        def tile(start, special):
            gram = lax.dot_general(
                rows, held[pl.ds(start, BLK), :], NT, preferred_element_type=jnp.float32
            )
            counts = left == cluster_row[:, pl.ds(start, BLK)]
            if special:
                column = start + lax.broadcasted_iota(jnp.int32, (height, BLK), 1)
                row = first + lax.broadcasted_iota(jnp.int32, (height, BLK), 0)
                counts = counts & (column != row) & (column < limit)
            values = jnp.where(counts, gram, jnp.float32(-1.0))
            top = jnp.max(values, axis=0, keepdims=True)
            best_ref[:, pl.ds(start, BLK)] = jnp.maximum(best_ref[:, pl.ds(start, BLK)], top)
            acc[0:height, :] = jnp.maximum(
                acc[0:height, :], jnp.maximum(values[:, :LANES], values[:, LANES:])
            )

        work(tile)
        span = slice(first, first + height)
        best_ref[:, span] = jnp.maximum(best_ref[:, span], best_of_rows(acc[...], height))

    for n, (chunk, news, groups, group, meets, last, halved) in enumerate(passes):
        first, height = chunk * size, news * size

        def masked(t, first=first, height=height):
            return (t * BLK < first + height and (t + 1) * BLK > first) or (t + 1) * BLK > limit

        if halved:
            count_of_tiles = len(last) // 2
            cut = last[count_of_tiles] * BLK - halved * size
            core = lax.axis_index("rep") % 2
            for h, (top, bottom) in enumerate(((0, cut), (cut, height))):

                def work(tile, h=h, masked=masked, last=last, count_of_tiles=count_of_tiles, core=core):
                    side = h + core - 2 * h * core
                    for t in range(count_of_tiles):
                        start = (last[t] + count_of_tiles * side) * BLK
                        special = masked(last[t]) or masked(last[t + count_of_tiles])
                        tile(pl.multiple_of(start, BLK), special)

                sweep(first + top, bottom - top, work)
            continue
        step = -(-group * BLK // size)

        def work(tile, n=n, groups=groups, group=group, meets=meets, last=last, masked=masked, step=step):
            for t in last:
                tile(t * BLK, masked(t))

            def visit(u, _):
                for i in range(step) if n == 0 else ():

                    @pl.when(u * step + i < low)
                    def _(i=i):
                        arrive(u * step + i)

                for t in range(group):
                    tile(pl.multiple_of((u * group + t) * BLK, BLK), meets)
                return 0

            lax.fori_loop(0, groups, visit, 0)

        sweep(first, height, work)


def gram_best(arrays, loads, size, cluster_row, before, passes, after=()):
    width = arrays[0].shape[1]
    limit = len(loads) * size
    held = -(-limit // BLK) * BLK
    tall = max(news for _, news, *_ in passes) * size
    padded = -(-tall // LANES) * LANES
    return pl.pallas_call(
        functools.partial(gram_kernel, passes, loads, size, limit),
        out_shape=jax.ShapeDtypeStruct(before.shape, jnp.float32),
        in_specs=[pl.BlockSpec(memory_space=pl.ANY)] * (len(arrays) + len(after))
        + [pl.BlockSpec(memory_space=pltpu.VMEM)] * 2,
        out_specs=pl.BlockSpec(memory_space=pltpu.VMEM),
        scratch_shapes=[
            pltpu.VMEM((held, width), jnp.bfloat16),
            pltpu.VMEM((padded, LANES), jnp.float32),
            pltpu.SemaphoreType.DMA((len(loads),)),
        ],
        compiler_params=pltpu.CompilerParams(vmem_limit_bytes=24 * MIB),
        cost_estimate=pl.CostEstimate(flops=0, bytes_accessed=0, transcendentals=0),
    )(*arrays, *after, cluster_row, before)


def join_kernel(size, *refs):
    out_ref, sems = refs[-2:]
    copies = [
        pltpu.make_async_copy(ref, out_ref.at[pl.ds(i * size, size)], sems.at[i])
        for i, ref in enumerate(refs[:-2])
    ]
    for copy in copies:
        copy.start()
    for copy in copies:
        copy.wait()


def join(chunks, work):
    size, width = chunks[0].shape
    return pl.pallas_call(
        functools.partial(join_kernel, size),
        out_shape=jax.ShapeDtypeStruct((len(chunks) * size, width), chunks[0].dtype),
        in_specs=[pl.BlockSpec(memory_space=pl.ANY)] * len(chunks),
        out_specs=pl.BlockSpec(memory_space=pl.ANY),
        scratch_shapes=[pltpu.SemaphoreType.DMA((len(chunks),))],
        compiler_params=pltpu.CompilerParams(vmem_limit_bytes=MIB),
        cost_estimate=pl.CostEstimate(flops=work, bytes_accessed=0, transcendentals=0),
    )(*chunks)


def new_pass(chunk, news, count, size):
    plain = chunk * size // BLK
    group = max(n for n in range(1, 8) if plain % n == 0)
    groups = plain // group
    tiles = -(-count * size // BLK)
    return (chunk, news, groups, group, False, tuple(range(groups * group, tiles)), 0)


def late_pass(chunk, news, low, high, size, halved=False):
    tiles = tuple(range(low * size // BLK, -(-high * size // BLK)))
    return (chunk, news, 0, 1, True, tiles, low if halved else 0)


def finish_kernel(size, order_ref, own_ref, other_ref, clusters_ref, best_ref, out_ref, acc):
    gram = lax.dot_general(own_ref[...], other_ref[...], NT, preferred_element_type=jnp.float32)
    left = as_column(clusters_ref, 14 * size, size)
    left = jnp.tile(left, (1, -(-size // LANES)))[:, :size]
    last = 15 * size
    values = jnp.where(left == clusters_ref[:, last : last + size], gram, jnp.float32(-1.0))
    acc[...] = jnp.full_like(acc, -1.0)
    acc[0:size, :] = jnp.broadcast_to(jnp.max(values, axis=1, keepdims=True), (size, LANES))
    for i in range(16):
        found = best_ref[:, i * size : (i + 1) * size]
        if i == 14:
            found = jnp.maximum(found, best_of_rows(acc[...], size))
        if i == 15:
            found = jnp.maximum(found, jnp.max(values, axis=0, keepdims=True))
        place = order_ref[i]
        source, half = place // 2, place % 2
        for rep in range(4):
            out_ref[source * 4 + rep, pl.ds(half, 1), :] = found


def finish(order, own, other, clusters, best):
    size = own.shape[0]
    padded = -(-size // LANES) * LANES
    return pl.pallas_call(
        functools.partial(finish_kernel, size),
        out_shape=jax.ShapeDtypeStruct((32, 2, size), jnp.float32),
        in_specs=[pl.BlockSpec(memory_space=pltpu.SMEM)]
        + [pl.BlockSpec(memory_space=pltpu.VMEM)] * 4,
        out_specs=pl.BlockSpec(memory_space=pltpu.VMEM),
        scratch_shapes=[pltpu.VMEM((padded, LANES), jnp.float32)],
        compiler_params=pltpu.CompilerParams(vmem_limit_bytes=16 * MIB),
    )(order, own, other, clusters, best)


def settle_kernel(sources, size, high, index_ref, values_ref, out_ref, left_ref, right_ref):
    wide = left_ref.shape[1] // len(sources)
    left_ref[...] = jnp.zeros_like(left_ref)
    right_ref[...] = jnp.zeros_like(right_ref)
    rows = lax.broadcasted_iota(jnp.int32, (high, size), 0)
    lanes = lax.broadcasted_iota(jnp.int32, (LANES, size), 0)
    for g, places in enumerate(sources):
        index = index_ref[g // 2, g % 2 : g % 2 + 1, :] if index_ref.ndim == 3 else index_ref[g : g + 1, :]
        value = values_ref[places[0][0], places[0][1] : places[0][1] + 1, :]
        for a, b in places[1:]:
            value = jnp.maximum(value, values_ref[a, b : b + 1, :])
        span = slice(g * wide, g * wide + size)
        here = rows == index // LANES
        for piece in range(3):
            head = value.astype(jnp.bfloat16).astype(jnp.float32)
            value = value - head
            left_ref[piece * high : (piece + 1) * high, span] = jnp.where(here, head, 0.0).astype(
                jnp.bfloat16
            )
        right_ref[:, span] = jnp.where(lanes == index % LANES, 1.0, 0.0).astype(jnp.bfloat16)
    total = lax.dot_general(left_ref[...], right_ref[...], NT, preferred_element_type=jnp.float32)
    total = total[2 * high : 3 * high] + total[high : 2 * high] + total[:high]
    out_ref[...] = total[: out_ref.shape[0]]


def settle(index, values, sources, documents):
    size = index.shape[-1]
    high = -(-documents // (16 * LANES)) * 16
    wide = -(-size // LANES) * LANES * len(sources)
    out = pl.pallas_call(
        functools.partial(settle_kernel, sources, size, high),
        out_shape=jax.ShapeDtypeStruct((documents // LANES, LANES), jnp.float32),
        scratch_shapes=[
            pltpu.VMEM((3 * high, wide), jnp.bfloat16),
            pltpu.VMEM((LANES, wide), jnp.bfloat16),
        ],
        compiler_params=pltpu.CompilerParams(vmem_limit_bytes=16 * MIB),
    )(index, values)
    return out.reshape(-1)


def hosted(embeddings, send_index, place_index, slot_cluster):
    documents = embeddings.shape[0]
    size = send_index.shape[0] // 16
    axes = ("shard", "rep")
    named = arrival_names(place_index, slot_cluster)
    embeddings = tie(embeddings, named)
    (early,) = gather_rows(embeddings, send_index, (0,), size)
    named = lax.ppermute(named, axes, metadata_pairs())
    early = tie(early, named)
    index = send_index.reshape(8, 2, size)

    def go(step, chunk):
        return lax.ppermute(chunk, axes, round_pairs(step - 1))

    def swap(chunk):
        return lax.ppermute(chunk, axes, SIBLINGS)

    own, other = [None] * 8, [None] * 8
    own[1], own[2] = go(1, early), go(2, early)
    late = gather_rows(tie(embeddings, early), send_index, (1, 2, 3, 4), size)
    own[0], other[0] = late[2:]
    own[3], own[4] = go(3, late[0]), go(4, late[0])
    own[1], own[2] = tie(own[1], late[0]), tie(own[2], late[0])
    own[5] = go(5, tie(late[1], own[4]))
    own[6] = go(6, tie(late[1], own[2]))

    named, table = tie(named, late[0]), tie(jnp.asarray(chunk_order()), late[0])
    order = table[lax.axis_index("shard"), lax.axis_index("rep")]
    flat = named.reshape(16, size)[order].reshape(1, 16 * size)

    def score(best, count, passes, after=()):
        arrays, loads = [], []
        for r, side in CHUNKS[:count]:
            chunk = (own, other)[side][r]
            array, place = chunk if isinstance(chunk, tuple) else (chunk, 0)
            if not any(array is known for known in arrays):
                arrays.append(array)
            loads.append(([array is known for known in arrays].index(True), place))
        return gram_best(arrays, tuple(loads), size, flat, best, passes, after)

    best = jnp.full((1, 16 * size), -1.0, jnp.float32)
    best = score(best, 4, (new_pass(1, 3, 4, size),), (order, index))
    other[1] = swap(tie(own[1], best))
    joined = join([own[2], tie(own[3], best), tie(own[4], best)], SHORT)
    own[7] = go(7, tie(late[2], own[3]))
    swapped = swap(joined)
    own[3], own[4] = (joined, 1), (joined, 2)
    best = score(best, 7, (new_pass(4, 2, 7, size), late_pass(2, 2, 6, 7, size)))
    other[2], other[3], other[4] = (swapped, 0), (swapped, 1), (swapped, 2)
    joined = join([tie(own[5], best), tie(own[6], best)], LONG)
    swapped = swap(joined)
    own[5], own[6] = (joined, 0), (joined, 1)
    best = score(best, 12, (new_pass(10, 2, 12, size), late_pass(3, 3, 7, 10, size, True)))
    other[5], other[6] = (swapped, 0), (swapped, 1)
    own[7] = tie(own[7], best)
    other[7] = swap(own[7])
    best = score(best, 15, (new_pass(14, 1, 15, size), late_pass(10, 2, 12, 14, size, True)))
    outbound = finish(order, own[7], other[7], flat, best)
    returned = lax.all_to_all(outbound, axes, split_axis=0, concat_axis=0, tiled=True)
    sources = []
    for owner in range(8):
        host, y = host_of(owner)
        for half in range(2):
            sources.append(tuple((host * 4 + y * 2 + core, half) for core in range(2)))
    return settle(index, returned, tuple(sources), documents)


def gathered(embeddings, send_index, place_index, slot_cluster):
    documents, width = embeddings.shape
    owners = lax.axis_size("shard")
    reps = lax.axis_size("rep")
    share = send_index.shape[0] // owners
    outgoing = normalize(embeddings.at[send_index].get(mode="promise_in_bounds"))
    arrived = lax.all_to_all(
        outgoing.reshape(owners, share, width), "shard", split_axis=0, concat_axis=0, tiled=True
    )
    parts = 16
    size = documents // parts
    news = parts // reps
    turn = lax.axis_index("rep") * news
    arrived = jnp.roll(arrived.reshape(parts, size, width), -turn, axis=0)
    clusters = arrival_names(place_index, slot_cluster).reshape(parts, size)
    clusters = jnp.roll(clusters, -turn, axis=0)
    best = jnp.full((1, documents), -1.0, jnp.float32)
    tiles = tuple(range(documents // BLK))
    passes = ((0, news, 0, 1, True, tiles, 0),)
    chunks = [arrived[i] for i in range(parts)]
    loads = tuple((i, 0) for i in range(parts))
    best = gram_best(chunks, loads, size, clusters.reshape(1, -1), best, passes)
    best = lax.all_gather(best[0, : news * size], "rep", axis=0, tiled=True)
    returned = lax.all_to_all(
        best.reshape(owners, share), "shard", split_axis=0, concat_axis=0, tiled=True
    )
    sources = tuple(((0, g),) for g in range(parts))
    return settle(send_index.reshape(parts, size), returned.reshape(1, parts, size), sources, documents)


def solution(mesh):
    planned = mesh.shape["shard"] == 8 and mesh.shape["rep"] == 4

    def shards(embeddings, send_index, place_index, slot_cluster, pair_list):
        del pair_list
        run = hosted if planned else gathered
        return run(embeddings, send_index, place_index, slot_cluster)

    return jax.shard_map(
        shards,
        mesh=mesh,
        in_specs=(P("shard", None), P("shard"), P("shard"), P("shard"), P(("shard", "rep"), None)),
        out_specs=P("shard"),
        check_vma=False,
    )
```

```python
import functools

import jax
import jax.numpy as jnp
import numpy as np
from jax import lax
from jax.experimental import pallas as pl
from jax.experimental.pallas import tpu as pltpu
from jax.sharding import PartitionSpec as P

BLK = 256
LANES = 128
NT = (((1,), (1,)), ((), ()))
MIB = 1024 * 1024
LONG = 40_000_000_000
SHORT = 2_000_000_000

HOSTS = (2, 3, 4, 5)
ROUNDS = ((2, 6, 3, 7, 4, 1, 5), (3, 7, 2, 6, 4, 1, 5))


CHUNKS = (
    (0, 1), (0, 0), (1, 0), (2, 0),
    (3, 0), (4, 0), (1, 1),
    (2, 1), (3, 1), (4, 1), (5, 0), (6, 0),
    (5, 1), (6, 1), (7, 0), (7, 1),
)


def host_of(owner):
    z, x = owner // 2, owner % 2
    return (1 if z < 2 else 2) * 2 + x, z % 2


def chunk_order():
    order = np.zeros((8, 4, 16), np.int32)
    for s in range(8):
        for rep in range(4):
            for i, (step, side) in enumerate(CHUNKS):
                half = rep % 2 ^ side
                order[s, rep, i] = (s ^ ((0,) + ROUNDS[half])[step]) * 2 + half
    return order


def round_pairs(step):
    pairs = []
    for rep in range(4):
        for host in HOSTS:
            pairs.append(((host ^ ROUNDS[rep % 2][step]) * 4 + rep, host * 4 + rep))
    return pairs


SIBLINGS = [(host * 4 + rep, host * 4 + (rep ^ 1)) for host in HOSTS for rep in range(4)]


def metadata_pairs():
    pairs = []
    for owner in range(8):
        host, y = host_of(owner)
        for core in range(2):
            pairs.append((owner * 4 + y * 2 + core, host * 4 + y * 2 + core))
    return pairs


def tie(value, *after):
    return lax.optimization_barrier((value, *after))[0]


def normalize(rows):
    wide = rows.astype(jnp.float32)
    return (wide * lax.rsqrt(jnp.sum(wide * wide, axis=1, keepdims=True) + 1e-06)).astype(
        jnp.bfloat16
    )


def write_names(place_ref, slots_ref, out_ref):
    block = place_ref[...] // BLK
    found = jnp.zeros_like(block)
    for i in range(slots_ref.shape[0] * LANES // BLK):
        row = i * BLK // LANES
        found = jnp.where(block == i, slots_ref[row : row + 1, 0:1], found)
    out_ref[...] = found


def arrival_names(place_index, slot_cluster):
    places = place_index.reshape(-1, LANES)
    return pl.pallas_call(
        write_names, out_shape=jax.ShapeDtypeStruct(places.shape, jnp.int32)
    )(places, slot_cluster.reshape(-1, LANES))


def chunk_start(slot, size):
    s, rep = lax.axis_index("shard"), lax.axis_index("rep")
    y, core = rep // 2, rep % 2
    inner = (s >= HOSTS[0]) & (s <= HOSTS[-1])
    turn = min(slot, 3)
    steps = [(order[2 * turn], (order + (0,))[2 * turn + 1]) for order in ROUNDS]
    outer_step = jnp.where(core == 0, steps[0][0], steps[1][0])
    inner_step = jnp.where(core == 0, steps[0][1], steps[1][1])
    target = s ^ jnp.where(inner, inner_step, outer_step)
    owner = (2 * (target // 2 - 1) + y) * 2 + target % 2
    half = 1 - core if slot == 4 else core
    return owner * (2 * size) + half * size


def gather_kernel(slots, size, group, sections, named, *refs):
    index_hbm, rows_ref = refs[:2]
    index_ref, raw, wide, picked, sems = refs[-5:]
    outs = refs[-5 - len(slots) : -5]
    listed = pltpu.make_async_copy(index_hbm, index_ref, sems.at[sections])
    listed.start()
    width = raw.shape[1]
    tiles = width // LANES
    part = raw.shape[0] // sections
    copies = []
    for i in range(sections):
        rows = pl.ds(i * part, part)
        copies.append(pltpu.make_async_copy(rows_ref.at[rows], raw.at[rows], sems.at[i]))
        copies[-1].start()
    if named:
        write_names(*refs[2:5])
    step = 160
    for i in range(sections):
        copies[i].wait()

        def widen(j, _, i=i):
            first = i * part + j * step
            rows = raw[pl.ds(pl.multiple_of(first, step), step), :].astype(jnp.float32)
            for t in range(tiles):
                wide[pl.ds(first * tiles + t, step, stride=tiles), :] = rows[:, t * LANES : (t + 1) * LANES]
            return 0

        lax.fori_loop(0, part // step, widen, 0)
    listed.wait()
    for c, slot in enumerate(slots):
        base = chunk_start(slot, size)

        def pick(j, _, c=c, base=base):
            for t in range(group):
                source = pl.multiple_of(index_ref[base + j * group + t] * tiles, tiles)
                picked[t * tiles : (t + 1) * tiles, :] = wide[pl.ds(source, tiles), :]
            for first in range(0, group, 16):
                rows = jnp.concatenate(
                    [picked[pl.ds(first * tiles + t, 16, stride=tiles), :] for t in range(tiles)],
                    axis=1,
                )
                scale = lax.rsqrt(jnp.sum(rows * rows, axis=1, keepdims=True) + 1e-06)
                outs[c][pl.ds(pl.multiple_of(j * group + first, 16), 16), :] = (rows * scale).astype(
                    jnp.bfloat16
                )
            return 0

        lax.fori_loop(0, size // group, pick, 0)


def gather_rows(embeddings, index, slots, size, names=()):
    documents, width = embeddings.shape
    count = len(slots)
    sections = 10
    group = 80
    names = [array.reshape(-1, LANES) for array in names]
    outs = [jax.ShapeDtypeStruct(array.shape, jnp.int32) for array in names[:1]]
    outs += [jax.ShapeDtypeStruct((size, width), jnp.bfloat16)] * count
    return pl.pallas_call(
        functools.partial(gather_kernel, slots, size, group, sections, bool(names)),
        out_shape=outs,
        in_specs=[pl.BlockSpec(memory_space=pltpu.HBM)] * 2
        + [pl.BlockSpec(memory_space=pltpu.VMEM)] * len(names),
        out_specs=[pl.BlockSpec(memory_space=pltpu.VMEM)] * len(outs),
        scratch_shapes=[
            pltpu.SMEM(index.shape, jnp.int32),
            pltpu.VMEM((documents, width), jnp.bfloat16),
            pltpu.VMEM((documents * width // LANES, LANES), jnp.float32),
            pltpu.VMEM((group * width // LANES, LANES), jnp.float32),
            pltpu.SemaphoreType.DMA((sections + 1,)),
        ],
        compiler_params=pltpu.CompilerParams(vmem_limit_bytes=45 * MIB),
        cost_estimate=pl.CostEstimate(flops=LONG, bytes_accessed=0, transcendentals=0),
    )(index, embeddings, *names)


def best_of_rows(acc, size):
    return jnp.max(jnp.transpose(acc), axis=0, keepdims=True)[:, :size]


def as_column(row_ref, start, size):
    wide = -(-size // LANES) * LANES
    row = row_ref[:, start : start + wide]
    return jnp.transpose(jnp.broadcast_to(row, (LANES, wide)))[:size]


def gram_kernel(passes, loads, size, limit, *refs):
    cluster_row, before_ref, best_ref, held, acc, sems = refs[-6:]
    count = len(loads)

    def source(i):
        array, place = loads[i]
        return refs[array].at[pl.ds(place * size, size)]

    def copy(i):
        return pltpu.make_async_copy(source(i), held.at[pl.ds(i * size, size)], sems.at[i])

    def arrive(i):
        rows = held.at[pl.ds(0, size)]
        pltpu.make_async_copy(rows, rows, sems.at[i]).wait()

    low = passes[0][5][0] * BLK // size
    for i in (*range(low, count), *range(low)):
        copy(i).start()
    best_ref[...] = before_ref[...]
    for i in range(low, count):
        copy(i).wait()

    def sweep(first, height, work):
        acc[...] = jnp.full_like(acc, -1.0)
        rows = held[first : first + height, :]
        left = as_column(cluster_row, first, height)
        left = jnp.concatenate([left, left], axis=1)

        def tile(start, special):
            gram = lax.dot_general(
                rows, held[pl.ds(start, BLK), :], NT, preferred_element_type=jnp.float32
            )
            counts = left == cluster_row[:, pl.ds(start, BLK)]
            if special:
                column = start + lax.broadcasted_iota(jnp.int32, (height, BLK), 1)
                row = first + lax.broadcasted_iota(jnp.int32, (height, BLK), 0)
                counts = counts & (column != row) & (column < limit)
            values = jnp.where(counts, gram, jnp.float32(-1.0))
            top = jnp.max(values, axis=0, keepdims=True)
            best_ref[:, pl.ds(start, BLK)] = jnp.maximum(best_ref[:, pl.ds(start, BLK)], top)
            acc[0:height, :] = jnp.maximum(
                acc[0:height, :], jnp.maximum(values[:, :LANES], values[:, LANES:])
            )

        work(tile)
        span = slice(first, first + height)
        best_ref[:, span] = jnp.maximum(best_ref[:, span], best_of_rows(acc[...], height))

    for n, (chunk, news, groups, group, meets, last, halved) in enumerate(passes):
        first, height = chunk * size, news * size

        def masked(t, first=first, height=height):
            return (t * BLK < first + height and (t + 1) * BLK > first) or (t + 1) * BLK > limit

        if halved:
            count_of_tiles = len(last) // 2
            cut = last[count_of_tiles] * BLK - halved * size
            core = lax.axis_index("rep") % 2
            for h, (top, bottom) in enumerate(((0, cut), (cut, height))):

                def work(tile, h=h, masked=masked, last=last, count_of_tiles=count_of_tiles, core=core):
                    side = h + core - 2 * h * core
                    for t in range(count_of_tiles):
                        start = (last[t] + count_of_tiles * side) * BLK
                        special = masked(last[t]) or masked(last[t + count_of_tiles])
                        tile(pl.multiple_of(start, BLK), special)

                sweep(first + top, bottom - top, work)
            continue
        step = -(-group * BLK // size)

        def work(tile, n=n, groups=groups, group=group, meets=meets, last=last, masked=masked, step=step):
            for t in last:
                tile(t * BLK, masked(t))

            def visit(u, _):
                for i in range(step) if n == 0 else ():

                    @pl.when(u * step + i < low)
                    def _(i=i):
                        arrive(u * step + i)

                for t in range(group):
                    tile(pl.multiple_of((u * group + t) * BLK, BLK), meets)
                return 0

            lax.fori_loop(0, groups, visit, 0)

        sweep(first, height, work)


def gram_best(arrays, loads, size, cluster_row, before, passes, after=()):
    width = arrays[0].shape[1]
    limit = len(loads) * size
    held = -(-limit // BLK) * BLK
    tall = max(news for _, news, *_ in passes) * size
    padded = -(-tall // LANES) * LANES
    return pl.pallas_call(
        functools.partial(gram_kernel, passes, loads, size, limit),
        out_shape=jax.ShapeDtypeStruct(before.shape, jnp.float32),
        in_specs=[pl.BlockSpec(memory_space=pl.ANY)] * (len(arrays) + len(after))
        + [pl.BlockSpec(memory_space=pltpu.VMEM)] * 2,
        out_specs=pl.BlockSpec(memory_space=pltpu.VMEM),
        scratch_shapes=[
            pltpu.VMEM((held, width), jnp.bfloat16),
            pltpu.VMEM((padded, LANES), jnp.float32),
            pltpu.SemaphoreType.DMA((len(loads),)),
        ],
        compiler_params=pltpu.CompilerParams(vmem_limit_bytes=24 * MIB),
        cost_estimate=pl.CostEstimate(flops=0, bytes_accessed=0, transcendentals=0),
    )(*arrays, *after, cluster_row, before)


def join_kernel(size, *refs):
    out_ref, sems = refs[-2:]
    copies = [
        pltpu.make_async_copy(ref, out_ref.at[pl.ds(i * size, size)], sems.at[i])
        for i, ref in enumerate(refs[:-2])
    ]
    for copy in copies:
        copy.start()
    for copy in copies:
        copy.wait()


def join(chunks, work):
    size, width = chunks[0].shape
    return pl.pallas_call(
        functools.partial(join_kernel, size),
        out_shape=jax.ShapeDtypeStruct((len(chunks) * size, width), chunks[0].dtype),
        in_specs=[pl.BlockSpec(memory_space=pl.ANY)] * len(chunks),
        out_specs=pl.BlockSpec(memory_space=pl.ANY),
        scratch_shapes=[pltpu.SemaphoreType.DMA((len(chunks),))],
        compiler_params=pltpu.CompilerParams(vmem_limit_bytes=MIB),
        cost_estimate=pl.CostEstimate(flops=work, bytes_accessed=0, transcendentals=0),
    )(*chunks)


def new_pass(chunk, news, count, size):
    plain = chunk * size // BLK
    group = max(n for n in range(1, 8) if plain % n == 0)
    groups = plain // group
    tiles = -(-count * size // BLK)
    return (chunk, news, groups, group, False, tuple(range(groups * group, tiles)), 0)


def late_pass(chunk, news, low, high, size, halved=False):
    tiles = tuple(range(low * size // BLK, -(-high * size // BLK)))
    return (chunk, news, 0, 1, True, tiles, low if halved else 0)


def finish_kernel(size, order_ref, own_ref, other_ref, clusters_ref, best_ref, out_ref, acc):
    gram = lax.dot_general(own_ref[...], other_ref[...], NT, preferred_element_type=jnp.float32)
    left = as_column(clusters_ref, 14 * size, size)
    left = jnp.tile(left, (1, -(-size // LANES)))[:, :size]
    last = 15 * size
    values = jnp.where(left == clusters_ref[:, last : last + size], gram, jnp.float32(-1.0))
    acc[...] = jnp.full_like(acc, -1.0)
    acc[0:size, :] = jnp.broadcast_to(jnp.max(values, axis=1, keepdims=True), (size, LANES))
    for i in range(16):
        found = best_ref[:, i * size : (i + 1) * size]
        if i == 14:
            found = jnp.maximum(found, best_of_rows(acc[...], size))
        if i == 15:
            found = jnp.maximum(found, jnp.max(values, axis=0, keepdims=True))
        place = order_ref[i]
        source, half = place // 2, place % 2
        for rep in range(4):
            out_ref[source * 4 + rep, pl.ds(half, 1), :] = found


def finish(order, own, other, clusters, best):
    size = own.shape[0]
    padded = -(-size // LANES) * LANES
    return pl.pallas_call(
        functools.partial(finish_kernel, size),
        out_shape=jax.ShapeDtypeStruct((32, 2, size), jnp.float32),
        in_specs=[pl.BlockSpec(memory_space=pltpu.SMEM)]
        + [pl.BlockSpec(memory_space=pltpu.VMEM)] * 4,
        out_specs=pl.BlockSpec(memory_space=pltpu.VMEM),
        scratch_shapes=[pltpu.VMEM((padded, LANES), jnp.float32)],
        compiler_params=pltpu.CompilerParams(vmem_limit_bytes=16 * MIB),
    )(order, own, other, clusters, best)


def settle_kernel(sources, size, high, index_ref, values_ref, out_ref, left_ref, right_ref):
    wide = left_ref.shape[1] // len(sources)
    left_ref[...] = jnp.zeros_like(left_ref)
    right_ref[...] = jnp.zeros_like(right_ref)
    rows = lax.broadcasted_iota(jnp.int32, (high, size), 0)
    lanes = lax.broadcasted_iota(jnp.int32, (LANES, size), 0)
    for g, places in enumerate(sources):
        index = index_ref[g // 2, g % 2 : g % 2 + 1, :] if index_ref.ndim == 3 else index_ref[g : g + 1, :]
        value = values_ref[places[0][0], places[0][1] : places[0][1] + 1, :]
        for a, b in places[1:]:
            value = jnp.maximum(value, values_ref[a, b : b + 1, :])
        span = slice(g * wide, g * wide + size)
        here = rows == index // LANES
        for piece in range(3):
            head = value.astype(jnp.bfloat16).astype(jnp.float32)
            value = value - head
            left_ref[piece * high : (piece + 1) * high, span] = jnp.where(here, head, 0.0).astype(
                jnp.bfloat16
            )
        right_ref[:, span] = jnp.where(lanes == index % LANES, 1.0, 0.0).astype(jnp.bfloat16)
    total = lax.dot_general(left_ref[...], right_ref[...], NT, preferred_element_type=jnp.float32)
    total = total[2 * high : 3 * high] + total[high : 2 * high] + total[:high]
    out_ref[...] = total[: out_ref.shape[0]]


def settle(index, values, sources, documents):
    size = index.shape[-1]
    high = -(-documents // (16 * LANES)) * 16
    wide = -(-size // LANES) * LANES * len(sources)
    out = pl.pallas_call(
        functools.partial(settle_kernel, sources, size, high),
        out_shape=jax.ShapeDtypeStruct((documents // LANES, LANES), jnp.float32),
        scratch_shapes=[
            pltpu.VMEM((3 * high, wide), jnp.bfloat16),
            pltpu.VMEM((LANES, wide), jnp.bfloat16),
        ],
        compiler_params=pltpu.CompilerParams(vmem_limit_bytes=16 * MIB),
    )(index, values)
    return out.reshape(-1)


def hosted(embeddings, send_index, place_index, slot_cluster):
    documents = embeddings.shape[0]
    size = send_index.shape[0] // 16
    axes = ("shard", "rep")
    named, early = gather_rows(embeddings, send_index, (0,), size, (place_index, slot_cluster))
    named = lax.ppermute(named, axes, metadata_pairs())
    early = tie(early, named)
    index = send_index.reshape(8, 2, size)

    def go(step, chunk):
        return lax.ppermute(chunk, axes, round_pairs(step - 1))

    def swap(chunk):
        return lax.ppermute(chunk, axes, SIBLINGS)

    own, other = [None] * 8, [None] * 8
    own[1], own[2] = go(1, early), go(2, early)
    late = gather_rows(tie(embeddings, early), send_index, (1, 2, 3, 4), size)
    own[0], other[0] = late[2:]
    own[3], own[4] = go(3, late[0]), go(4, late[0])
    own[1], own[2] = tie(own[1], late[0]), tie(own[2], late[0])
    own[5] = go(5, tie(late[1], own[4]))
    own[6] = go(6, tie(late[1], own[2]))

    named, table = tie(named, late[0]), tie(jnp.asarray(chunk_order()), late[0])
    order = table[lax.axis_index("shard"), lax.axis_index("rep")]
    flat = named.reshape(16, size)[order].reshape(1, 16 * size)

    def score(best, count, passes, after=()):
        arrays, loads = [], []
        for r, side in CHUNKS[:count]:
            chunk = (own, other)[side][r]
            array, place = chunk if isinstance(chunk, tuple) else (chunk, 0)
            if not any(array is known for known in arrays):
                arrays.append(array)
            loads.append(([array is known for known in arrays].index(True), place))
        return gram_best(arrays, tuple(loads), size, flat, best, passes, after)

    best = jnp.full((1, 16 * size), -1.0, jnp.float32)
    best = score(best, 4, (new_pass(1, 3, 4, size),), (order, index))
    other[1] = swap(tie(own[1], best))
    joined = join([own[2], tie(own[3], best), tie(own[4], best)], SHORT)
    own[7] = go(7, tie(late[2], own[3]))
    swapped = swap(joined)
    own[3], own[4] = (joined, 1), (joined, 2)
    best = score(best, 7, (new_pass(4, 2, 7, size), late_pass(2, 2, 6, 7, size)))
    other[2], other[3], other[4] = (swapped, 0), (swapped, 1), (swapped, 2)
    joined = join([tie(own[5], best), tie(own[6], best)], LONG)
    swapped = swap(joined)
    own[5], own[6] = (joined, 0), (joined, 1)
    best = score(best, 12, (new_pass(10, 2, 12, size), late_pass(3, 3, 7, 10, size, True)))
    other[5], other[6] = (swapped, 0), (swapped, 1)
    own[7] = tie(own[7], best)
    other[7] = swap(own[7])
    best = score(best, 15, (new_pass(14, 1, 15, size), late_pass(10, 2, 12, 14, size, True)))
    outbound = finish(order, own[7], other[7], flat, best)
    returned = lax.all_to_all(outbound, axes, split_axis=0, concat_axis=0, tiled=True)
    sources = []
    for owner in range(8):
        host, y = host_of(owner)
        for half in range(2):
            sources.append(tuple((host * 4 + y * 2 + core, half) for core in range(2)))
    return settle(index, returned, tuple(sources), documents)


def gathered(embeddings, send_index, place_index, slot_cluster):
    documents, width = embeddings.shape
    owners = lax.axis_size("shard")
    reps = lax.axis_size("rep")
    share = send_index.shape[0] // owners
    outgoing = normalize(embeddings.at[send_index].get(mode="promise_in_bounds"))
    arrived = lax.all_to_all(
        outgoing.reshape(owners, share, width), "shard", split_axis=0, concat_axis=0, tiled=True
    )
    parts = 16
    size = documents // parts
    news = parts // reps
    turn = lax.axis_index("rep") * news
    arrived = jnp.roll(arrived.reshape(parts, size, width), -turn, axis=0)
    clusters = arrival_names(place_index, slot_cluster).reshape(parts, size)
    clusters = jnp.roll(clusters, -turn, axis=0)
    best = jnp.full((1, documents), -1.0, jnp.float32)
    tiles = tuple(range(documents // BLK))
    passes = ((0, news, 0, 1, True, tiles, 0),)
    chunks = [arrived[i] for i in range(parts)]
    loads = tuple((i, 0) for i in range(parts))
    best = gram_best(chunks, loads, size, clusters.reshape(1, -1), best, passes)
    best = lax.all_gather(best[0, : news * size], "rep", axis=0, tiled=True)
    returned = lax.all_to_all(
        best.reshape(owners, share), "shard", split_axis=0, concat_axis=0, tiled=True
    )
    sources = tuple(((0, g),) for g in range(parts))
    return settle(send_index.reshape(parts, size), returned.reshape(1, parts, size), sources, documents)


def solution(mesh):
    planned = mesh.shape["shard"] == 8 and mesh.shape["rep"] == 4

    def shards(embeddings, send_index, place_index, slot_cluster, pair_list):
        del pair_list
        run = hosted if planned else gathered
        return run(embeddings, send_index, place_index, slot_cluster)

    return jax.shard_map(
        shards,
        mesh=mesh,
        in_specs=(P("shard", None), P("shard"), P("shard"), P("shard"), P(("shard", "rep"), None)),
        out_specs=P("shard"),
        check_vma=False,
    )
```

```python
import functools

import jax
import jax.numpy as jnp
import numpy as np
from jax import lax
from jax.experimental import pallas as pl
from jax.experimental.pallas import tpu as pltpu
from jax.sharding import PartitionSpec as P

BLK = 256
LANES = 128
NT = (((1,), (1,)), ((), ()))
MIB = 1024 * 1024
LONG = 40_000_000_000
SHORT = 2_000_000_000

HOSTS = (2, 3, 4, 5)
ROUNDS = ((2, 6, 3, 7, 4, 1, 5), (3, 7, 2, 6, 4, 1, 5))


CHUNKS = (
    (0, 1), (0, 0), (1, 0), (2, 0),
    (3, 0), (4, 0), (1, 1),
    (2, 1), (3, 1), (4, 1), (5, 0), (6, 0),
    (5, 1), (6, 1), (7, 0), (7, 1),
)


def host_of(owner):
    z, x = owner // 2, owner % 2
    return (1 if z < 2 else 2) * 2 + x, z % 2


def chunk_order():
    order = np.zeros((8, 4, 16), np.int32)
    for s in range(8):
        for rep in range(4):
            for i, (step, side) in enumerate(CHUNKS):
                half = rep % 2 ^ side
                order[s, rep, i] = (s ^ ((0,) + ROUNDS[half])[step]) * 2 + half
    return order


def round_pairs(step):
    pairs = []
    for rep in range(4):
        for host in HOSTS:
            pairs.append(((host ^ ROUNDS[rep % 2][step]) * 4 + rep, host * 4 + rep))
    return pairs


SIBLINGS = [(host * 4 + rep, host * 4 + (rep ^ 1)) for host in HOSTS for rep in range(4)]


def metadata_pairs():
    pairs = []
    for owner in range(8):
        host, y = host_of(owner)
        for core in range(2):
            pairs.append((owner * 4 + y * 2 + core, host * 4 + y * 2 + core))
    return pairs


def tie(value, *after):
    return lax.optimization_barrier((value, *after))[0]


def normalize(rows):
    wide = rows.astype(jnp.float32)
    return (wide * lax.rsqrt(jnp.sum(wide * wide, axis=1, keepdims=True) + 1e-06)).astype(
        jnp.bfloat16
    )


def names_kernel(place_ref, slots_ref, out_ref):
    block = place_ref[...] // BLK
    found = jnp.zeros_like(block)
    for i in range(slots_ref.shape[0] * LANES // BLK):
        row = i * BLK // LANES
        found = jnp.where(block == i, slots_ref[row : row + 1, 0:1], found)
    out_ref[...] = found


def arrival_names(place_index, slot_cluster):
    places = place_index.reshape(-1, LANES)
    return pl.pallas_call(
        names_kernel, out_shape=jax.ShapeDtypeStruct(places.shape, jnp.int32)
    )(places, slot_cluster.reshape(-1, LANES))


def chunk_start(slot, size):
    s, rep = lax.axis_index("shard"), lax.axis_index("rep")
    y, core = rep // 2, rep % 2
    inner = (s >= HOSTS[0]) & (s <= HOSTS[-1])
    turn = min(slot, 3)
    steps = [(order[2 * turn], (order + (0,))[2 * turn + 1]) for order in ROUNDS]
    outer_step = jnp.where(core == 0, steps[0][0], steps[1][0])
    inner_step = jnp.where(core == 0, steps[0][1], steps[1][1])
    target = s ^ jnp.where(inner, inner_step, outer_step)
    owner = (2 * (target // 2 - 1) + y) * 2 + target % 2
    half = 1 - core if slot == 4 else core
    return owner * (2 * size) + half * size


def gather_kernel(slots, size, group, sections, *refs):
    index_hbm, rows_ref = refs[:2]
    index_ref, raw, wide, picked, sems = refs[-5:]
    outs = refs[-5 - len(slots) : -5]
    listed = pltpu.make_async_copy(index_hbm, index_ref, sems.at[sections])
    listed.start()
    width = raw.shape[1]
    tiles = width // LANES
    part = raw.shape[0] // sections
    copies = []
    for i in range(sections):
        rows = pl.ds(i * part, part)
        copies.append(pltpu.make_async_copy(rows_ref.at[rows], raw.at[rows], sems.at[i]))
        copies[-1].start()
    step = 160
    for i in range(sections):
        copies[i].wait()

        def widen(j, _, i=i):
            first = i * part + j * step
            rows = raw[pl.ds(pl.multiple_of(first, step), step), :].astype(jnp.float32)
            for t in range(tiles):
                wide[pl.ds(first * tiles + t, step, stride=tiles), :] = rows[:, t * LANES : (t + 1) * LANES]
            return 0

        lax.fori_loop(0, part // step, widen, 0)
    listed.wait()
    for c, slot in enumerate(slots):
        base = chunk_start(slot, size)

        def pick(j, _, c=c, base=base):
            for t in range(group):
                source = pl.multiple_of(index_ref[base + j * group + t] * tiles, tiles)
                picked[t * tiles : (t + 1) * tiles, :] = wide[pl.ds(source, tiles), :]
            for first in range(0, group, 16):
                rows = jnp.concatenate(
                    [picked[pl.ds(first * tiles + t, 16, stride=tiles), :] for t in range(tiles)],
                    axis=1,
                )
                scale = lax.rsqrt(jnp.sum(rows * rows, axis=1, keepdims=True) + 1e-06)
                outs[c][pl.ds(pl.multiple_of(j * group + first, 16), 16), :] = (rows * scale).astype(
                    jnp.bfloat16
                )
            return 0

        lax.fori_loop(0, size // group, pick, 0)


def gather_rows(embeddings, index, slots, size):
    documents, width = embeddings.shape
    count = len(slots)
    sections = 10
    group = 80
    return pl.pallas_call(
        functools.partial(gather_kernel, slots, size, group, sections),
        out_shape=[jax.ShapeDtypeStruct((size, width), jnp.bfloat16)] * count,
        in_specs=[pl.BlockSpec(memory_space=pltpu.HBM)] * 2,
        out_specs=[pl.BlockSpec(memory_space=pltpu.VMEM)] * count,
        scratch_shapes=[
            pltpu.SMEM(index.shape, jnp.int32),
            pltpu.VMEM((documents, width), jnp.bfloat16),
            pltpu.VMEM((documents * width // LANES, LANES), jnp.float32),
            pltpu.VMEM((group * width // LANES, LANES), jnp.float32),
            pltpu.SemaphoreType.DMA((sections + 1,)),
        ],
        compiler_params=pltpu.CompilerParams(vmem_limit_bytes=45 * MIB),
        cost_estimate=pl.CostEstimate(flops=LONG, bytes_accessed=0, transcendentals=0),
    )(index, embeddings)


def best_of_rows(acc, size):
    return jnp.max(jnp.transpose(acc), axis=0, keepdims=True)[:, :size]


def as_column(row_ref, start, size):
    wide = -(-size // LANES) * LANES
    row = row_ref[:, start : start + wide]
    return jnp.transpose(jnp.broadcast_to(row, (LANES, wide)))[:size]


def gram_kernel(passes, loads, size, limit, *refs):
    cluster_row, before_ref, best_ref, held, acc, sems = refs[-6:]
    count = len(loads)

    def source(i):
        array, place = loads[i]
        return refs[array].at[pl.ds(place * size, size)]

    def copy(i):
        return pltpu.make_async_copy(source(i), held.at[pl.ds(i * size, size)], sems.at[i])

    def arrive(i):
        rows = held.at[pl.ds(0, size)]
        pltpu.make_async_copy(rows, rows, sems.at[i]).wait()

    low = passes[0][5][0] * BLK // size
    for i in (*range(low, count), *range(low)):
        copy(i).start()
    best_ref[...] = before_ref[...]
    for i in range(low, count):
        copy(i).wait()

    def sweep(first, height, work):
        acc[...] = jnp.full_like(acc, -1.0)
        rows = held[first : first + height, :]
        left = as_column(cluster_row, first, height)
        left = jnp.concatenate([left, left], axis=1)

        def tile(start, special):
            gram = lax.dot_general(
                rows, held[pl.ds(start, BLK), :], NT, preferred_element_type=jnp.float32
            )
            counts = left == cluster_row[:, pl.ds(start, BLK)]
            if special:
                column = start + lax.broadcasted_iota(jnp.int32, (height, BLK), 1)
                row = first + lax.broadcasted_iota(jnp.int32, (height, BLK), 0)
                counts = counts & (column != row) & (column < limit)
            values = jnp.where(counts, gram, jnp.float32(-1.0))
            top = jnp.max(values, axis=0, keepdims=True)
            best_ref[:, pl.ds(start, BLK)] = jnp.maximum(best_ref[:, pl.ds(start, BLK)], top)
            acc[0:height, :] = jnp.maximum(
                acc[0:height, :], jnp.maximum(values[:, :LANES], values[:, LANES:])
            )

        work(tile)
        span = slice(first, first + height)
        best_ref[:, span] = jnp.maximum(best_ref[:, span], best_of_rows(acc[...], height))

    for n, (chunk, news, groups, group, meets, last, halved) in enumerate(passes):
        first, height = chunk * size, news * size

        def masked(t, first=first, height=height):
            return (t * BLK < first + height and (t + 1) * BLK > first) or (t + 1) * BLK > limit

        if halved:
            count_of_tiles = len(last) // 2
            cut = last[count_of_tiles] * BLK - halved * size
            core = lax.axis_index("rep") % 2
            for h, (top, bottom) in enumerate(((0, cut), (cut, height))):

                def work(tile, h=h, masked=masked, last=last, count_of_tiles=count_of_tiles, core=core):
                    side = h + core - 2 * h * core
                    for t in range(count_of_tiles):
                        start = (last[t] + count_of_tiles * side) * BLK
                        special = masked(last[t]) or masked(last[t + count_of_tiles])
                        tile(pl.multiple_of(start, BLK), special)

                sweep(first + top, bottom - top, work)
            continue
        step = -(-group * BLK // size)

        def work(tile, n=n, groups=groups, group=group, meets=meets, last=last, masked=masked, step=step):
            for t in last:
                tile(t * BLK, masked(t))

            def visit(u, _):
                for i in range(step) if n == 0 else ():

                    @pl.when(u * step + i < low)
                    def _(i=i):
                        arrive(u * step + i)

                for t in range(group):
                    tile(pl.multiple_of((u * group + t) * BLK, BLK), meets)
                return 0

            lax.fori_loop(0, groups, visit, 0)

        sweep(first, height, work)


def gram_best(arrays, loads, size, cluster_row, before, passes, after=()):
    width = arrays[0].shape[1]
    limit = len(loads) * size
    held = -(-limit // BLK) * BLK
    tall = max(news for _, news, *_ in passes) * size
    padded = -(-tall // LANES) * LANES
    return pl.pallas_call(
        functools.partial(gram_kernel, passes, loads, size, limit),
        out_shape=jax.ShapeDtypeStruct(before.shape, jnp.float32),
        in_specs=[pl.BlockSpec(memory_space=pl.ANY)] * (len(arrays) + len(after))
        + [pl.BlockSpec(memory_space=pltpu.VMEM)] * 2,
        out_specs=pl.BlockSpec(memory_space=pltpu.VMEM),
        scratch_shapes=[
            pltpu.VMEM((held, width), jnp.bfloat16),
            pltpu.VMEM((padded, LANES), jnp.float32),
            pltpu.SemaphoreType.DMA((len(loads),)),
        ],
        compiler_params=pltpu.CompilerParams(vmem_limit_bytes=24 * MIB),
        cost_estimate=pl.CostEstimate(flops=0, bytes_accessed=0, transcendentals=0),
    )(*arrays, *after, cluster_row, before)


def join_kernel(size, *refs):
    out_ref, sems = refs[-2:]
    copies = [
        pltpu.make_async_copy(ref, out_ref.at[pl.ds(i * size, size)], sems.at[i])
        for i, ref in enumerate(refs[:-2])
    ]
    for copy in copies:
        copy.start()
    for copy in copies:
        copy.wait()


def join(chunks, work):
    size, width = chunks[0].shape
    return pl.pallas_call(
        functools.partial(join_kernel, size),
        out_shape=jax.ShapeDtypeStruct((len(chunks) * size, width), chunks[0].dtype),
        in_specs=[pl.BlockSpec(memory_space=pl.ANY)] * len(chunks),
        out_specs=pl.BlockSpec(memory_space=pl.ANY),
        scratch_shapes=[pltpu.SemaphoreType.DMA((len(chunks),))],
        compiler_params=pltpu.CompilerParams(vmem_limit_bytes=MIB),
        cost_estimate=pl.CostEstimate(flops=work, bytes_accessed=0, transcendentals=0),
    )(*chunks)


def new_pass(chunk, news, count, size):
    plain = chunk * size // BLK
    group = max(n for n in range(1, 8) if plain % n == 0)
    groups = plain // group
    tiles = -(-count * size // BLK)
    return (chunk, news, groups, group, False, tuple(range(groups * group, tiles)), 0)


def late_pass(chunk, news, low, high, size, halved=False):
    tiles = tuple(range(low * size // BLK, -(-high * size // BLK)))
    return (chunk, news, 0, 1, True, tiles, low if halved else 0)


def finish_kernel(size, order_ref, own_ref, other_ref, clusters_ref, best_ref, out_ref, acc):
    gram = lax.dot_general(own_ref[...], other_ref[...], NT, preferred_element_type=jnp.float32)
    left = as_column(clusters_ref, 14 * size, size)
    left = jnp.tile(left, (1, -(-size // LANES)))[:, :size]
    last = 15 * size
    values = jnp.where(left == clusters_ref[:, last : last + size], gram, jnp.float32(-1.0))
    acc[...] = jnp.full_like(acc, -1.0)
    acc[0:size, :] = jnp.broadcast_to(jnp.max(values, axis=1, keepdims=True), (size, LANES))
    for i in range(16):
        found = best_ref[:, i * size : (i + 1) * size]
        if i == 14:
            found = jnp.maximum(found, best_of_rows(acc[...], size))
        if i == 15:
            found = jnp.maximum(found, jnp.max(values, axis=0, keepdims=True))
        place = order_ref[i]
        source, half = place // 2, place % 2
        for rep in range(4):
            out_ref[source * 4 + rep, pl.ds(half, 1), :] = found


def finish(order, own, other, clusters, best):
    size = own.shape[0]
    padded = -(-size // LANES) * LANES
    return pl.pallas_call(
        functools.partial(finish_kernel, size),
        out_shape=jax.ShapeDtypeStruct((32, 2, size), jnp.float32),
        in_specs=[pl.BlockSpec(memory_space=pltpu.SMEM)]
        + [pl.BlockSpec(memory_space=pltpu.VMEM)] * 4,
        out_specs=pl.BlockSpec(memory_space=pltpu.VMEM),
        scratch_shapes=[pltpu.VMEM((padded, LANES), jnp.float32)],
        compiler_params=pltpu.CompilerParams(vmem_limit_bytes=16 * MIB),
    )(order, own, other, clusters, best)


def settle_kernel(sources, size, high, index_ref, values_ref, out_ref, left_ref, right_ref):
    wide = left_ref.shape[1] // len(sources)
    rows = lax.broadcasted_iota(jnp.int32, (high, size), 0)
    lanes = lax.broadcasted_iota(jnp.int32, (LANES, size), 0)
    for g, places in enumerate(sources):
        index = index_ref[g // 2, g % 2 : g % 2 + 1, :] if index_ref.ndim == 3 else index_ref[g : g + 1, :]
        value = values_ref[places[0][0], places[0][1] : places[0][1] + 1, :]
        for a, b in places[1:]:
            value = jnp.maximum(value, values_ref[a, b : b + 1, :])
        span = slice(g * wide, g * wide + size)
        if size % LANES:
            tail = slice((g + 1) * wide - LANES, (g + 1) * wide)
            left_ref[:, tail] = jnp.zeros((3 * high, LANES), jnp.bfloat16)
            right_ref[:, tail] = jnp.zeros((LANES, LANES), jnp.bfloat16)
        here = rows == index // LANES
        for piece in range(3):
            head = value.astype(jnp.bfloat16).astype(jnp.float32)
            value = value - head
            left_ref[piece * high : (piece + 1) * high, span] = jnp.where(here, head, 0.0).astype(
                jnp.bfloat16
            )
        right_ref[:, span] = jnp.where(lanes == index % LANES, 1.0, 0.0).astype(jnp.bfloat16)
    total = lax.dot_general(left_ref[...], right_ref[...], NT, preferred_element_type=jnp.float32)
    total = total[2 * high : 3 * high] + total[high : 2 * high] + total[:high]
    out_ref[...] = total[: out_ref.shape[0]]


def settle(index, values, sources, documents):
    size = index.shape[-1]
    high = -(-documents // (16 * LANES)) * 16
    wide = -(-size // LANES) * LANES * len(sources)
    out = pl.pallas_call(
        functools.partial(settle_kernel, sources, size, high),
        out_shape=jax.ShapeDtypeStruct((documents // LANES, LANES), jnp.float32),
        scratch_shapes=[
            pltpu.VMEM((3 * high, wide), jnp.bfloat16),
            pltpu.VMEM((LANES, wide), jnp.bfloat16),
        ],
        compiler_params=pltpu.CompilerParams(vmem_limit_bytes=16 * MIB),
    )(index, values)
    return out.reshape(-1)


def hosted(embeddings, send_index, place_index, slot_cluster):
    documents = embeddings.shape[0]
    size = send_index.shape[0] // 16
    axes = ("shard", "rep")
    named = arrival_names(place_index, slot_cluster)
    embeddings = tie(embeddings, named)
    (early,) = gather_rows(embeddings, send_index, (0,), size)
    named = lax.ppermute(named, axes, metadata_pairs())
    early = tie(early, named)
    index = send_index.reshape(8, 2, size)

    def go(step, chunk):
        return lax.ppermute(chunk, axes, round_pairs(step - 1))

    def swap(chunk):
        return lax.ppermute(chunk, axes, SIBLINGS)

    own, other = [None] * 8, [None] * 8
    own[1], own[2] = go(1, early), go(2, early)
    late = gather_rows(tie(embeddings, early), send_index, (1, 2, 3, 4), size)
    own[0], other[0] = late[2:]
    own[3], own[4] = go(3, late[0]), go(4, late[0])
    own[1], own[2] = tie(own[1], late[0]), tie(own[2], late[0])
    own[5] = go(5, tie(late[1], own[4]))
    own[6] = go(6, tie(late[1], own[2]))

    named, table = tie(named, late[0]), tie(jnp.asarray(chunk_order()), late[0])
    order = table[lax.axis_index("shard"), lax.axis_index("rep")]
    flat = named.reshape(16, size)[order].reshape(1, 16 * size)

    def score(best, count, passes, after=()):
        arrays, loads = [], []
        for r, side in CHUNKS[:count]:
            chunk = (own, other)[side][r]
            array, place = chunk if isinstance(chunk, tuple) else (chunk, 0)
            if not any(array is known for known in arrays):
                arrays.append(array)
            loads.append(([array is known for known in arrays].index(True), place))
        return gram_best(arrays, tuple(loads), size, flat, best, passes, after)

    best = jnp.full((1, 16 * size), -1.0, jnp.float32)
    best = score(best, 4, (new_pass(1, 3, 4, size),), (order, index))
    other[1] = swap(tie(own[1], best))
    joined = join([own[2], tie(own[3], best), tie(own[4], best)], SHORT)
    own[7] = go(7, tie(late[2], own[3]))
    swapped = swap(joined)
    own[3], own[4] = (joined, 1), (joined, 2)
    best = score(best, 7, (new_pass(4, 2, 7, size), late_pass(2, 2, 6, 7, size)))
    other[2], other[3], other[4] = (swapped, 0), (swapped, 1), (swapped, 2)
    joined = join([tie(own[5], best), tie(own[6], best)], LONG)
    swapped = swap(joined)
    own[5], own[6] = (joined, 0), (joined, 1)
    best = score(best, 12, (new_pass(10, 2, 12, size), late_pass(3, 3, 7, 10, size, True)))
    other[5], other[6] = (swapped, 0), (swapped, 1)
    own[7] = tie(own[7], best)
    other[7] = swap(own[7])
    best = score(best, 15, (new_pass(14, 1, 15, size), late_pass(10, 2, 12, 14, size, True)))
    outbound = finish(order, own[7], other[7], flat, best)
    returned = lax.all_to_all(outbound, axes, split_axis=0, concat_axis=0, tiled=True)
    sources = []
    for owner in range(8):
        host, y = host_of(owner)
        for half in range(2):
            sources.append(tuple((host * 4 + y * 2 + core, half) for core in range(2)))
    return settle(index, returned, tuple(sources), documents)


def gathered(embeddings, send_index, place_index, slot_cluster):
    documents, width = embeddings.shape
    owners = lax.axis_size("shard")
    reps = lax.axis_size("rep")
    share = send_index.shape[0] // owners
    outgoing = normalize(embeddings.at[send_index].get(mode="promise_in_bounds"))
    arrived = lax.all_to_all(
        outgoing.reshape(owners, share, width), "shard", split_axis=0, concat_axis=0, tiled=True
    )
    parts = 16
    size = documents // parts
    news = parts // reps
    turn = lax.axis_index("rep") * news
    arrived = jnp.roll(arrived.reshape(parts, size, width), -turn, axis=0)
    clusters = arrival_names(place_index, slot_cluster).reshape(parts, size)
    clusters = jnp.roll(clusters, -turn, axis=0)
    best = jnp.full((1, documents), -1.0, jnp.float32)
    tiles = tuple(range(documents // BLK))
    passes = ((0, news, 0, 1, True, tiles, 0),)
    chunks = [arrived[i] for i in range(parts)]
    loads = tuple((i, 0) for i in range(parts))
    best = gram_best(chunks, loads, size, clusters.reshape(1, -1), best, passes)
    best = lax.all_gather(best[0, : news * size], "rep", axis=0, tiled=True)
    returned = lax.all_to_all(
        best.reshape(owners, share), "shard", split_axis=0, concat_axis=0, tiled=True
    )
    sources = tuple(((0, g),) for g in range(parts))
    return settle(send_index.reshape(parts, size), returned.reshape(1, parts, size), sources, documents)


def solution(mesh):
    planned = mesh.shape["shard"] == 8 and mesh.shape["rep"] == 4

    def shards(embeddings, send_index, place_index, slot_cluster, pair_list):
        del pair_list
        run = hosted if planned else gathered
        return run(embeddings, send_index, place_index, slot_cluster)

    return jax.shard_map(
        shards,
        mesh=mesh,
        in_specs=(P("shard", None), P("shard"), P("shard"), P("shard"), P(("shard", "rep"), None)),
        out_specs=P("shard"),
        check_vma=False,
    )
```
